32 devices in a mesh: dp: 4 (over x, core), fsdp: 8 (over z, y).
Axes of the slice: x: 2, y: 2, z: 4, core: 2. Of those that a mesh axis runs over, the one named last changes fastest.
Arguments:
- x_query: bfloat16 [64, 256, 768], P(('dp', 'fsdp')), may hold values from -6 to 6
- x_key: bfloat16 [64, 256, 768], P(('dp', 'fsdp')), may hold values from -6 to 6
- len_query: int32 [64], P(('dp', 'fsdp')), may hold values from 1 to 256, as said below
- len_key: int32 [64], P(('dp', 'fsdp')), may hold values from 1 to 256, as said below
- queue: bfloat16 [16384, 768], P(('dp', 'fsdp')), may hold values from -0.875 to 0.875
- qkv_weight: bfloat16 [2, 768, 2304], P(None, 'fsdp'), may hold values from -0.21875 to 0.21875
- query_bias: bfloat16 [2, 768], P(None, 'fsdp'), may hold values from -0.625 to 0.625
- value_bias: bfloat16 [2, 768], P(None, 'fsdp'), may hold values from -0.625 to 0.625
- proj_weight: bfloat16 [2, 768, 768], P(None, 'fsdp'), may hold values from -2.5 to 2.5
- proj_bias: bfloat16 [2, 768], P(None, 'fsdp'), may hold values from -0.625 to 0.625
- first_gain: bfloat16 [2, 768], P(None, 'fsdp'), may hold values from 0.5 to 1.5
- first_shift: bfloat16 [2, 768], P(None, 'fsdp'), may hold values from -0.625 to 0.625
- expand_weight: bfloat16 [2, 768, 3072], P(None, 'fsdp'), may hold values from -0.21875 to 0.21875
- expand_bias: bfloat16 [2, 3072], P(None, 'fsdp'), may hold values from -0.625 to 0.625
- shrink_weight: bfloat16 [2, 3072, 768], P(None, 'fsdp'), may hold values from -0.109375 to 0.109375
- shrink_bias: bfloat16 [2, 768], P(None, 'fsdp'), may hold values from -0.625 to 0.625
- second_gain: bfloat16 [2, 768], P(None, 'fsdp'), may hold values from 0.5 to 1.5
- second_shift: bfloat16 [2, 768], P(None, 'fsdp'), may hold values from -0.625 to 0.625
- key_qkv: float32 [2, 768, 2304], P(None, 'fsdp'), may hold values from -0.21875 to 0.21875
- key_querybias: float32 [2, 768], P(None, 'fsdp'), may hold values from -0.625 to 0.625
- key_valuebias: float32 [2, 768], P(None, 'fsdp'), may hold values from -0.625 to 0.625
- key_proj: float32 [2, 768, 768], P(None, 'fsdp'), may hold values from -2.5 to 2.5
- key_projbias: float32 [2, 768], P(None, 'fsdp'), may hold values from -0.625 to 0.625
- key_firstgain: float32 [2, 768], P(None, 'fsdp'), may hold values from 0.5 to 1.5
- key_firstshift: float32 [2, 768], P(None, 'fsdp'), may hold values from -0.625 to 0.625
- key_expand: float32 [2, 768, 3072], P(None, 'fsdp'), may hold values from -0.21875 to 0.21875
- key_expandbias: float32 [2, 3072], P(None, 'fsdp'), may hold values from -0.625 to 0.625
- key_shrink: float32 [2, 3072, 768], P(None, 'fsdp'), may hold values from -0.109375 to 0.109375
- key_shrinkbias: float32 [2, 768], P(None, 'fsdp'), may hold values from -0.625 to 0.625
- key_secondgain: float32 [2, 768], P(None, 'fsdp'), may hold values from 0.5 to 1.5
- key_secondshift: float32 [2, 768], P(None, 'fsdp'), may hold values from -0.625 to 0.625
Outputs:
- hidden_out: bfloat16 [64, 256, 768], P(('dp', 'fsdp'))
- grad_input: bfloat16 [64, 256, 768], P(('dp', 'fsdp'))
- grad_qkv: float32 [2, 768, 2304], P(None, 'fsdp')
- grad_querybias: float32 [2, 768], P(None, 'fsdp')
- grad_valuebias: float32 [2, 768], P(None, 'fsdp')
- grad_proj: float32 [2, 768, 768], P(None, 'fsdp')
- grad_projbias: float32 [2, 768], P(None, 'fsdp')
- grad_firstgain: float32 [2, 768], P(None, 'fsdp')
- grad_firstshift: float32 [2, 768], P(None, 'fsdp')
- grad_expand: float32 [2, 768, 3072], P(None, 'fsdp')
- grad_expandbias: float32 [2, 3072], P(None, 'fsdp')
- grad_shrink: float32 [2, 3072, 768], P(None, 'fsdp')
- grad_shrinkbias: float32 [2, 768], P(None, 'fsdp')
- grad_secondgain: float32 [2, 768], P(None, 'fsdp')
- grad_secondshift: float32 [2, 768], P(None, 'fsdp')
- crop_loss: float32 [64], P(('dp', 'fsdp'))
The draws below stay inside these ranges and needn't reach their ends.
Inputs may be any that keep to these rules, and one draw needn't show every extreme that they name: `len_query`: the crops of one device share a domain; the bound of a domain is 256, 192, 128 or 64, and a crop's length lies between three quarters of its bound and the bound, except one crop of 256 tokens. `len_key`: the same law as len_query, with the same domain for each device and lengths drawn afresh.
All inputs are finite; a program needn't handle non-finite values.
Results may differ from the reference program's by a relative error of at most 0.04.
Values may be sent and summed in bfloat16 or wider, within the bound.
A program may use at most 192 MiB of HBM per device.

```python
import math
import jax
import jax.numpy as jnp
from jax import lax

D = 768
HEADS = 12
FF = 3072
LAYERS = 2
LEN = 256
CROPS_DEV = 2
CROPS = 64
QUEUE = 16384


def crop_lengths(key, salt_num):
    domains = jax.random.randint(jax.random.fold_in(key, 101), (CROPS // CROPS_DEV,), 0, 4)
    domain = jnp.repeat(domains, CROPS_DEV, total_repeat_length=CROPS)
    bounds = jnp.array([LEN, LEN * 3 // 4, LEN // 2, LEN // 4], dtype=jnp.int32)
    ceiling = bounds[domain]
    base_len = ceiling * 3 // 4
    offsets = jax.random.randint(jax.random.fold_in(key, salt_num), (CROPS,), 0, 1 << 20)
    length = base_len + offsets % (ceiling - base_len + 1)
    chosen = jax.random.randint(jax.random.fold_in(key, salt_num + 1), (), 0, CROPS)
    return jnp.where(jnp.arange(CROPS) == chosen, LEN, length).astype(jnp.int32)


def draw_len_query(key, part):
    return crop_lengths(key, 7)


def draw_len_key(key, part):
    return crop_lengths(key, 13)


def levels(stream_key, shape, shards, smallest, high):
    level = 1.0
    for dim, shards_of in shards:
        steps = jax.random.uniform(jax.random.fold_in(jax.random.fold_in(stream_key, 6), dim), (shards_of,), jnp.float32, smallest / len(shards), high / len(shards))
        level = level * jnp.repeat(jnp.exp(steps), shape[dim] // shards_of).reshape((-1,) + (1,) * (len(shape) - 1 - dim))
    return level


def bell_draw(own_key, extent, scale, most, cuts=(), kind=jnp.bfloat16):
    values = scale * jax.random.normal(own_key, extent, jnp.float32)
    if cuts:
        values = values * levels(own_key, extent, cuts, -0.22, 0.18)
    return jnp.clip(values, -most, most).astype(kind)


def setup_inputs(seed: int = 0) -> dict:
    key_list = jax.random.split(jax.random.key(seed), 32)
    x_query = bell_draw(key_list[0], (CROPS, LEN, D), 1.0, 6.0, ((0, 32),))
    x_key = bell_draw(key_list[1], (CROPS, LEN, D), 1.0, 6.0, ((0, 32),))
    len_query = draw_len_query(jax.random.fold_in(key_list[31], 71), 0)
    len_key = draw_len_key(jax.random.fold_in(key_list[31], 71), 0)
    queue = bell_draw(key_list[4], (QUEUE, D), 0.15, 0.875, ((0, 32),))
    qkv_weight = bell_draw(key_list[5], (LAYERS, D, 3 * D), D ** -0.5, 0.21875, ((1, 8),))
    query_bias = bell_draw(key_list[6], (LAYERS, D), 0.1, 0.625, ((1, 8),))
    value_bias = bell_draw(key_list[7], (LAYERS, D), 0.1, 0.625, ((1, 8),))
    proj_weight = bell_draw(key_list[8], (LAYERS, D, D), (2 * D // LEN) ** -0.5, 2.5, ((1, 8),))
    proj_bias = bell_draw(key_list[9], (LAYERS, D), 0.1, 0.625, ((1, 8),))
    first_gain = jnp.clip(1.0 + 0.1 * jax.random.normal(key_list[10], (LAYERS, D), jnp.float32), 0.5, 1.5).astype(jnp.bfloat16)
    first_shift = bell_draw(key_list[11], (LAYERS, D), 0.1, 0.625, ((1, 8),))
    expand_weight = bell_draw(key_list[12], (LAYERS, D, FF), D ** -0.5, 0.21875, ((1, 8),))
    expand_bias = bell_draw(key_list[13], (LAYERS, FF), 0.1, 0.625, ((1, 8),))
    shrink_weight = bell_draw(key_list[14], (LAYERS, FF, D), FF ** -0.5, 0.109375, ((1, 8),))
    shrink_bias = bell_draw(key_list[15], (LAYERS, D), 0.1, 0.625, ((1, 8),))
    second_gain = jnp.clip(1.0 + 0.1 * jax.random.normal(key_list[16], (LAYERS, D), jnp.float32), 0.5, 1.5).astype(jnp.bfloat16)
    second_shift = bell_draw(key_list[17], (LAYERS, D), 0.1, 0.625, ((1, 8),))
    key_qkv = bell_draw(key_list[18], (LAYERS, D, 3 * D), D ** -0.5, 0.21875, ((1, 8),), jnp.float32)
    key_querybias = bell_draw(key_list[19], (LAYERS, D), 0.1, 0.625, ((1, 8),), jnp.float32)
    key_valuebias = bell_draw(key_list[20], (LAYERS, D), 0.1, 0.625, ((1, 8),), jnp.float32)
    key_proj = bell_draw(key_list[21], (LAYERS, D, D), (2 * D // LEN) ** -0.5, 2.5, ((1, 8),), jnp.float32)
    key_projbias = bell_draw(key_list[22], (LAYERS, D), 0.1, 0.625, ((1, 8),), jnp.float32)
    key_firstgain = jnp.clip(1.0 + 0.1 * jax.random.normal(key_list[23], (LAYERS, D), jnp.float32), 0.5, 1.5)
    key_firstshift = bell_draw(key_list[24], (LAYERS, D), 0.1, 0.625, ((1, 8),), jnp.float32)
    key_expand = bell_draw(key_list[25], (LAYERS, D, FF), D ** -0.5, 0.21875, ((1, 8),), jnp.float32)
    key_expandbias = bell_draw(key_list[26], (LAYERS, FF), 0.1, 0.625, ((1, 8),), jnp.float32)
    key_shrink = bell_draw(key_list[27], (LAYERS, FF, D), FF ** -0.5, 0.109375, ((1, 8),), jnp.float32)
    key_shrinkbias = bell_draw(key_list[28], (LAYERS, D), 0.1, 0.625, ((1, 8),), jnp.float32)
    key_secondgain = jnp.clip(1.0 + 0.1 * jax.random.normal(key_list[29], (LAYERS, D), jnp.float32), 0.5, 1.5)
    key_secondshift = bell_draw(key_list[30], (LAYERS, D), 0.1, 0.625, ((1, 8),), jnp.float32)
    return {"x_query": x_query, "x_key": x_key, "len_query": len_query, "len_key": len_key, "queue": queue, "qkv_weight": qkv_weight, "query_bias": query_bias, "value_bias": value_bias, "proj_weight": proj_weight, "proj_bias": proj_bias, "first_gain": first_gain, "first_shift": first_shift, "expand_weight": expand_weight, "expand_bias": expand_bias, "shrink_weight": shrink_weight, "shrink_bias": shrink_bias, "second_gain": second_gain, "second_shift": second_shift, "key_qkv": key_qkv, "key_querybias": key_querybias, "key_valuebias": key_valuebias, "key_proj": key_proj, "key_projbias": key_projbias, "key_firstgain": key_firstgain, "key_firstshift": key_firstshift, "key_expand": key_expand, "key_expandbias": key_expandbias, "key_shrink": key_shrink, "key_shrinkbias": key_shrinkbias, "key_secondgain": key_secondgain, "key_secondshift": key_secondshift}


@jax.custom_vjp
def low(v):
    return lax.optimization_barrier(v.astype(jnp.bfloat16)).astype(jnp.float32)

@jax.custom_vjp
def low_back(v):
    return v

def low_keep(v):
    return (low(v), None)

def low_pass(kept, grad):
    return (grad,)

def back_keep(v):
    return (v, None)

def back_low(kept, grad):
    return (low(grad),)
low.defvjp(low_keep, low_pass)
low_back.defvjp(back_keep, back_low)
contrast_sharpness = 0.05
objective_factor = 512.0
momentum = 0.9995
norm_eps = 1e-12
unit_eps = 1e-06
masked = -1000000000.0
highest_accuracy_mode = lax.Precision.HIGHEST

def layer_norm(residual, gain_vec, shift_vec):
    centered = residual - lax.optimization_barrier(jnp.mean(residual, -1, keepdims=True))
    spread = lax.optimization_barrier(jnp.mean(centered * centered, -1, keepdims=True))
    return centered * lax.rsqrt(spread + norm_eps) * gain_vec + shift_vec

def unit_rows(pooled):
    return pooled * lax.rsqrt(lax.optimization_barrier(jnp.sum(pooled * pooled, -1, keepdims=True)) + unit_eps)

def gelu_exact(pre_act):
    return jax.nn.gelu(pre_act, approximate=False)

def pool_rows(final_out, key_valid, lengths):
    summed = lax.optimization_barrier(jnp.sum(jnp.where(key_valid[:, :, None], final_out, 0.0), 1))
    return summed / lengths[:, None].astype(jnp.float32)

def matmul(left, right):
    return jnp.einsum('gtd,de->gte', left, right, precision=highest_accuracy_mode)

def layer_apply(inputs, key_valid, weights):
    qkv_mat, query_add, value_add, proj_mat, proj_add, first_gain, first_shift, expand_mat, expand_add, shrink_mat, shrink_add, second_gain, second_shift = weights
    group_size, seq_len, model_width = inputs.shape
    head_dim = model_width // HEADS
    head_shape = (group_size, seq_len, HEADS, head_dim)
    projected = matmul(inputs, qkv_mat)
    queries = low_back(low(projected[:, :, :model_width] + query_add))
    key_vecs = low_back(low(projected[:, :, model_width:2 * model_width]))
    values = low_back(low(projected[:, :, 2 * model_width:] + value_add))
    raw_scores = jnp.einsum('gqhe,gkhe->ghqk', queries.reshape(head_shape), key_vecs.reshape(head_shape), precision=highest_accuracy_mode) * head_dim ** (-0.5)
    scores = jnp.where(key_valid[:, None, None, :], low_back(raw_scores), masked)
    prob_low = low(jax.nn.softmax(scores, axis=-1))
    context = jnp.einsum('ghqk,gkhe->gqhe', prob_low, values.reshape(head_shape), precision=highest_accuracy_mode)
    context = low_back(low(context.reshape(group_size, seq_len, model_width)))
    attn_out = low_back(matmul(context, proj_mat) + proj_add)
    hidden_a = layer_norm(inputs + attn_out, first_gain, first_shift)
    ffn_inner = low_back(matmul(low(hidden_a), expand_mat) + expand_add)
    active = low(gelu_exact(ffn_inner))
    branch = low_back(matmul(active, shrink_mat) + shrink_add)
    return layer_norm(hidden_a + branch, second_gain, second_shift)

def encode(inputs, key_valid, params):
    hidden = inputs
    final_out = inputs
    for layer_idx in range(LAYERS):
        final_out = layer_apply(hidden, key_valid, tuple((member[layer_idx] for member in params)))
        hidden = low(final_out)
    return (final_out, hidden)

def reference(x_query, x_key, len_query, len_key, queue, qkv_weight, query_bias, value_bias, proj_weight, proj_bias, first_gain, first_shift, expand_weight, expand_bias, shrink_weight, shrink_bias, second_gain, second_shift, key_qkv, key_querybias, key_valuebias, key_proj, key_projbias, key_firstgain, key_firstshift, key_expand, key_expandbias, key_shrink, key_shrinkbias, key_secondgain, key_secondshift):
    query_params = tuple((member.astype(jnp.float32) for member in (qkv_weight, query_bias, value_bias, proj_weight, proj_bias, first_gain, first_shift, expand_weight, expand_bias, shrink_weight, shrink_bias, second_gain, second_shift)))
    mirror_params = (key_qkv, key_querybias, key_valuebias, key_proj, key_projbias, key_firstgain, key_firstshift, key_expand, key_expandbias, key_shrink, key_shrinkbias, key_secondgain, key_secondshift)
    updated = tuple((momentum * mirror_arr + (1.0 - momentum) * source for mirror_arr, source in zip(mirror_params, query_params)))
    mirror_low = tuple((low(member) for member in updated))
    num_crops = x_query.shape[0]
    group_size = math.gcd(num_crops, max(1, 4096 // LEN))
    group_count = num_crops // group_size
    positions = jnp.arange(LEN, dtype=jnp.int32)
    memory_bank_items = queue.astype(jnp.float32)
    block_shape = (group_count, group_size, LEN, D)

    def key_step(carried, scan_items):
        crop_block, crop_lens = scan_items
        key_valid = positions[None, :] < crop_lens[:, None]
        final_out, unused = encode(crop_block.astype(jnp.float32), key_valid, mirror_low)
        return (carried, low(unit_rows(pool_rows(final_out, key_valid, crop_lens))))
    unused, key_units = lax.scan(key_step, jnp.float32(0.0), (x_key.reshape(block_shape), len_key.reshape(group_count, group_size)))

    def objective(params, inputs):

        def query_step(loss_sum, scan_items):
            crop_block, crop_lens, target_block = scan_items
            key_valid = positions[None, :] < crop_lens[:, None]
            final_out, rounded = encode(crop_block, key_valid, params)
            anchor_embedding = low(unit_rows(pool_rows(final_out, key_valid, crop_lens)))
            distractor_similarity = low_back(jnp.dot(anchor_embedding, memory_bank_items.T, precision=highest_accuracy_mode)) / contrast_sharpness
            matching_similarity = lax.optimization_barrier(jnp.sum(anchor_embedding * target_block, -1)) / contrast_sharpness
            all_logits = jnp.concatenate([distractor_similarity, matching_similarity[:, None]], 1)
            losses = jax.nn.logsumexp(all_logits, axis=1) - matching_similarity
            return (loss_sum + jnp.sum(losses), (rounded, losses))
        loss_sum, scanned = lax.scan(jax.checkpoint(query_step), jnp.float32(0.0), (inputs.reshape(block_shape), len_query.reshape(group_count, group_size), key_units))
        return (objective_factor * loss_sum, scanned)
    objective_value, pullback, aux_out = jax.vjp(objective, query_params, x_query.astype(jnp.float32), has_aux=True)
    grad_params, grad_inputs = pullback(jnp.ones_like(objective_value))
    rounded, losses = aux_out
    hidden_out = rounded.reshape(num_crops, LEN, D).astype(jnp.bfloat16)
    grad_input = grad_inputs.astype(jnp.bfloat16)
    return (hidden_out, grad_input, grad_params[0], grad_params[1], grad_params[2], grad_params[3], grad_params[4], grad_params[5], grad_params[6], grad_params[7], grad_params[8], grad_params[9], grad_params[10], grad_params[11], grad_params[12], losses.reshape(num_crops))
```

```python
import functools

import jax
import jax.numpy as jnp
from jax import lax
from jax.experimental import pallas as pl
from jax.experimental.pallas import tpu as pltpu
from jax.sharding import PartitionSpec as P

MESH=pl.DeviceIdType.MESH

def coords(D,F):
    d=lax.axis_index("dp"); f=lax.axis_index("fsdp")
    B=F//4
    return d,f,f//B,f%B,(d//2)%2,d%2


def ag_kernel(D,F,L,opt,w,vec,g,vg,lsem,vsem,vrsem,zs,zr,ys,yr,xs,xr,cs,cr,csx,crx):
    A=4;B=F//4
    R=w.shape[1]; T=R//16
    half=T//2; nx=(half*opt['nx'])//36; nyz=half-nx
    d,f,a,b,x,c=coords(D,F)
    h=c*half
    xn=nx*16; yzn=nyz*16
    def rows(t0,n): return pl.ds(pl.multiple_of(t0*16,16),n)
    yzr=rows(h+x*nx,yzn); xsr=rows(h+x*nyz,xn); xrr=rows(h+(1-x)*nyz,xn)
    hc=(1-c)*half
    oyz=rows(hc+x*nx,yzn); oxr=rows(hc+(1-x)*nyz,xn)
    xd=d+2-4*x; cd=d+1-2*c
    bar=pltpu.get_barrier_semaphore()
    for s in range(1,F):
        pl.semaphore_signal(bar,inc=1,device_id=(d,(f+s)%F),device_id_type=MESH)
    pl.semaphore_signal(bar,inc=1,device_id=(xd,f),device_id_type=MESH)
    pl.semaphore_signal(bar,inc=1,device_id=(cd,f),device_id_type=MESH)
    pl.semaphore_wait(bar,F+1)
    def rc(src,dst,ss,rs,dev):
        return pltpu.make_async_remote_copy(src,dst,ss,rs,device_id=dev,device_id_type=MESH)
    def vcopy(s):
        return rc(vec,vg.at[f],vsem.at[s],vrsem.at[s],(d,(f+s)%F))
    for s in range(1,F): vcopy(s).start()
    vl=pltpu.make_async_copy(vec,vg.at[f],vsem.at[0]); vl.start()
    def own(l): return pltpu.make_async_copy(w.at[l],g.at[l,f],lsem.at[l])
    def src_a(hd):
        hh,dr=hd
        return a-hh if dr==0 else a+hh
    def has(hd):
        hh,dr=hd
        return (a>=hh) if dr==0 else (a+hh<A)
    def when(cond,fn):
        if cond is True: fn()
        else: pl.when(cond)(fn)
    def zsend(l,src,hd,fs):
        hh,dr=hd
        na=a+1 if dr==0 else a-1
        return rc(src,g.at[l,fs,yzr],zs.at[l,dr,hh],zr.at[l,dr,hh],(d,na*B+b))
    def canpass(dr): return (a+1<A) if dr==0 else (a>0)
    def zrecv(l,hd):
        fs=src_a(hd)*B+b
        return rc(g.at[l,fs,yzr],g.at[l,fs,yzr],zs.at[l,hd[1],hd[0]],zr.at[l,hd[1],hd[0]],(d,f))
    def slot(hd): return hd[0]*2+hd[1]
    def ycopy(l,src,hd,fs,t): return rc(src,g.at[l,fs,yzr],ys.at[l,slot(hd),t],yr.at[l,slot(hd),t],(d,a*B+(b+t)%B))
    def yrecv(l,hd,t):
        fs=src_a(hd)*B+(b-t)%B
        return fs,rc(g.at[l,fs,yzr],g.at[l,fs,yzr],ys.at[l,slot(hd),t],yr.at[l,slot(hd),t],(d,f))
    def xcopy(l,fs,i): return rc(g.at[l,fs,xsr],g.at[l,fs,xsr],xs.at[l,i],xr.at[l,i],(xd,f))
    def xrecv(l,fs,i): return rc(g.at[l,fs,xrr],g.at[l,fs,xrr],xs.at[l,i],xr.at[l,i],(xd,f))
    def ccopy(l,fs,i): return rc(g.at[l,fs,yzr],g.at[l,fs,yzr],cs.at[l,i],cr.at[l,i],(cd,f))
    def cxcopy(l,fs,i): return rc(g.at[l,fs,xrr],g.at[l,fs,xrr],csx.at[l,i],crx.at[l,i],(cd,f))
    def crecv(l,fs,i): return rc(g.at[l,fs,oyz],g.at[l,fs,oyz],cs.at[l,i],cr.at[l,i],(cd,f))
    def cxrecv(l,fs,i): return rc(g.at[l,fs,oxr],g.at[l,fs,oxr],csx.at[l,i],crx.at[l,i],(cd,f))
    OWN=(0,0)
    def start(l):
        for dr in (0,1): when(canpass(dr),lambda dr=dr: zsend(l,w.at[l,yzr],(1,dr),f).start())
        for t in range(1,B): ycopy(l,w.at[l,yzr],OWN,f,t).start()
        own(l).start()
    def handle_z(l,hh):
        for dr in (0,1):
            hd=(hh,dr)
            def go(hd=hd,dr=dr):
                fs=src_a(hd)*B+b
                zrecv(l,hd).wait_recv()
                if hh+1<A:
                    when(canpass(dr),lambda: zsend(l,g.at[l,fs,yzr],(hh+1,dr),fs).start())
                for t in range(1,B): ycopy(l,g.at[l,fs,yzr],hd,fs,t).start()
                xcopy(l,fs,slot(hd)*B).start()
                ccopy(l,fs,slot(hd)*B).start()
            pl.when(has(hd))(go)
    def hds(hh): return [(0,0)] if hh==0 else [(hh,0),(hh,1)]
    def handle_y(l,hh):
        for hd in hds(hh):
            for t in range(1,B):
                def go(hd=hd,t=t):
                    fs,r=yrecv(l,hd,t); r.wait_recv()
                    xcopy(l,fs,slot(hd)*B+t).start()
                    ccopy(l,fs,slot(hd)*B+t).start()
                when(True if hh==0 else has(hd),go)
    def each_foreign(fn):
        for hh in range(A):
            for hd in hds(hh):
                for t in range(B):
                    if hh==0 and t==0: continue
                    def go(hd=hd,t=t): fn(src_a(hd)*B+(b-t)%B,slot(hd)*B+t)
                    when(True if hh==0 else has(hd),go)
    def xphase(l):
        def go(fs,i):
            xrecv(l,fs,i).wait_recv(); cxcopy(l,fs,i).start()
        each_foreign(go)
    start(0)
    for l in range(L):
        for hh in range(1,A):
            if hh==opt['pre'] and l+1<L: start(l+1)
            handle_z(l,hh)
            handle_y(l,hh-1)
            if hh==1 and l: xphase(l-1)
        if opt['pre']==A and l+1<L: start(l+1)
        handle_y(l,A-1)
    xphase(L-1)
    for l in range(L):
        def go(fs,i):
            crecv(l,fs,i).wait_recv(); cxrecv(l,fs,i).wait_recv()
            xcopy(l,fs,i).wait_send(); ccopy(l,fs,i).wait_send(); cxcopy(l,fs,i).wait_send()
        each_foreign(go)
        for dr in (0,1):
            for hh in range(1,A):
                cond=canpass(dr)
                if hh>1: cond=jnp.logical_and(cond,has((hh-1,dr)))
                pl.when(cond)(lambda hh=hh,dr=dr: zsend(l,w.at[l,yzr],(hh,dr),f).wait_send())
        for hh in range(A):
            for hd in hds(hh):
                for t in range(1,B):
                    when(True if hh==0 else has(hd),lambda hd=hd,t=t: ycopy(l,w.at[l,yzr],hd,f,t).wait_send())
        own(l).wait()
    vl.wait()
    for s in range(1,F):
        vcopy(s).wait_send()
        rc(vec,vg.at[f],vsem.at[s],vrsem.at[s],(d,f)).wait_recv()

def all_gather(D,F,w,vec,cid=1,opt=None):
    L,R,C=w.shape
    A=4;B=F//4
    S=pltpu.SemaphoreType.DMA
    N=2*A*B
    return pl.pallas_call(functools.partial(ag_kernel,D,F,L,opt),
        out_shape=(jax.ShapeDtypeStruct((L,F,R,C),w.dtype),jax.ShapeDtypeStruct((F,)+vec.shape,vec.dtype)),
        in_specs=[pl.BlockSpec(memory_space=pl.ANY)]*2,out_specs=[pl.BlockSpec(memory_space=pl.ANY)]*2,
        scratch_shapes=[S((L,)),S((F,)),S((F,)),S((L,2,A)),S((L,2,A)),S((L,2*A,B)),S((L,2*A,B))]+[S((L,N))]*6,
        compiler_params=pltpu.CompilerParams(collective_id=cid,has_side_effects=True),name="gather_weights")(w,vec)
f32=jnp.float32; bf16=jnp.bfloat16
HEADS=12
def dot(a,b): return lax.dot_general(a,b,(((1,),(0,)),((),())),preferred_element_type=f32)
def dot_t(a,b): return lax.dot_general(a,b,(((1,),(1,)),((),())),preferred_element_type=f32)
def tdot(a,b): return lax.dot_general(a,b,(((0,),(0,)),((),())),preferred_element_type=f32)

def phi_parts(u):
    z=jnp.abs(u)*0.7071067811865476
    t=1.0/(1.0+0.3275911*z)
    e=jnp.exp(-z*z)
    poly=t*(0.254829592+t*(-0.284496736+t*(1.421413741+t*(-1.453152027+t*1.061405429))))
    half=0.5*poly*e
    cdf=jnp.where(u>=0,1.0-half,half)
    return cdf,e*0.3989422804014327

def load_weights(l,g,wv,sv,sem):
    F=g.shape[1]; r=768//F; rs=3072//F
    cps=[]
    for j in range(8):
        cps.append(pltpu.make_async_copy(g.at[l,:,pl.ds(j*r,r),:],wv.at[j],sem.at[j]))
    for j in range(4):
        cps.append(pltpu.make_async_copy(g.at[l,pl.ds(j*(F//4),F//4),pl.ds(8*r,rs),:],sv.at[j],sem.at[8+j]))
    return cps

def fwd_kernel(l,save,lens,x,vec,g,*rest):
    if save:
        (y,pooled,qkv_o,pb_o,ctx_o,xh1_o,rs1_o,h1_o,act_o,der_o,xh2_o,rs2_o,
         wv,sv,qkv,pb,ctx,xh1,rs1,h1,act,der,xh2,rs2,acc,sem,osem)=rest
    else:
        (y,pooled,wv,sv,qkv,ctx,xh1,h1,acc,sem)=rest
    cps=load_weights(l,g,wv,sv,sem)
    for c in cps: c.start()
    outs=[]
    def out(i,src,dst):
        if save:
            cp=pltpu.make_async_copy(src,dst,osem.at[i]); cp.start(); outs.append(cp)
    def W(j): return wv[j].reshape(768,768)
    def S(j): return sv[j].reshape(768,768)
    NR=512
    for j in range(3):
        cps[j].wait()
        r=dot(x[...],W(j))
        if j==0: r=r+vec[0:1,:]
        if j==2: r=r+vec[1:2,:]
        qkv[:,j*768:(j+1)*768]=r.astype(bf16)
    if save: out(0,qkv,qkv_o)
    lane=lax.broadcasted_iota(jnp.int32,(256,128),1)
    low_half=lane<64
    kpos=lax.broadcasted_iota(jnp.int32,(256,256),1)
    def pair(i,_):
        c=i//6; p=i-c*6
        rows=pl.ds(pl.multiple_of(c*256,256),256)
        o=pl.multiple_of(p*128,128)
        q2=qkv[rows,pl.ds(o,128)]*jnp.asarray(0.125,bf16)
        k2=qkv[rows,pl.ds(pl.multiple_of(768+o,128),128)]
        v2=qkv[rows,pl.ds(pl.multiple_of(1536+o,128),128)]
        ok=kpos<lens[c]
        res=[]
        for hh in range(2):
            qm=jnp.where(low_half if hh==0 else jnp.logical_not(low_half),q2,jnp.zeros_like(q2))
            s=jnp.where(ok,dot_t(qm,k2),-1e9)
            m=jnp.max(s,-1,keepdims=True)
            e=jnp.exp(s-m)
            pr=(e*(1.0/jnp.sum(e,-1,keepdims=True))).astype(bf16)
            if save: pb[i*2+hh]=pr
            res.append(dot(pr,v2))
        ctx[rows,pl.ds(o,128)]=jnp.where(low_half,res[0],res[1]).astype(bf16)
        return 0
    lax.fori_loop(0,12,pair,0,unroll=3)
    if save: out(1,pb,pb_o); out(2,ctx,ctx_o)
    cps[3].wait()
    def ln(z,gain,shift):
        mu=jnp.mean(z,-1,keepdims=True); cz=z-mu
        rstd=lax.rsqrt(jnp.mean(cz*cz,-1,keepdims=True)+1e-12)
        xh=cz*rstd
        return xh,rstd,xh*gain+shift
    z=dot(ctx[...],W(3))+vec[2:3,:]+x[...].astype(f32)
    xh,rstd,h=ln(z,vec[3:4,:],vec[4:5,:])
    if save:
        xh1[...]=xh; rs1[...]=jnp.broadcast_to(rstd,(NR,128)); out(3,xh1,xh1_o); out(4,rs1,rs1_o)
    h1[...]=h.astype(bf16)
    acc[...]=h+vec[5:6,:]
    if save: out(5,h1,h1_o)
    for j in range(4):
        cps[4+j].wait(); cps[8+j].wait()
        u=dot(h1[...],W(4+j))+vec[8+j:9+j,:]
        cdf,pdf=phi_parts(u)
        gb=(u*cdf).astype(bf16)
        if save:
            act[:,j*768:(j+1)*768]=gb
            der[:,j*768:(j+1)*768]=(cdf+u*pdf).astype(bf16)
        acc[...]+=dot(gb,S(j))
    if save: out(6,act,act_o); out(7,der,der_o)
    xh,rstd,yy=ln(acc[...],vec[6:7,:],vec[7:8,:])
    if save:
        xh2[...]=xh; rs2[...]=jnp.broadcast_to(rstd,(NR,128)); out(8,xh2,xh2_o); out(9,rs2,rs2_o)
    y[...]=yy.astype(bf16)
    tpos=lax.broadcasted_iota(jnp.int32,(256,768),0)
    for c in range(2):
        pooled[c:c+1,:]=jnp.sum(jnp.where(tpos<lens[c],yy[c*256:(c+1)*256],0.0),0,keepdims=True)/lens[c].astype(f32)
    for cp in outs: cp.wait()

def layer_fwd(l,save,lens,x,vec,g):
    F=g.shape[1]
    sd=jax.ShapeDtypeStruct
    V=pl.BlockSpec(memory_space=pltpu.VMEM); ANY=pl.BlockSpec(memory_space=pl.ANY)
    saved=[sd((512,2304),bf16),sd((24,256,256),bf16),sd((512,768),bf16),sd((512,768),f32),sd((512,128),f32),sd((512,768),bf16),sd((512,3072),bf16),sd((512,3072),bf16),sd((512,768),f32),sd((512,128),f32)]
    outs=[sd((512,768),bf16),sd((2,768),f32)]+(saved if save else [])
    wscr=[pltpu.VMEM((8,F,768//F,768),bf16),pltpu.VMEM((4,F//4,3072//F,768),bf16)]
    if save: scr=wscr+[pltpu.VMEM(s.shape,s.dtype) for s in saved]+[pltpu.VMEM((512,768),f32),pltpu.SemaphoreType.DMA((12,)),pltpu.SemaphoreType.DMA((10,))]
    else: scr=wscr+[pltpu.VMEM((512,2304),bf16),pltpu.VMEM((512,768),bf16),pltpu.VMEM((512,768),f32),pltpu.VMEM((512,768),bf16),pltpu.VMEM((512,768),f32),pltpu.SemaphoreType.DMA((12,))]
    return pl.pallas_call(functools.partial(fwd_kernel,l,save),out_shape=outs,
        in_specs=[pl.BlockSpec(memory_space=pltpu.SMEM),V,V,ANY],out_specs=[V,V]+([ANY]*10 if save else []),
        scratch_shapes=scr,compiler_params=pltpu.CompilerParams(vmem_limit_bytes=60<<20),name="layer_fwd")(lens,x,vec,g)
def bwd_kernel(l,first,lens,dyin,x,vec,g,qkv_i,pb_i,ctx_i,xh1_i,rs1_i,h1_i,act_i,der_i,xh2_i,rs2_i,
               dx,dg,vg,wv,sv,qkv,pb,ctx,xh1,rs1,h1,act,der,xh2,rs2,dmix,dacc,dr2,dctx,dv,ds,sem,isem,osem):
    F=g.shape[1]; r=768//F; rs_=3072//F
    cps=load_weights(l,g,wv,sv,sem)
    ins=[pltpu.make_async_copy(s,d,isem.at[i]) for i,(s,d) in enumerate([(qkv_i,qkv),(pb_i,pb),(ctx_i,ctx),(xh1_i,xh1),(rs1_i,rs1),(h1_i,h1),(act_i,act),(der_i,der),(xh2_i,xh2),(rs2_i,rs2)])]
    QKV,PB,CTX,XH1,RS1,H1,ACT,DER,XH2,RS2=range(10)
    for i in (XH2,RS2): ins[i].start()
    for j in range(4):
        cps[8+j].start()
        if j==0: ins[ACT].start(); ins[DER].start(); ins[H1].start()
        cps[4+j].start()
    for i in (XH1,RS1,CTX): ins[i].start()
    cps[3].start(); ins[QKV].start(); ins[PB].start()
    for j in range(3): cps[j].start()
    def W(j): return wv[j].reshape(768,768)
    def S(j): return sv[j].reshape(768,768)
    outs=[]
    def outw(j,val):
        if j<8:
            dv[j]=val.astype(bf16).reshape(F,r,768)
            cp=pltpu.make_async_copy(dv.at[j],dg.at[:,pl.ds(j*r,r),:],osem.at[j])
        else:
            q=j-8
            ds[q]=val.astype(bf16).reshape(F//4,rs_,768)
            cp=pltpu.make_async_copy(ds.at[q],dg.at[pl.ds(q*(F//4),F//4),pl.ds(8*r,rs_),:],osem.at[j])
        cp.start(); outs.append(cp)
    vg[...]=jnp.zeros_like(vg)
    tpos=lax.broadcasted_iota(jnp.int32,(256,768),0)
    if first:
        dy=jnp.concatenate([jnp.where(tpos<lens[c],dyin[c:c+1,:],0.0) for c in range(2)],0)
    else: dy=dyin[...]
    def ln_back(dy,xh,rstd,gain):
        t=dy*gain
        return rstd*(t-jnp.mean(t,-1,keepdims=True)-xh*jnp.mean(t*xh,-1,keepdims=True))
    def colsum(v): return jnp.sum(v,0,keepdims=True)
    ins[XH2].wait(); ins[RS2].wait()
    xh=xh2[...]
    vg[6:7,:]=colsum(dy*xh); vg[7:8,:]=colsum(dy)
    d2=ln_back(dy,xh,rs2[:,0:1],vec[6:7,:])
    dacc[...]=d2
    dfb=d2.astype(bf16)
    dr2[...]=dfb
    vg[5:6,:]=colsum(dfb.astype(f32))
    for i in (ACT,DER,H1): ins[i].wait()
    for j in range(4):
        cps[8+j].wait(); cps[4+j].wait()
        a=act[:,j*768:(j+1)*768]
        outw(8+j,tdot(a,dr2[...]))
        du=(dot_t(dr2[...],S(j))*der[:,j*768:(j+1)*768].astype(f32)).astype(bf16)
        vg[8+j:9+j,:]=colsum(du.astype(f32))
        outw(4+j,tdot(h1[...],du))
        dacc[...]+=dot_t(du,W(4+j))
    for i in (XH1,RS1,CTX): ins[i].wait()
    dh=dacc[...]; xh=xh1[...]
    vg[3:4,:]=colsum(dh*xh); vg[4:5,:]=colsum(dh)
    d1=ln_back(dh,xh,rs1[:,0:1],vec[3:4,:])
    dacc[...]=d1
    dr2[...]=d1.astype(bf16)
    vg[2:3,:]=colsum(dr2[...].astype(f32))
    cps[3].wait()
    outw(3,tdot(ctx[...],dr2[...]))
    dctx[...]=dot_t(dr2[...],W(3)).astype(bf16)
    ins[QKV].wait(); ins[PB].wait()
    lane=lax.broadcasted_iota(jnp.int32,(256,128),1); low_half=lane<64
    def pair(i,_):
        c=i//6; p=i-c*6
        rows=pl.ds(pl.multiple_of(c*256,256),256); o=pl.multiple_of(p*128,128)
        o1=pl.multiple_of(768+o,128); o2=pl.multiple_of(1536+o,128)
        q2=qkv[rows,pl.ds(o,128)]; k2=qkv[rows,pl.ds(o1,128)]; v2=qkv[rows,pl.ds(o2,128)]
        dc=dctx[rows,pl.ds(o,128)]
        res=[]
        for hh in range(2):
            m=low_half if hh==0 else jnp.logical_not(low_half)
            P=pb[i*2+hh]; pf=P.astype(f32)
            dP=dot_t(jnp.where(m,dc,jnp.zeros_like(dc)),v2)
            pd=pf*dP
            dS=(pd-pf*jnp.sum(pd,-1,keepdims=True)).astype(bf16)
            res.append((dot(dS,k2),tdot(dS,q2),tdot(P,dc)))
        sel=lambda t: jnp.where(low_half,res[0][t],res[1][t])
        dmix[rows,pl.ds(o,128)]=(sel(0)*0.125).astype(bf16)
        dmix[rows,pl.ds(o1,128)]=(sel(1)*0.125).astype(bf16)
        dmix[rows,pl.ds(o2,128)]=sel(2).astype(bf16)
        return 0
    lax.fori_loop(0,12,pair,0,unroll=3)
    for j in range(3):
        cps[j].wait()
        dm=dmix[:,j*768:(j+1)*768]
        if j==0: vg[0:1,:]=colsum(dm.astype(f32))
        if j==2: vg[1:2,:]=colsum(dm.astype(f32))
        outw(j,tdot(x[...],dm))
        dacc[...]+=dot_t(dm,W(j))
    dx[...]=dacc[...].astype(dx.dtype)
    for c in outs: c.wait()

def layer_bwd(l,first,lens,dy,x,vec,g,saved,dxt):
    F=g.shape[1]; sd=jax.ShapeDtypeStruct
    V=pl.BlockSpec(memory_space=pltpu.VMEM); ANY=pl.BlockSpec(memory_space=pl.ANY)
    S=pltpu.SemaphoreType.DMA
    w=[pltpu.VMEM((8,F,768//F,768),bf16),pltpu.VMEM((4,F//4,3072//F,768),bf16)]
    scr=w+[pltpu.VMEM(s.shape,s.dtype) for s in saved]+[pltpu.VMEM((512,2304),bf16),pltpu.VMEM((512,768),f32),pltpu.VMEM((512,768),bf16),pltpu.VMEM((512,768),bf16)]+w+[S((12,)),S((10,)),S((12,))]
    return pl.pallas_call(functools.partial(bwd_kernel,l,first),out_shape=[sd((512,768),dxt),sd((F,12*768//F,768),bf16),sd((16,768),f32)],
        in_specs=[pl.BlockSpec(memory_space=pltpu.SMEM),V,V,V]+[ANY]*11,out_specs=[V,ANY,V],scratch_shapes=scr,
        compiler_params=pltpu.CompilerParams(vmem_limit_bytes=61<<20),name="layer_bwd")(lens,dy,x,vec,g,*saved)

def sizes(F):
    n=4*(768//F); np_=n//3; nq=n-np_
    return n,np_,nq
def rs_scratch(D,F,NP):
    A=4;B=F//4;O=D//4; n,np_,nq=sizes(F); nh=n//2; Sm=pltpu.SemaphoreType.DMA
    V=pltpu.VMEM
    return dict(T=V((NP,F,n,384),bf16),RC=V((NP,F,n,384),bf16),RPX=V((NP,F,np_//2,384),bf16),RPY=V((NP,B-1,A,np_//2,384),bf16),
      RQY=V((NP,B-1,A,nq,384),bf16),RQX=V((NP,A,nq//2,384),bf16),T3=V((NP,A,nh,384),bf16),RZ=V((NP,A-1,nh,384),bf16),
      **(dict(RO=V((NP,O-1,nh,384),bf16),TO=V((NP,nh,384),bf16)) if O>1 else {}),
      VS=V((5,32,768),f32),VRC=V((1,32,768),f32),VRX=V((1,32,768),f32),VRY=V((B-1,32,768),f32),VRZ=V((A-1,32,768),f32),
      **(dict(VRO=V((O-1,32,768),f32)) if O>1 else {}),
      LS=Sm((NP,)),SS=Sm((NP,8+B+A+B+A+O,)),RS=Sm((NP,8+B+A+B+A+O)),VSS=Sm((8+B+A+O,)),VRS=Sm((8+B+A+O,)))
class Reduce:
    def __init__(self,D,F,src,fin,vin,vout,buf):
        self.D,self.F=D,F; self.A=4; self.B=F//4; self.O=D//4
        d=lax.axis_index("dp"); f=lax.axis_index("fsdp")
        self.d,self.f=d,f; self.a=f//self.B; self.b=f%self.B; self.x=(d//2)%2; self.c=d%2; self.o=d//4
        self.xd=d+2-4*self.x; self.cd=d+1-2*self.c
        self.src,self.fin,self.vin,self.vout=src,fin,vin,vout
        self.__dict__.update(buf); self.n,self.np,self.nq=sizes(F)
        self.hp=self.np//2; self.hq=self.nq//2
        self.pending=[]
        m=pl.multiple_of
        self.mycols=pl.ds(m(self.c*384,128),384); self.ocols=pl.ds(m((1-self.c)*384,128),384)
        self.Pown=pl.ds(m(self.x*self.hp,16),self.hp); self.Poth=pl.ds(m((1-self.x)*self.hp,16),self.hp)
        self.Qown=pl.ds(m(self.np+self.x*self.hq,16),self.hq); self.Qoth=pl.ds(m(self.np+(1-self.x)*self.hq,16),self.hq)
        self.Qall=pl.ds(self.np,self.nq)
    def peers(self):
        out=[(self.d,(self.f+s)%self.F) for s in range(1,self.F)]
        out+=[(self.xd,self.f),(self.cd,self.f)]+[((self.d+4*s)%self.D,self.f) for s in range(1,self.O)]
        return out
    def rc(self,i,k,src,dst,dev):
        cp=pltpu.make_async_remote_copy(src,dst,self.SS.at[i,k],self.RS.at[i,k],device_id=dev,device_id_type=MESH)
        return cp
    def go(self,cp): cp.start(); self.pending.append(cp)
    def kPy(self,t): return 8+t
    def kQy(self,t): return 8+self.B+t
    def kZ(self,s): return 8+2*self.B+s
    def kO(self,s): return 8+2*self.B+self.A+s
    def Yd(self,t): return (self.d,self.a*self.B+(self.b+t)%self.B)
    def Zd(self,s): return (self.d,((self.a+s)%self.A)*self.B+self.b)
    def s0(self,i):
        s=self.src(i)
        self.cC=lambda i: self.rc(i,0,self.src(i).at[:,:,self.ocols],self.RC.at[i],(self.cd,self.f))
        self.go(self.cC(i))
        self.lc=lambda i: pltpu.make_async_copy(self.src(i).at[:,:,self.mycols],self.T.at[i],self.LS.at[i])
        self.lc(i).start()
    def s1(self,i):
        self.lc(i).wait(); self.cC(i).wait_recv()
        T,RC=self.T,self.RC
        def body(f,_):
            T[i,f]=(T[i,f].astype(f32)+RC[i,f].astype(f32)).astype(bf16); return 0
        lax.fori_loop(0,self.F,body,0)
        self.go(self.cPx(i))
        for t in range(1,self.B):
            for a in range(self.A): pass
        for t in range(1,self.B):
            fb=(self.b+t)%self.B
            for a in range(self.A):
                pass
        self.startQy(i)
    def cPx(self,i): return self.rc(i,1,self.T.at[i,:,self.Poth],self.RPX.at[i],(self.xd,self.f))
    def Tab(self,i):
        return self.T.at[i].reshape(self.A,self.B,self.n,384)
    def cQy(self,i,t): return self.rc(i,self.kQy(t),self.Tab(i).at[:,(self.b+t)%self.B,self.Qall],self.RQY.at[i,t-1],self.Yd(t))
    def cPy(self,i,t): return self.rc(i,self.kPy(t),self.Tab(i).at[:,(self.b+t)%self.B,self.Pown],self.RPY.at[i,t-1],self.Yd(t))
    def startQy(self,i):
        for t in range(1,self.B): self.go(self.cQy(i,t))
    def s2(self,i):
        T=self.T
        self.cPx(i).wait_recv()
        def body(f,_):
            T[i,f,self.Pown]=(T[i,f,self.Pown].astype(f32)+self.RPX[i,f].astype(f32)).astype(bf16); return 0
        lax.fori_loop(0,self.F,body,0)
        for t in range(1,self.B): self.go(self.cPy(i,t))
        for t in range(1,self.B): self.cQy(i,t).wait_recv()
        def bodyq(a,_):
            fo=a*self.B+self.b
            v=T[i,fo,self.Qall].astype(f32)
            for t in range(1,self.B): v=v+self.RQY[i,t-1,a].astype(f32)
            T[i,fo,self.Qall]=v.astype(bf16); return 0
        lax.fori_loop(0,self.A,bodyq,0)
        self.go(self.cQx(i))
    def cQx(self,i): return self.rc(i,2,self.Tab(i).at[:,self.b,self.Qoth],self.RQX.at[i],(self.xd,self.f))
    def s3(self,i):
        for t in range(1,self.B): self.cPy(i,t).wait_recv()
        self.cQx(i).wait_recv()
        def body(a,_):
            fo=a*self.B+self.b
            v=self.T[i,fo,self.Pown].astype(f32)
            for t in range(1,self.B): v=v+self.RPY[i,t-1,a].astype(f32)
            self.T3[i,a,0:self.hp]=v.astype(bf16)
            self.T3[i,a,self.hp:self.hp+self.hq]=(self.T[i,fo,self.Qown].astype(f32)+self.RQX[i,a].astype(f32)).astype(bf16)
            return 0
        lax.fori_loop(0,self.A,body,0)
        for s in range(1,self.A): self.go(self.cZ(i,s))
    def cZ(self,i,s): return self.rc(i,self.kZ(s),self.T3.at[i,(self.a+s)%self.A],self.RZ.at[i,s-1],self.Zd(s))
    def cO(self,i,s): return self.rc(i,self.kO(s),self.TO.at[i],self.RO.at[i,s-1],((self.d+4*s)%self.D,self.f))
    def put(self,i,v):
        v=v.astype(bf16)
        self.fin[i,self.Pown,self.mycols]=v[:self.hp]; self.fin[i,self.Qown,self.mycols]=v[self.hp:]
        self.go(self.cFX(i,0)); self.go(self.cFX(i,1))
    def cFX(self,i,w):
        r=(self.Pown,self.Qown)[w]; v=self.fin.at[i,r,self.mycols]
        return self.rc(i,3+w,v,v,(self.xd,self.f))
    def rFX(self,i,w):
        r=(self.Poth,self.Qoth)[w]; v=self.fin.at[i,r,self.mycols]
        return self.rc(i,3+w,v,v,(self.xd,self.f))
    def s4(self,i):
        v=self.T3[i,self.a].astype(f32)
        for s in range(1,self.A):
            self.cZ(i,s).wait_recv()
            v=v+self.RZ[i,s-1].astype(f32)
        if self.O>1:
            self.TO[i]=v.astype(bf16)
            for s in range(1,self.O): self.go(self.cO(i,s))
            for s in range(1,self.O):
                self.cO(i,s).wait_recv(); v=v+self.RO[i,s-1].astype(f32)
        self.put(i,v)
    def s5(self,i):
        for w in (0,1): self.rFX(i,w).wait_recv()
        v=self.fin.at[i,:,self.mycols]; self.go(self.rc(i,5,v,v,(self.cd,self.f)))
    def s6(self,i):
        v=self.fin.at[i,:,self.ocols]; self.rc(i,5,v,v,(self.cd,self.f)).wait_recv()
    def vstage(self,k):
        st=[(self.VRC,[(self.cd,self.f)],0),(self.VRX,[(self.xd,self.f)],1),(self.VRY,[self.Yd(t) for t in range(1,self.B)],8),(self.VRZ,[self.Zd(s) for s in range(1,self.A)],8+self.B)]
        if self.O>1: st.append((self.VRO,[((self.d+4*s)%self.D,self.f) for s in range(1,self.O)],8+self.B+self.A))
        def cps(k):
            buf,devs,k0=st[k]
            return [pltpu.make_async_remote_copy(self.VS.at[k],buf.at[q],self.VSS.at[k0+q],self.VRS.at[k0+q],device_id=dv,device_id_type=MESH) for q,dv in enumerate(devs)]
        if k==0: self.VS[0]=self.vin[...]
        elif k<=len(st):
            v=self.VS[k-1]
            for q,cp in enumerate(cps(k-1)):
                cp.wait_recv(); v=v+st[k-1][0][q]
            if k<len(st): self.VS[k]=v
            else: self.vout[...]=v
        if k<len(st):
            for cp in cps(k): self.go(cp)
    def finish(self):
        for cp in self.pending: cp.wait_send()

def rs_kernel(D,F,names,dgs,vin,fin,vout,*scr):
    buf=dict(zip(names,scr))
    n=4*(768//F)
    NP=3*len(dgs)
    src=lambda i: dgs[i//3].at[:,pl.ds((2-i%3)*n,n),:]
    R=Reduce(D,F,src,fin,vin,vout,buf)
    bar=pltpu.get_barrier_semaphore(); ps=R.peers()
    for p in ps: pl.semaphore_signal(bar,inc=1,device_id=p,device_id_type=MESH)
    pl.semaphore_wait(bar,len(ps))
    stages=[R.s0,R.s1,R.s2,R.s3,R.s4,R.s5,R.s6]
    for t in range(NP+6):
        if t<6: R.vstage(t)
        for i in range(NP):
            if 0<=t-i<=6: stages[t-i](i)
    R.finish()

def reduce_grads(D,F,dgs,vin,cid):
    n,np_,nq=sizes(F); NP=3*len(dgs)
    buf=rs_scratch(D,F,NP); sd=jax.ShapeDtypeStruct
    V=pl.BlockSpec(memory_space=pltpu.VMEM); ANY=pl.BlockSpec(memory_space=pl.ANY)
    def k(*refs):
        nd=len(dgs)
        rs_kernel(D,F,list(buf),refs[:nd],refs[nd],refs[nd+1],refs[nd+2],*refs[nd+3:])
    return pl.pallas_call(k,out_shape=[sd((NP,n,768),bf16),sd((32,768),f32)],in_specs=[ANY]*len(dgs)+[V],out_specs=[V,V],
        scratch_shapes=list(buf.values()),compiler_params=pltpu.CompilerParams(collective_id=cid,has_side_effects=True,vmem_limit_bytes=61<<20),name="reduce_grads")(*dgs,vin)

contrast_sharpness = 0.05
objective_factor = 512.0
momentum = 0.9995
unit_eps = 1e-06


def unit_rows(pooled):
    return pooled * lax.rsqrt(jnp.sum(pooled * pooled, -1, keepdims=True) + unit_eps)


def pack_mats(qkv, proj, expand, shrink):
    w = proj.shape[-1]
    return jnp.concatenate(
        [qkv[:, :, i * w : (i + 1) * w] for i in range(3)]
        + [proj]
        + [expand[:, :, i * w : (i + 1) * w] for i in range(4)]
        + [shrink],
        1,
    )


def on_device(dp, fsdp, x_query, x_key, len_query, len_key, queue, *params):
    query_params, key_params = params[:13], params[13:]
    num_crops, seq_len, width = x_query.shape
    mirror = tuple(
        (momentum * k + (1.0 - momentum) * q.astype(f32)).astype(bf16)
        for k, q in zip(key_params, query_params)
    )
    both = [jnp.concatenate([q, m], 0) for q, m in zip(query_params, mirror)]
    qkv, qb, vb, proj, pb, g1, b1, expand, eb, shrink, sb, g2, b2 = both
    mats = pack_mats(qkv, proj, expand, shrink)
    small = jnp.concatenate([qb, vb, pb, g1, b1, sb, g2, b2, eb], 1)
    small_len = small.shape[1]
    vec = jnp.pad(small.reshape(-1), (0, 16 * width - 4 * small_len)).reshape(16, width)
    gathered, vec_all = all_gather(dp, fsdp, mats, vec, cid=1, opt=dict(nx=13, pre=2))
    vec_all = vec_all.reshape(fsdp, 16 * width)[:, : 4 * small_len].reshape(fsdp, 4, small_len)
    r = width // fsdp
    rows8 = vec_all[:, :, : 8 * r].reshape(fsdp, 4, 8, r).transpose(1, 2, 0, 3).reshape(4, 8, width)
    rows4 = vec_all[:, :, 8 * r :].transpose(1, 0, 2).reshape(4, 4, width)
    vecs = jnp.concatenate([rows8, rows4, jnp.zeros((4, 4, width), bf16)], 1).astype(f32)
    x0 = x_query.reshape(num_crops * seq_len, width)
    y0, _, *saved0 = layer_fwd(0, True, len_query, x0, vecs[0], gathered)
    y1, pooled, *saved1 = layer_fwd(1, True, len_query, y0, vecs[1], gathered)
    xk = x_key.reshape(num_crops * seq_len, width)
    k0, _ = layer_fwd(2, False, len_key, xk, vecs[2], gathered)
    _, pooled_key = layer_fwd(3, False, len_key, k0, vecs[3], gathered)
    key_unit = unit_rows(pooled_key).astype(bf16)
    query_unit = unit_rows(pooled).astype(bf16)
    pos = jnp.sum(query_unit.astype(f32) * key_unit.astype(f32), -1) / contrast_sharpness
    everyone = ("dp", "fsdp")
    logits = (
        jnp.einsum("cd,kd->ck", lax.all_gather(query_unit, everyone, axis=0, tiled=True), queue, preferred_element_type=f32)
        / contrast_sharpness
    )
    start_own = lax.axis_index(everyone) * num_crops
    own = lambda v: lax.dynamic_slice_in_dim(v, start_own, num_crops, 0)
    peak = jnp.max(logits, 1)
    peak = lax.dynamic_update_slice_in_dim(peak, jnp.maximum(own(peak), pos), start_own, 0)
    peak = lax.pmax(peak, everyone)
    shifted = jnp.exp(logits - peak[:, None])
    part = jnp.dot(shifted.astype(bf16), queue, preferred_element_type=f32)
    sums = jnp.sum(shifted, 1)
    payload = jnp.concatenate([part, jnp.broadcast_to(sums[:, None], (sums.shape[0], 128))], 1)
    payload = lax.psum_scatter(payload, everyone, scatter_dimension=0, tiled=True)
    own_peak = own(peak)
    pos_exp = jnp.exp(pos - own_peak)
    total = payload[:, width] + pos_exp
    crop_losses = own_peak + jnp.log(total) - pos
    scale = objective_factor / contrast_sharpness
    grad_unit = payload[:, :width] * (scale / total)[:, None]
    grad_unit = grad_unit + (scale * (pos_exp / total - 1.0))[:, None] * key_unit.astype(f32)
    _, unit_back = jax.vjp(unit_rows, pooled)
    grad_pooled = unit_back(grad_unit)[0] / len_query[:, None].astype(f32)
    dx1, d1, v1 = layer_bwd(1, True, len_query, grad_pooled, y0, vecs[1], gathered, saved1, f32)
    dx0, d0, v0 = layer_bwd(0, False, len_query, dx1, x0, vecs[0], gathered, saved0, bf16)
    fin, vsum = reduce_grads(dp, fsdp, [d1, d0], jnp.concatenate([v1, v0], 0), 2)
    me = lax.axis_index("fsdp")
    n = fin.shape[1]
    fin = fin.astype(f32).reshape(2, 3, n, width)[::-1]
    sh_g, ex_g, at_g = fin[:, 0], fin[:, 1], fin[:, 2]
    grad_qkv = jnp.concatenate([at_g[:, i * r : (i + 1) * r] for i in range(3)], 2)
    grad_proj = at_g[:, 3 * r :]
    grad_expand = jnp.concatenate([ex_g[:, i * r : (i + 1) * r] for i in range(4)], 2)
    vsum = vsum.reshape(2, 16, width)[::-1]
    mine = lax.dynamic_slice_in_dim(vsum[:, :8], me * r, r, 2)
    ebg = lax.dynamic_slice_in_dim(vsum[:, 8:12].reshape(2, 4 * width), me * 4 * r, 4 * r, 1)
    qb, vb, pb, g1, b1, sb, g2, b2 = [mine[:, i] for i in range(8)]
    hidden = y1.reshape(num_crops, seq_len, width)
    grad_input = dx0.reshape(num_crops, seq_len, width)
    return (hidden, grad_input, grad_qkv, qb, vb, grad_proj, pb, g1, b1, grad_expand, ebg, sh_g, sb, g2, b2, crop_losses)


def solution(mesh):
    in_specs = (
        P(("dp", "fsdp"), None, None),
        P(("dp", "fsdp"), None, None),
        P(("dp", "fsdp")),
        P(("dp", "fsdp")),
        P(("dp", "fsdp"), None),
        P(None, "fsdp", None),
        P(None, "fsdp"),
        P(None, "fsdp"),
        P(None, "fsdp", None),
        P(None, "fsdp"),
        P(None, "fsdp"),
        P(None, "fsdp"),
        P(None, "fsdp", None),
        P(None, "fsdp"),
        P(None, "fsdp", None),
        P(None, "fsdp"),
        P(None, "fsdp"),
        P(None, "fsdp"),
        P(None, "fsdp", None),
        P(None, "fsdp"),
        P(None, "fsdp"),
        P(None, "fsdp", None),
        P(None, "fsdp"),
        P(None, "fsdp"),
        P(None, "fsdp"),
        P(None, "fsdp", None),
        P(None, "fsdp"),
        P(None, "fsdp", None),
        P(None, "fsdp"),
        P(None, "fsdp"),
        P(None, "fsdp"),
    )
    out_specs = (
        P(("dp", "fsdp"), None, None),
        P(("dp", "fsdp"), None, None),
        P(None, "fsdp", None),
        P(None, "fsdp"),
        P(None, "fsdp"),
        P(None, "fsdp", None),
        P(None, "fsdp"),
        P(None, "fsdp"),
        P(None, "fsdp"),
        P(None, "fsdp", None),
        P(None, "fsdp"),
        P(None, "fsdp", None),
        P(None, "fsdp"),
        P(None, "fsdp"),
        P(None, "fsdp"),
        P(("dp", "fsdp")),
    )
    return jax.shard_map(
        functools.partial(on_device, mesh.shape["dp"], mesh.shape["fsdp"]), mesh=mesh, in_specs=in_specs, out_specs=out_specs, check_vma=False
    )
```

```python
import functools

import jax
import jax.numpy as jnp
from jax import lax
from jax.experimental import pallas as pl
from jax.experimental.pallas import tpu as pltpu
from jax.sharding import PartitionSpec as P

f32=jnp.float32; bf16=jnp.bfloat16
HEADS=12
def dot(a,b): return lax.dot_general(a,b,(((1,),(0,)),((),())),preferred_element_type=f32)
def dot_t(a,b): return lax.dot_general(a,b,(((1,),(1,)),((),())),preferred_element_type=f32)
def tdot(a,b): return lax.dot_general(a,b,(((0,),(0,)),((),())),preferred_element_type=f32)

def phi_parts(u):
    z=jnp.abs(u)*0.7071067811865476
    t=1.0/(1.0+0.3275911*z)
    e=jnp.exp(-z*z)
    poly=t*(0.254829592+t*(-0.284496736+t*(1.421413741+t*(-1.453152027+t*1.061405429))))
    half=0.5*poly*e
    cdf=jnp.where(u>=0,1.0-half,half)
    return cdf,e*0.3989422804014327

def load_weights(l,g,wv,sv,sem):
    F=g.shape[1]; r=768//F; rs=3072//F
    cps=[]
    for j in range(8):
        cps.append(pltpu.make_async_copy(g.at[l,:,pl.ds(j*r,r),:],wv.at[j],sem.at[j]))
    for j in range(4):
        cps.append(pltpu.make_async_copy(g.at[l,pl.ds(j*(F//4),F//4),pl.ds(8*r,rs),:],sv.at[j],sem.at[8+j]))
    return cps

MESH=pl.DeviceIdType.MESH
SHARP=0.05
FACTOR=512.0
MOM=0.9995

def remote(src,dst,ss,rs,dev):
    return pltpu.make_async_remote_copy(src,dst,ss,rs,device_id=dev,device_id_type=MESH)

def when(cond,fn):
    if cond is True: fn()
    else: pl.when(cond)(fn)

class Place:
    def __init__(self,D,F):
        self.D,self.F=D,F; self.A=4; self.B=F//4; self.O=D//4
        d=self.d=lax.axis_index("dp"); f=self.f=lax.axis_index("fsdp")
        self.a=f//self.B; self.b=f%self.B; self.o=d//4; self.x=(d//2)%2; self.c=d%2
        self.xd=d+2-4*self.x; self.cd=d+1-2*self.c
        self.N=D*F; self.me=d*F+f
    def peer(self,s):
        p=(self.me+s)%self.N
        return p,(p//self.F,p%self.F)

class Gather:
    def __init__(self,pos,g,chunks,ready,sems):
        self.p,self.g,self.chunks,self.ready=pos,g,chunks,ready
        self.zs,self.zr,self.ys,self.yr,self.xs,self.xr,self.cs,self.cr,self.ks,self.kr=sems
    def rows(self,q,t0,n):
        return pl.ds(pl.multiple_of(self.chunks[q][1]+t0*16,16),n*16)
    def parts(self,q):
        p=self.p; half=self.chunks[q][2]//32; nx=(half*13+18)//36; nyz=half-nx
        h=p.c*half; hc=(1-p.c)*half
        R=lambda t0,n: self.rows(q,t0,n)
        return dict(yz=R(h+p.x*nx,nyz),xs=R(h+p.x*nyz,nx),xr=R(h+(1-p.x)*nyz,nx),oyz=R(hc+p.x*nx,nyz),oxr=R(hc+(1-p.x)*nyz,nx))
    def at(self,q,fs,part): return self.g.at[self.chunks[q][0],fs,self.parts(q)[part]]
    def src_a(self,hd): return self.p.a-hd[0] if hd[1]==0 else self.p.a+hd[0]
    def has(self,hd):
        if hd[0]==0: return True
        return (self.p.a>=hd[0]) if hd[1]==0 else (self.p.a+hd[0]<self.p.A)
    def canpass(self,dr): return (self.p.a+1<self.p.A) if dr==0 else (self.p.a>0)
    def z(self,q,hd,fs):
        na=self.p.a+1 if hd[1]==0 else self.p.a-1
        r=self.at(q,fs,"yz")
        return remote(r,r,self.zs.at[q,hd[1],hd[0]],self.zr.at[q,hd[1],hd[0]],(self.p.d,na*self.p.B+self.p.b))
    def slot(self,hd): return hd[0]*2+hd[1]
    def y(self,q,hd,fs,t):
        r=self.at(q,fs,"yz"); s=self.slot(hd)
        return remote(r,r,self.ys.at[q,s,t],self.yr.at[q,s,t],(self.p.d,self.p.a*self.p.B+(self.p.b+t)%self.p.B))
    def xc(self,q,fs,i,part="xs"):
        r=self.at(q,fs,part); return remote(r,r,self.xs.at[q,i],self.xr.at[q,i],(self.p.xd,self.p.f))
    def cc(self,q,fs,i,part="yz"):
        r=self.at(q,fs,part); return remote(r,r,self.cs.at[q,i],self.cr.at[q,i],(self.p.cd,self.p.f))
    def kc(self,q,fs,i,part="xr"):
        r=self.at(q,fs,part); return remote(r,r,self.ks.at[q,i],self.kr.at[q,i],(self.p.cd,self.p.f))
    def shard(self,hd,t=0): return self.src_a(hd)*self.p.B+(self.p.b-t)%self.p.B
    def hds(self,hh): return [(0,0)] if hh==0 else [(hh,0),(hh,1)]
    def start(self,q):
        self.ready(q)
        f=self.p.f
        for dr in (0,1): when(self.canpass(dr),lambda dr=dr: self.z(q,(1,dr),f).start())
        for t in range(1,self.p.B): self.y(q,(0,0),f,t).start()
    def on_z(self,q,hh):
        for hd in self.hds(hh):
            def go(hd=hd):
                fs=self.shard(hd); dr=hd[1]
                self.z(q,hd,fs).wait_recv()
                if hh+1<self.p.A: when(self.canpass(dr),lambda: self.z(q,(hh+1,dr),fs).start())
                for t in range(1,self.p.B): self.y(q,hd,fs,t).start()
                i=self.slot(hd)*self.p.B
                self.xc(q,fs,i).start(); self.cc(q,fs,i).start()
            when(self.has(hd),go)
    def on_y(self,q,hh):
        for hd in self.hds(hh):
            for t in range(1,self.p.B):
                def go(hd=hd,t=t):
                    fs=self.shard(hd,t); i=self.slot(hd)*self.p.B+t
                    self.y(q,hd,fs,t).wait_recv()
                    self.xc(q,fs,i).start(); self.cc(q,fs,i).start()
                when(self.has(hd),go)
    def each(self,hh,fn):
        for hd in self.hds(hh):
            for t in range(self.p.B):
                if hh==0 and t==0: continue
                when(self.has(hd),lambda hd=hd,t=t: fn(self.shard(hd,t),self.slot(hd)*self.p.B+t))
    def on_x(self,q,hh):
        def go(fs,i):
            self.xc(q,fs,i,"xr").wait_recv(); self.kc(q,fs,i).start()
        self.each(hh,go)
    def on_c(self,q):
        def go(fs,i):
            self.cc(q,fs,i,"oyz").wait_recv(); self.kc(q,fs,i,"oxr").wait_recv()
        for hh in range(self.p.A): self.each(hh,go)
    def handlers(self,q,pre):
        hs=[]; A=self.p.A
        for hh in range(1,A):
            if hh==pre and q+1<len(self.chunks): hs.append(lambda: self.start(q+1))
            hs.append(lambda hh=hh: self.on_z(q,hh))
            hs.append(lambda hh=hh: self.on_y(q,hh-1))
            if hh>=2: hs.append(lambda hh=hh: self.on_x(q,hh-2))
        hs.append(lambda: self.on_y(q,A-1))
        hs.append(lambda: self.on_x(q,A-2)); hs.append(lambda: self.on_x(q,A-1))
        hs.append(lambda: self.on_c(q))
        return hs
    def finish(self):
        f=self.p.f
        for q in range(len(self.chunks)):
            def go(fs,i):
                self.xc(q,fs,i).wait_send(); self.cc(q,fs,i).wait_send(); self.kc(q,fs,i).wait_send()
            for hh in range(self.p.A):
                self.each(hh,go)
                for hd in self.hds(hh):
                    for t in range(1,self.p.B): when(self.has(hd),lambda hd=hd,t=t: self.y(q,hd,f,t).wait_send())
            for dr in (0,1):
                for hh in range(1,self.p.A):
                    cond=self.canpass(dr)
                    if hh>1: cond=jnp.logical_and(cond,self.has((hh-1,dr)))
                    pl.when(cond)(lambda hh=hh,dr=dr: self.z(q,(hh,dr),f).wait_send())

def interleave(handlers,steps):
    done=0; n=max(len(steps),1)
    for k,s in enumerate(steps):
        s()
        upto=(k+1)*len(handlers)//n
        for h in handlers[done:upto]: h()
        done=upto
    for h in handlers[done:]: h()

SAVED=("qkv","pb","ctx","xh1","rs1","h1","act","der","xh2","rs2")
def saved_shapes():
    sd=jax.ShapeDtypeStruct
    return [sd((512,2304),bf16),sd((24,256,256),bf16),sd((512,768),bf16),sd((512,768),f32),sd((512,128),f32),sd((512,768),bf16),sd((512,3072),bf16),sd((512,3072),bf16),sd((512,768),f32),sd((512,128),f32)]

class Forward:
    def __init__(self,g,vecs,lens,R):
        self.g,self.vecs,self.lens=g,vecs,lens
        self.__dict__.update(R)
    def W(self,j): return self.wv[j].reshape(768,768)
    def S(self,j): return self.sv[j].reshape(768,768)
    def load(self,l,js):
        for j in js: self.wcp(l,j).start()
    def wcp(self,l,j):
        F=self.g.shape[1]; r=768//F; rs=3072//F
        if j<8: return pltpu.make_async_copy(self.g.at[l,:,pl.ds(j*r,r),:],self.wv.at[j],self.wsem.at[j])
        j-=8
        return pltpu.make_async_copy(self.g.at[l,pl.ds(j*(F//4),F//4),pl.ds(8*r,rs),:],self.sv.at[j],self.wsem.at[8+j])
    def ocp(self,l,i): return pltpu.make_async_copy(self.__dict__[SAVED[i]],self.outs[l][i],self.osem.at[l,i])
    def out(self,l,*names):
        for n in names: self.ocp(l,SAVED.index(n)).start()
    def drain(self,l):
        for i in range(len(SAVED)): self.ocp(l,i).wait()
    def ln(self,z,gain,shift):
        mu=jnp.mean(z,-1,keepdims=True); cz=z-mu
        rstd=lax.rsqrt(jnp.mean(cz*cz,-1,keepdims=True)+1e-12)
        xh=cz*rstd
        return xh,rstd,xh*gain+shift
    def attn_steps(self,l,save,x,lens,before=None):
        V=lambda i: self.vecs[l,i:i+1,:]
        def proj_in(j):
            if j==0 and before: before()
            if j==0: self.load(l,range(4))
            self.wcp(l,j).wait()
            r=dot(x[...],self.W(j))
            if j==0: r=r+V(0)
            if j==2: r=r+V(1)
            self.qkv[:,j*768:(j+1)*768]=r.astype(bf16)
            if save and j==2: self.out(l,"qkv")
        lane=lax.broadcasted_iota(jnp.int32,(256,128),1); low_half=lane<64
        kpos=lax.broadcasted_iota(jnp.int32,(256,256),1)
        def pair(i,_):
            c=i//6; p=i-c*6
            rows=pl.ds(pl.multiple_of(c*256,256),256); o=pl.multiple_of(p*128,128)
            q2=self.qkv[rows,pl.ds(o,128)]*jnp.asarray(0.125,bf16)
            k2=self.qkv[rows,pl.ds(pl.multiple_of(768+o,128),128)]; v2=self.qkv[rows,pl.ds(pl.multiple_of(1536+o,128),128)]
            ok=kpos<lens[c]
            res=[]
            for hh in range(2):
                qm=jnp.where(low_half if hh==0 else jnp.logical_not(low_half),q2,jnp.zeros_like(q2))
                s=jnp.where(ok,dot_t(qm,k2),-1e9)
                e=jnp.exp(s-jnp.max(s,-1,keepdims=True))
                pr=(e*(1.0/jnp.sum(e,-1,keepdims=True))).astype(bf16)
                if save: self.pb[i*2+hh]=pr
                res.append(dot(pr,v2))
            self.ctx[rows,pl.ds(o,128)]=jnp.where(low_half,res[0],res[1]).astype(bf16)
            return 0
        def attend(s):
            lax.fori_loop(6*s,6*s+6,pair,0,unroll=3)
            if save and s==1: self.out(l,"pb","ctx")
        def proj_out():
            self.wcp(l,3).wait()
            z=dot(self.ctx[...],self.W(3))+V(2)+x[...].astype(f32)
            xh,rstd,h=self.ln(z,V(3),V(4))
            if save: self.xh1[...]=xh; self.rs1[...]=jnp.broadcast_to(rstd,(512,128))
            self.h1[...]=h.astype(bf16)
            self.acc[...]=h+V(5)
            if save: self.out(l,"xh1","rs1","h1")
        return [functools.partial(proj_in,j) for j in range(3)]+[functools.partial(attend,s) for s in range(2)]+[proj_out]
    def ffn_steps(self,l,save,y,lens,pooled):
        V=lambda i: self.vecs[l,i:i+1,:]
        def part(j):
            if j==0: self.load(l,[4,8,5,9,6,10,7,11])
            self.wcp(l,4+j).wait(); self.wcp(l,8+j).wait()
            u=dot(self.h1[...],self.W(4+j))+V(8+j)
            cdf,pdf=phi_parts(u)
            gb=(u*cdf).astype(bf16)
            if save:
                self.act[:,j*768:(j+1)*768]=gb
                self.der[:,j*768:(j+1)*768]=(cdf+u*pdf).astype(bf16)
            self.acc[...]+=dot(gb,self.S(j))
            if save and j==3: self.out(l,"act","der")
        def end():
            xh,rstd,yy=self.ln(self.acc[...],V(6),V(7))
            if save:
                self.xh2[...]=xh; self.rs2[...]=jnp.broadcast_to(rstd,(512,128)); self.out(l,"xh2","rs2")
            y[...]=yy.astype(bf16)
            if pooled is not None:
                tpos=lax.broadcasted_iota(jnp.int32,(256,768),0)
                for c in range(2):
                    pooled[c:c+1,:]=jnp.sum(jnp.where(tpos<lens[c],yy[c*256:(c+1)*256],0.0),0,keepdims=True)/lens[c].astype(f32)
        return [functools.partial(part,j) for j in range(4)]+[end]

def unit_scale(p): return lax.rsqrt(jnp.sum(p*p,-1,keepdims=True)+1e-6)

class Contrast:
    def __init__(self,pos,queue,lens,R):
        self.p,self.queue,self.lens=pos,queue,lens
        self.__dict__.update(R)
    def ucp(self,s):
        _,dev=self.p.peer(s)
        return remote(self.units.at[self.p.me],self.units.at[self.p.me],self.us.at[s],self.ur.at[s],dev)
    def gcp(self,s):
        j,dev=self.p.peer(s)
        return remote(self.sends.at[j],self.gets.at[self.p.me],self.gs.at[s],self.gr.at[s],dev)
    def loop(self,fn): lax.fori_loop(1,self.p.N,lambda s,_: (fn(s),0)[1],0)
    def send_units(self):
        p=self.pool_q[...]
        self.units[self.p.me]=(p*unit_scale(p)).astype(bf16).astype(f32)
        self.loop(lambda s: self.ucp(s).start())
    def share(self):
        self.loop(lambda s: self.ucp(s).wait_recv())
        N=self.p.N
        for i in range(N): self.q_all[2*i:2*i+2,:]=self.units[i]
        lg=dot_t(self.q_all[...].astype(bf16),self.queue[...])*(1.0/SHARP)
        m=jnp.max(lg,-1,keepdims=True)
        e=jnp.exp(lg-m)
        self.part[:,0:768]=dot(e.astype(bf16),self.queue[...])
        self.part[:,768:896]=jnp.broadcast_to(m,(2*N,128))
        self.part[:,896:1024]=jnp.broadcast_to(jnp.sum(e,-1,keepdims=True),(2*N,128))
        for i in range(N): self.sends[i]=self.part[2*i:2*i+2,:]
        self.gets[self.p.me]=self.sends[self.p.me]
        self.loop(lambda s: self.gcp(s).start())
    def end(self,loss,grad):
        pk=self.pool_k[...]; pq=self.pool_q[...]
        ku=(pk*unit_scale(pk)).astype(bf16).astype(f32)
        rs=unit_scale(pq)
        qu=(pq*rs).astype(bf16).astype(f32)
        pos=jnp.sum(qu*ku,-1,keepdims=True)/SHARP
        self.loop(lambda s: self.gcp(s).wait_recv())
        mi=self.gets[:,:,768:896]
        top=jnp.maximum(jnp.max(mi,0),pos)
        w=jnp.exp(mi-top[None])
        pe=jnp.exp(pos-top)
        total=jnp.sum(w*self.gets[:,:,896:1024],0)+pe
        loss[...]=top+jnp.log(total)-pos
        scale=FACTOR/SHARP
        inv=scale/total
        cp=scale*(pe/total-1.0)
        for k in range(6):
            cols=slice(k*128,(k+1)*128)
            grad[:,cols]=jnp.sum(w*self.gets[:,:,cols],0)*inv+cp*ku[:,cols]
        g=grad[...]
        d=rs*g-pq*(rs*rs*rs)*jnp.sum(pq*g,-1,keepdims=True)
        for c in range(2): grad[c:c+1,:]=d[c:c+1]/self.lens[c].astype(f32)
    def finish(self):
        self.loop(lambda s: self.ucp(s).wait_send())
        self.loop(lambda s: self.gcp(s).wait_send())

def forward_kernel(D,F,pre,names,lenq,lenk,xq,xk,queue,msg,qw,pw,ew,sw,kqw,kpw,kew,ksw,
                   g,vecs,y0,y1,loss,gp,*rest):
    outs=(rest[:10],rest[10:20]); R=dict(zip(names,rest[20:]))
    pos=Place(D,F); r=768//F; rs=3072//F; f=pos.f
    bar=pltpu.get_barrier_semaphore()
    def hello(s,_):
        _,dev=pos.peer(s)
        pl.semaphore_signal(bar,inc=1,device_id=dev,device_id_type=MESH); return 0
    lax.fori_loop(1,pos.N,hello,0)
    def own(l,j):
        dst=lambda j,n: g.at[l,f,pl.ds(j*r,n)]
        if j<3: s,d=qw.at[l,:,pl.ds(j*768,768)],dst(j,r)
        elif j==3: s,d=pw.at[l],dst(3,r)
        elif j<8: s,d=ew.at[l,:,pl.ds((j-4)*768,768)],dst(j,r)
        else: s,d=sw.at[l],dst(8,rs)
        return pltpu.make_async_copy(s,d,R["lsem"].at[l,j])
    groups={0:range(4),1:range(4,9)}
    for l in range(2):
        for j in range(9): own(l,j).start()
    def kload(l):
        pairs=[(kqw,"kq"),(kpw,"kp"),(kew,"ke"),(ksw,"ks"),(qw,"qq"),(pw,"qp"),(ew,"qe"),(sw,"qs")]
        return [pltpu.make_async_copy(a.at[l],R[b],R["ksem"].at[i]) for i,(a,b) in enumerate(pairs)]
    def mcp(l): return pltpu.make_async_copy(R["mo"].at[l],g.at[2+l,f],R["msem"].at[l])
    for c in kload(0): c.start()
    def mirror(l):
        for c in kload(l): c.wait()
        mo=R["mo"]
        mix=lambda k,q: (MOM*k+(1.0-MOM)*q.astype(f32)).astype(bf16)
        for j in range(3):
            cols=slice(j*768,(j+1)*768); mo[l,j*r:(j+1)*r,:]=mix(R["kq"][:,cols],R["qq"][:,cols])
        mo[l,3*r:4*r,:]=mix(R["kp"][...],R["qp"][...])
        for j in range(4):
            cols=slice(j*768,(j+1)*768); mo[l,(4+j)*r:(5+j)*r,:]=mix(R["ke"][:,cols],R["qe"][:,cols])
        mo[l,8*r:8*r+rs,:]=mix(R["ks"][...],R["qs"][...])
        mcp(l).start()
        if l==0:
            for c in kload(1): c.start()
    waited=set()
    def ready(q):
        l=q//2
        if l<2:
            for j in groups[q%2]: own(l,j).wait()
        elif l not in waited:
            waited.add(l); mcp(l-2).wait()
    chunks=[(l,r0,n) for l in range(4) for r0,n in ((0,4*r),(4*r,8*r))]
    G=Gather(pos,g,chunks,ready,[R[k] for k in ("zs","zr","ys","yr","xs","xr","cs","cr","ks_","kr_")])
    vmsg=R["vmsg"]
    def vcp(s): return remote(msg,vmsg.at[f],R["vs"].at[s],R["vr"].at[s],(pos.d,(f+s)%F))
    vmsg[f]=msg[...]
    pl.semaphore_wait(bar,pos.N-1)
    G.start(0)
    for s in range(1,F): vcp(s).start()
    def vectors():
        for s in range(1,F): vcp(s).wait_recv()
        row=lax.broadcasted_iota(jnp.int32,(128,768),0); col=lax.broadcasted_iota(jnp.int32,(128,768),1)
        v=jnp.zeros((32,768),f32)
        for i in range(F):
            hot=jnp.logical_and(col==row+i*r,row<r)
            v=v+dot(vmsg[i,:,0:128],jnp.where(hot,1.0,0.0).astype(bf16))
        row=lax.broadcasted_iota(jnp.int32,(384,768),0); col=lax.broadcasted_iota(jnp.int32,(384,768),1)
        for l in range(4): vecs[l,0:8,:]=v[8*l:8*l+8]; vecs[l,8:16,:]=jnp.zeros((8,768),f32)
        for j in range(4):
            e=jnp.zeros((32,768),f32)
            for i in range(F//4):
                hot=jnp.logical_and(col==row+i*rs,row<rs)
                e=e+dot(vmsg[j*(F//4)+i,:,128:512],jnp.where(hot,1.0,0.0).astype(bf16))
            for l in range(4): vecs[l,8+j:9+j,:]=e[8*l:8*l+1]
    Fw=Forward(g,vecs,None,R); Fw.outs=outs
    Ct=Contrast(pos,queue,lenq,R)
    yk=R["yk"]
    work=[]
    for l,(save,x,y,lens,pool) in enumerate([(True,xq,y0,lenq,None),(True,y0,y1,lenq,R["pool_q"]),(False,xk,yk,lenk,None),(False,yk,R["yl"],lenk,R["pool_k"])]):
        work.append(Fw.attn_steps(l,save,x,lens,(lambda k=l-1: Fw.drain(k)) if l in (1,2) else None))
        work.append(Fw.ffn_steps(l,save,y,lens,pool))
    work[3].append(Ct.send_units)
    work[4].append(Ct.share)
    interleave(G.handlers(0,pre),[vectors,lambda: mirror(0),lambda: mirror(1)])
    for q in range(1,8): interleave(G.handlers(q,pre),work[q-1])
    for s in work[7]: s()
    Ct.end(loss,gp)
    G.finish(); Ct.finish()
    for s in range(1,F): vcp(s).wait_send()

def forward(D,F,lenq,lenk,xq,xk,queue,msg,mats,kmats,cid,pre=2):
    sd=jax.ShapeDtypeStruct; S=pltpu.SemaphoreType.DMA; VM=pltpu.VMEM
    V=pl.BlockSpec(memory_space=pltpu.VMEM); ANY=pl.BlockSpec(memory_space=pl.ANY); SM=pl.BlockSpec(memory_space=pltpu.SMEM)
    A=4;B=F//4;Q=8;N=D*F; r=768//F; rs=3072//F; M=2*A*B
    buf=dict(zip(SAVED,[VM(s.shape,s.dtype) for s in saved_shapes()]))
    buf.update(acc=VM((512,768),f32),yk=VM((512,768),bf16),yl=VM((512,768),bf16),wv=VM((8,F,r,768),bf16),sv=VM((4,F//4,rs,768),bf16),
        pool_q=VM((2,768),f32),pool_k=VM((2,768),f32),units=VM((N,2,768),f32),q_all=VM((2*N,768),f32),part=VM((2*N,1024),f32),
        sends=VM((N,2,1024),f32),gets=VM((N,2,1024),f32),vmsg=VM((F,32,512),bf16),
        kq=VM((r,2304),f32),kp=VM((r,768),f32),ke=VM((r,3072),f32),ks=VM((rs,768),f32),qq=VM((r,2304),bf16),qp=VM((r,768),bf16),qe=VM((r,3072),bf16),qs=VM((rs,768),bf16),
        mo=VM((2,12*r,768),bf16),
        wsem=S((12,)),osem=S((2,10)),lsem=S((2,9)),ksem=S((8,)),msem=S((2,)),us=S((N,)),ur=S((N,)),gs=S((N,)),gr=S((N,)),vs=S((F,)),vr=S((F,)),
        zs=S((Q,2,A)),zr=S((Q,2,A)),ys=S((Q,2*A,B)),yr=S((Q,2*A,B)),xs=S((Q,M)),xr=S((Q,M)),cs=S((Q,M)),cr=S((Q,M)),ks_=S((Q,M)),kr_=S((Q,M)))
    saved=saved_shapes()
    outs=[sd((4,F,12*r,768),bf16),sd((4,16,768),f32),sd((512,768),bf16),sd((512,768),bf16),sd((2,128),f32),sd((2,768),f32)]+saved*2
    res=pl.pallas_call(functools.partial(forward_kernel,D,F,pre,list(buf)),out_shape=outs,
        in_specs=[SM,SM,V,V,V,V]+[ANY]*8,out_specs=[ANY,V,V,V,V,V]+[ANY]*20,scratch_shapes=list(buf.values()),
        compiler_params=pltpu.CompilerParams(collective_id=cid,has_side_effects=True,vmem_limit_bytes=61<<20),name="forward")(lenq,lenk,xq,xk,queue,msg,*mats,*kmats)
    return res[:6],res[6:16],res[16:26]
def bwd_kernel(l,first,lens,dyin,x,vec,g,qkv_i,pb_i,ctx_i,xh1_i,rs1_i,h1_i,act_i,der_i,xh2_i,rs2_i,
               dx,dg,vg,wv,sv,qkv,pb,ctx,xh1,rs1,h1,act,der,xh2,rs2,dmix,dacc,dr2,dctx,dv,ds,sem,isem,osem):
    F=g.shape[1]; r=768//F; rs_=3072//F
    cps=load_weights(l,g,wv,sv,sem)
    ins=[pltpu.make_async_copy(s,d,isem.at[i]) for i,(s,d) in enumerate([(qkv_i,qkv),(pb_i,pb),(ctx_i,ctx),(xh1_i,xh1),(rs1_i,rs1),(h1_i,h1),(act_i,act),(der_i,der),(xh2_i,xh2),(rs2_i,rs2)])]
    QKV,PB,CTX,XH1,RS1,H1,ACT,DER,XH2,RS2=range(10)
    for i in (XH2,RS2): ins[i].start()
    for j in range(4):
        cps[8+j].start()
        if j==0: ins[ACT].start(); ins[DER].start(); ins[H1].start()
        cps[4+j].start()
    for i in (XH1,RS1,CTX): ins[i].start()
    cps[3].start(); ins[QKV].start(); ins[PB].start()
    for j in range(3): cps[j].start()
    def W(j): return wv[j].reshape(768,768)
    def S(j): return sv[j].reshape(768,768)
    outs=[]
    def outw(j,val):
        if j<8:
            dv[j]=val.astype(bf16).reshape(F,r,768)
            cp=pltpu.make_async_copy(dv.at[j],dg.at[:,pl.ds(j*r,r),:],osem.at[j])
        else:
            q=j-8
            ds[q]=val.astype(bf16).reshape(F//4,rs_,768)
            cp=pltpu.make_async_copy(ds.at[q],dg.at[pl.ds(q*(F//4),F//4),pl.ds(8*r,rs_),:],osem.at[j])
        cp.start(); outs.append(cp)
    vg[...]=jnp.zeros_like(vg)
    tpos=lax.broadcasted_iota(jnp.int32,(256,768),0)
    if first:
        dy=jnp.concatenate([jnp.where(tpos<lens[c],dyin[c:c+1,:],0.0) for c in range(2)],0)
    else: dy=dyin[...]
    def ln_back(dy,xh,rstd,gain):
        t=dy*gain
        return rstd*(t-jnp.mean(t,-1,keepdims=True)-xh*jnp.mean(t*xh,-1,keepdims=True))
    def colsum(v): return jnp.sum(v,0,keepdims=True)
    ins[XH2].wait(); ins[RS2].wait()
    xh=xh2[...]
    vg[6:7,:]=colsum(dy*xh); vg[7:8,:]=colsum(dy)
    d2=ln_back(dy,xh,rs2[:,0:1],vec[6:7,:])
    dacc[...]=d2
    dfb=d2.astype(bf16)
    dr2[...]=dfb
    vg[5:6,:]=colsum(dfb.astype(f32))
    for i in (ACT,DER,H1): ins[i].wait()
    for j in range(4):
        cps[8+j].wait(); cps[4+j].wait()
        a=act[:,j*768:(j+1)*768]
        outw(8+j,tdot(a,dr2[...]))
        du=(dot_t(dr2[...],S(j))*der[:,j*768:(j+1)*768].astype(f32)).astype(bf16)
        vg[8+j:9+j,:]=colsum(du.astype(f32))
        outw(4+j,tdot(h1[...],du))
        dacc[...]+=dot_t(du,W(4+j))
    for i in (XH1,RS1,CTX): ins[i].wait()
    dh=dacc[...]; xh=xh1[...]
    vg[3:4,:]=colsum(dh*xh); vg[4:5,:]=colsum(dh)
    d1=ln_back(dh,xh,rs1[:,0:1],vec[3:4,:])
    dacc[...]=d1
    dr2[...]=d1.astype(bf16)
    vg[2:3,:]=colsum(dr2[...].astype(f32))
    cps[3].wait()
    outw(3,tdot(ctx[...],dr2[...]))
    dctx[...]=dot_t(dr2[...],W(3)).astype(bf16)
    ins[QKV].wait(); ins[PB].wait()
    lane=lax.broadcasted_iota(jnp.int32,(256,128),1); low_half=lane<64
    def pair(i,_):
        c=i//6; p=i-c*6
        rows=pl.ds(pl.multiple_of(c*256,256),256); o=pl.multiple_of(p*128,128)
        o1=pl.multiple_of(768+o,128); o2=pl.multiple_of(1536+o,128)
        q2=qkv[rows,pl.ds(o,128)]; k2=qkv[rows,pl.ds(o1,128)]; v2=qkv[rows,pl.ds(o2,128)]
        dc=dctx[rows,pl.ds(o,128)]
        res=[]
        for hh in range(2):
            m=low_half if hh==0 else jnp.logical_not(low_half)
            P=pb[i*2+hh]; pf=P.astype(f32)
            dP=dot_t(jnp.where(m,dc,jnp.zeros_like(dc)),v2)
            pd=pf*dP
            dS=(pd-pf*jnp.sum(pd,-1,keepdims=True)).astype(bf16)
            res.append((dot(dS,k2),tdot(dS,q2),tdot(P,dc)))
        sel=lambda t: jnp.where(low_half,res[0][t],res[1][t])
        dmix[rows,pl.ds(o,128)]=(sel(0)*0.125).astype(bf16)
        dmix[rows,pl.ds(o1,128)]=(sel(1)*0.125).astype(bf16)
        dmix[rows,pl.ds(o2,128)]=sel(2).astype(bf16)
        return 0
    lax.fori_loop(0,12,pair,0,unroll=3)
    for j in range(3):
        cps[j].wait()
        dm=dmix[:,j*768:(j+1)*768]
        if j==0: vg[0:1,:]=colsum(dm.astype(f32))
        if j==2: vg[1:2,:]=colsum(dm.astype(f32))
        outw(j,tdot(x[...],dm))
        dacc[...]+=dot_t(dm,W(j))
    dx[...]=dacc[...].astype(dx.dtype)
    for c in outs: c.wait()

def layer_bwd(l,first,lens,dy,x,vec,g,saved,dxt):
    F=g.shape[1]; sd=jax.ShapeDtypeStruct
    V=pl.BlockSpec(memory_space=pltpu.VMEM); ANY=pl.BlockSpec(memory_space=pl.ANY)
    S=pltpu.SemaphoreType.DMA
    w=[pltpu.VMEM((8,F,768//F,768),bf16),pltpu.VMEM((4,F//4,3072//F,768),bf16)]
    scr=w+[pltpu.VMEM(s.shape,s.dtype) for s in saved]+[pltpu.VMEM((512,2304),bf16),pltpu.VMEM((512,768),f32),pltpu.VMEM((512,768),bf16),pltpu.VMEM((512,768),bf16)]+w+[S((12,)),S((10,)),S((12,))]
    return pl.pallas_call(functools.partial(bwd_kernel,l,first),out_shape=[sd((512,768),dxt),sd((F,12*768//F,768),bf16),sd((16,768),f32)],
        in_specs=[pl.BlockSpec(memory_space=pltpu.SMEM),V,V,V]+[ANY]*11,out_specs=[V,ANY,V],scratch_shapes=scr,
        compiler_params=pltpu.CompilerParams(vmem_limit_bytes=61<<20),name="layer_bwd")(lens,dy,x,vec,g,*saved)

def sizes(F):
    n=4*(768//F); np_=n//3; nq=n-np_
    return n,np_,nq
def rs_scratch(D,F,NP):
    A=4;B=F//4;O=D//4; n,np_,nq=sizes(F); nh=n//2; Sm=pltpu.SemaphoreType.DMA
    V=pltpu.VMEM
    return dict(T=V((NP,F,n,384),bf16),RC=V((NP,F,n,384),bf16),RPX=V((NP,F,np_//2,384),bf16),RPY=V((NP,B-1,A,np_//2,384),bf16),
      RQY=V((NP,B-1,A,nq,384),bf16),RQX=V((NP,A,nq//2,384),bf16),T3=V((NP,A,nh,384),bf16),RZ=V((NP,A-1,nh,384),bf16),
      **(dict(RO=V((NP,O-1,nh,384),bf16),TO=V((NP,nh,384),bf16)) if O>1 else {}),
      VS=V((5,32,768),f32),VRC=V((1,32,768),f32),VRX=V((1,32,768),f32),VRY=V((B-1,32,768),f32),VRZ=V((A-1,32,768),f32),
      **(dict(VRO=V((O-1,32,768),f32)) if O>1 else {}),
      LS=Sm((NP,)),SS=Sm((NP,8+B+A+B+A+O,)),RS=Sm((NP,8+B+A+B+A+O)),VSS=Sm((8+B+A+O,)),VRS=Sm((8+B+A+O,)))
class Reduce:
    def __init__(self,D,F,src,fin,vin,vout,buf):
        self.D,self.F=D,F; self.A=4; self.B=F//4; self.O=D//4
        d=lax.axis_index("dp"); f=lax.axis_index("fsdp")
        self.d,self.f=d,f; self.a=f//self.B; self.b=f%self.B; self.x=(d//2)%2; self.c=d%2; self.o=d//4
        self.xd=d+2-4*self.x; self.cd=d+1-2*self.c
        self.src,self.fin,self.vin,self.vout=src,fin,vin,vout
        self.__dict__.update(buf); self.n,self.np,self.nq=sizes(F)
        self.hp=self.np//2; self.hq=self.nq//2
        self.pending=[]
        m=pl.multiple_of
        self.mycols=pl.ds(m(self.c*384,128),384); self.ocols=pl.ds(m((1-self.c)*384,128),384)
        self.Pown=pl.ds(m(self.x*self.hp,16),self.hp); self.Poth=pl.ds(m((1-self.x)*self.hp,16),self.hp)
        self.Qown=pl.ds(m(self.np+self.x*self.hq,16),self.hq); self.Qoth=pl.ds(m(self.np+(1-self.x)*self.hq,16),self.hq)
        self.Qall=pl.ds(self.np,self.nq)
    def peers(self):
        out=[(self.d,(self.f+s)%self.F) for s in range(1,self.F)]
        out+=[(self.xd,self.f),(self.cd,self.f)]+[((self.d+4*s)%self.D,self.f) for s in range(1,self.O)]
        return out
    def rc(self,i,k,src,dst,dev):
        cp=pltpu.make_async_remote_copy(src,dst,self.SS.at[i,k],self.RS.at[i,k],device_id=dev,device_id_type=MESH)
        return cp
    def go(self,cp): cp.start(); self.pending.append(cp)
    def kPy(self,t): return 8+t
    def kQy(self,t): return 8+self.B+t
    def kZ(self,s): return 8+2*self.B+s
    def kO(self,s): return 8+2*self.B+self.A+s
    def Yd(self,t): return (self.d,self.a*self.B+(self.b+t)%self.B)
    def Zd(self,s): return (self.d,((self.a+s)%self.A)*self.B+self.b)
    def s0(self,i):
        s=self.src(i)
        self.cC=lambda i: self.rc(i,0,self.src(i).at[:,:,self.ocols],self.RC.at[i],(self.cd,self.f))
        self.go(self.cC(i))
        self.lc=lambda i: pltpu.make_async_copy(self.src(i).at[:,:,self.mycols],self.T.at[i],self.LS.at[i])
        self.lc(i).start()
    def s1(self,i):
        self.lc(i).wait(); self.cC(i).wait_recv()
        T,RC=self.T,self.RC
        def body(f,_):
            T[i,f]=(T[i,f].astype(f32)+RC[i,f].astype(f32)).astype(bf16); return 0
        lax.fori_loop(0,self.F,body,0)
        self.go(self.cPx(i))
        for t in range(1,self.B):
            for a in range(self.A): pass
        for t in range(1,self.B):
            fb=(self.b+t)%self.B
            for a in range(self.A):
                pass
        self.startQy(i)
    def cPx(self,i): return self.rc(i,1,self.T.at[i,:,self.Poth],self.RPX.at[i],(self.xd,self.f))
    def Tab(self,i):
        return self.T.at[i].reshape(self.A,self.B,self.n,384)
    def cQy(self,i,t): return self.rc(i,self.kQy(t),self.Tab(i).at[:,(self.b+t)%self.B,self.Qall],self.RQY.at[i,t-1],self.Yd(t))
    def cPy(self,i,t): return self.rc(i,self.kPy(t),self.Tab(i).at[:,(self.b+t)%self.B,self.Pown],self.RPY.at[i,t-1],self.Yd(t))
    def startQy(self,i):
        for t in range(1,self.B): self.go(self.cQy(i,t))
    def s2(self,i):
        T=self.T
        self.cPx(i).wait_recv()
        def body(f,_):
            T[i,f,self.Pown]=(T[i,f,self.Pown].astype(f32)+self.RPX[i,f].astype(f32)).astype(bf16); return 0
        lax.fori_loop(0,self.F,body,0)
        for t in range(1,self.B): self.go(self.cPy(i,t))
        for t in range(1,self.B): self.cQy(i,t).wait_recv()
        def bodyq(a,_):
            fo=a*self.B+self.b
            v=T[i,fo,self.Qall].astype(f32)
            for t in range(1,self.B): v=v+self.RQY[i,t-1,a].astype(f32)
            T[i,fo,self.Qall]=v.astype(bf16); return 0
        lax.fori_loop(0,self.A,bodyq,0)
        self.go(self.cQx(i))
    def cQx(self,i): return self.rc(i,2,self.Tab(i).at[:,self.b,self.Qoth],self.RQX.at[i],(self.xd,self.f))
    def s3(self,i):
        for t in range(1,self.B): self.cPy(i,t).wait_recv()
        self.cQx(i).wait_recv()
        def body(a,_):
            fo=a*self.B+self.b
            v=self.T[i,fo,self.Pown].astype(f32)
            for t in range(1,self.B): v=v+self.RPY[i,t-1,a].astype(f32)
            self.T3[i,a,0:self.hp]=v.astype(bf16)
            self.T3[i,a,self.hp:self.hp+self.hq]=(self.T[i,fo,self.Qown].astype(f32)+self.RQX[i,a].astype(f32)).astype(bf16)
            return 0
        lax.fori_loop(0,self.A,body,0)
        for s in range(1,self.A): self.go(self.cZ(i,s))
    def cZ(self,i,s): return self.rc(i,self.kZ(s),self.T3.at[i,(self.a+s)%self.A],self.RZ.at[i,s-1],self.Zd(s))
    def cO(self,i,s): return self.rc(i,self.kO(s),self.TO.at[i],self.RO.at[i,s-1],((self.d+4*s)%self.D,self.f))
    def put(self,i,v):
        v=v.astype(bf16)
        self.fin[i,self.Pown,self.mycols]=v[:self.hp]; self.fin[i,self.Qown,self.mycols]=v[self.hp:]
        self.go(self.cFX(i,0)); self.go(self.cFX(i,1))
    def cFX(self,i,w):
        r=(self.Pown,self.Qown)[w]; v=self.fin.at[i,r,self.mycols]
        return self.rc(i,3+w,v,v,(self.xd,self.f))
    def rFX(self,i,w):
        r=(self.Poth,self.Qoth)[w]; v=self.fin.at[i,r,self.mycols]
        return self.rc(i,3+w,v,v,(self.xd,self.f))
    def s4(self,i):
        v=self.T3[i,self.a].astype(f32)
        for s in range(1,self.A):
            self.cZ(i,s).wait_recv()
            v=v+self.RZ[i,s-1].astype(f32)
        if self.O>1:
            self.TO[i]=v.astype(bf16)
            for s in range(1,self.O): self.go(self.cO(i,s))
            for s in range(1,self.O):
                self.cO(i,s).wait_recv(); v=v+self.RO[i,s-1].astype(f32)
        self.put(i,v)
    def s5(self,i):
        for w in (0,1): self.rFX(i,w).wait_recv()
        v=self.fin.at[i,:,self.mycols]; self.go(self.rc(i,5,v,v,(self.cd,self.f)))
    def s6(self,i):
        v=self.fin.at[i,:,self.ocols]; self.rc(i,5,v,v,(self.cd,self.f)).wait_recv()
    def vstage(self,k):
        st=[(self.VRC,[(self.cd,self.f)],0),(self.VRX,[(self.xd,self.f)],1),(self.VRY,[self.Yd(t) for t in range(1,self.B)],8),(self.VRZ,[self.Zd(s) for s in range(1,self.A)],8+self.B)]
        if self.O>1: st.append((self.VRO,[((self.d+4*s)%self.D,self.f) for s in range(1,self.O)],8+self.B+self.A))
        def cps(k):
            buf,devs,k0=st[k]
            return [pltpu.make_async_remote_copy(self.VS.at[k],buf.at[q],self.VSS.at[k0+q],self.VRS.at[k0+q],device_id=dv,device_id_type=MESH) for q,dv in enumerate(devs)]
        if k==0: self.VS[0]=self.vin[...]
        elif k<=len(st):
            v=self.VS[k-1]
            for q,cp in enumerate(cps(k-1)):
                cp.wait_recv(); v=v+st[k-1][0][q]
            if k<len(st): self.VS[k]=v
            else: self.vout[...]=v
        if k<len(st):
            for cp in cps(k): self.go(cp)
    def finish(self):
        for cp in self.pending: cp.wait_send()

def rs_kernel(D,F,names,dgs,vin,fin,vout,*scr):
    buf=dict(zip(names,scr))
    n=4*(768//F)
    NP=3*len(dgs)
    src=lambda i: dgs[i//3].at[:,pl.ds((2-i%3)*n,n),:]
    R=Reduce(D,F,src,fin,vin,vout,buf)
    bar=pltpu.get_barrier_semaphore(); ps=R.peers()
    for p in ps: pl.semaphore_signal(bar,inc=1,device_id=p,device_id_type=MESH)
    pl.semaphore_wait(bar,len(ps))
    stages=[R.s0,R.s1,R.s2,R.s3,R.s4,R.s5,R.s6]
    for t in range(NP+6):
        if t<6: R.vstage(t)
        for i in range(NP):
            if 0<=t-i<=6: stages[t-i](i)
    R.finish()

def reduce_grads(D,F,dgs,vin,cid):
    n,np_,nq=sizes(F); NP=3*len(dgs)
    buf=rs_scratch(D,F,NP); sd=jax.ShapeDtypeStruct
    V=pl.BlockSpec(memory_space=pltpu.VMEM); ANY=pl.BlockSpec(memory_space=pl.ANY)
    def k(*refs):
        nd=len(dgs)
        rs_kernel(D,F,list(buf),refs[:nd],refs[nd],refs[nd+1],refs[nd+2],*refs[nd+3:])
    return pl.pallas_call(k,out_shape=[sd((NP,n,768),bf16),sd((32,768),f32)],in_specs=[ANY]*len(dgs)+[V],out_specs=[V,V],
        scratch_shapes=list(buf.values()),compiler_params=pltpu.CompilerParams(collective_id=cid,has_side_effects=True,vmem_limit_bytes=61<<20),name="reduce_grads")(*dgs,vin)


def on_device(dp, fsdp, x_query, x_key, len_query, len_key, queue, *params):
    query_params, key_params = params[:13], params[13:]
    num_crops, seq_len, width = x_query.shape
    r = width // fsdp
    order = (1, 2, 4, 5, 6, 10, 11, 12)
    small_q = jnp.stack([query_params[i] for i in order], 1)
    small_k = jnp.stack([key_params[i] for i in order], 1)
    bias_q, bias_k = query_params[8], key_params[8]
    mix = lambda k, q: (MOM * k + (1.0 - MOM) * q.astype(f32)).astype(bf16)
    small = jnp.concatenate([small_q, mix(small_k, small_q)], 0).reshape(32, r)
    wide = jnp.concatenate([bias_q, mix(bias_k, bias_q)], 0)
    wide = jnp.pad(wide[:, None, :], ((0, 0), (0, 7), (0, 384 - wide.shape[1]))).reshape(32, 384)
    msg = jnp.concatenate([jnp.pad(small, ((0, 0), (0, 128 - r))), wide], 1)
    big = (0, 3, 7, 9)
    x0 = x_query.reshape(num_crops * seq_len, width)
    xk = x_key.reshape(num_crops * seq_len, width)
    (gathered, vecs, y0, y1, loss, grad_pooled), saved0, saved1 = forward(
        dp, fsdp, len_query, len_key, x0, xk, queue, msg,
        [query_params[i] for i in big], [key_params[i] for i in big], 1)
    dx1, d1, v1 = layer_bwd(1, True, len_query, grad_pooled, y0, vecs[1], gathered, saved1, f32)
    dx0, d0, v0 = layer_bwd(0, False, len_query, dx1, x0, vecs[0], gathered, saved0, bf16)
    fin, vsum = reduce_grads(dp, fsdp, [d1, d0], jnp.concatenate([v1, v0], 0), 2)
    me = lax.axis_index("fsdp")
    n = fin.shape[1]
    fin = fin.astype(f32).reshape(2, 3, n, width)[::-1]
    sh_g, ex_g, at_g = fin[:, 0], fin[:, 1], fin[:, 2]
    grad_qkv = jnp.concatenate([at_g[:, i * r : (i + 1) * r] for i in range(3)], 2)
    grad_proj = at_g[:, 3 * r :]
    grad_expand = jnp.concatenate([ex_g[:, i * r : (i + 1) * r] for i in range(4)], 2)
    vsum = vsum.reshape(2, 16, width)[::-1]
    mine = lax.dynamic_slice_in_dim(vsum[:, :8], me * r, r, 2)
    ebg = lax.dynamic_slice_in_dim(vsum[:, 8:12].reshape(2, 4 * width), me * 4 * r, 4 * r, 1)
    qb, vb, pb, g1, b1, sb, g2, b2 = [mine[:, i] for i in range(8)]
    hidden = y1.reshape(num_crops, seq_len, width)
    grad_input = dx0.reshape(num_crops, seq_len, width)
    return (hidden, grad_input, grad_qkv, qb, vb, grad_proj, pb, g1, b1, grad_expand, ebg, sh_g, sb, g2, b2, loss[:, 0])


def solution(mesh):
    in_specs = (
        P(("dp", "fsdp"), None, None),
        P(("dp", "fsdp"), None, None),
        P(("dp", "fsdp")),
        P(("dp", "fsdp")),
        P(("dp", "fsdp"), None),
        P(None, "fsdp", None),
        P(None, "fsdp"),
        P(None, "fsdp"),
        P(None, "fsdp", None),
        P(None, "fsdp"),
        P(None, "fsdp"),
        P(None, "fsdp"),
        P(None, "fsdp", None),
        P(None, "fsdp"),
        P(None, "fsdp", None),
        P(None, "fsdp"),
        P(None, "fsdp"),
        P(None, "fsdp"),
        P(None, "fsdp", None),
        P(None, "fsdp"),
        P(None, "fsdp"),
        P(None, "fsdp", None),
        P(None, "fsdp"),
        P(None, "fsdp"),
        P(None, "fsdp"),
        P(None, "fsdp", None),
        P(None, "fsdp"),
        P(None, "fsdp", None),
        P(None, "fsdp"),
        P(None, "fsdp"),
        P(None, "fsdp"),
    )
    out_specs = (
        P(("dp", "fsdp"), None, None),
        P(("dp", "fsdp"), None, None),
        P(None, "fsdp", None),
        P(None, "fsdp"),
        P(None, "fsdp"),
        P(None, "fsdp", None),
        P(None, "fsdp"),
        P(None, "fsdp"),
        P(None, "fsdp"),
        P(None, "fsdp", None),
        P(None, "fsdp"),
        P(None, "fsdp", None),
        P(None, "fsdp"),
        P(None, "fsdp"),
        P(None, "fsdp"),
        P(("dp", "fsdp")),
    )
    return jax.shard_map(
        functools.partial(on_device, mesh.shape["dp"], mesh.shape["fsdp"]), mesh=mesh, in_specs=in_specs, out_specs=out_specs, check_vma=False
    )
```

```python
import functools

import jax
import jax.numpy as jnp
from jax import lax
from jax.experimental import pallas as pl
from jax.experimental.pallas import tpu as pltpu
from jax.sharding import PartitionSpec as P

f32=jnp.float32; bf16=jnp.bfloat16
HEADS=12
def dot(a,b): return lax.dot_general(a,b,(((1,),(0,)),((),())),preferred_element_type=f32)
def dot_t(a,b): return lax.dot_general(a,b,(((1,),(1,)),((),())),preferred_element_type=f32)
def tdot(a,b): return lax.dot_general(a,b,(((0,),(0,)),((),())),preferred_element_type=f32)

def phi_parts(u):
    z=jnp.abs(u)*0.7071067811865476
    t=1.0/(1.0+0.3275911*z)
    e=jnp.exp(-z*z)
    poly=t*(0.254829592+t*(-0.284496736+t*(1.421413741+t*(-1.453152027+t*1.061405429))))
    half=0.5*poly*e
    cdf=jnp.where(u>=0,1.0-half,half)
    return cdf,e*0.3989422804014327

def load_weights(l,g,wv,sv,sem):
    F=g.shape[1]; r=768//F; rs=3072//F
    cps=[]
    for j in range(8):
        cps.append(pltpu.make_async_copy(g.at[l,:,pl.ds(j*r,r),:],wv.at[j],sem.at[j]))
    for j in range(4):
        cps.append(pltpu.make_async_copy(g.at[l,pl.ds(j*(F//4),F//4),pl.ds(8*r,rs),:],sv.at[j],sem.at[8+j]))
    return cps

MESH=pl.DeviceIdType.MESH
SHARP=0.05
FACTOR=512.0
MOM=0.9995

def remote(src,dst,ss,rs,dev):
    return pltpu.make_async_remote_copy(src,dst,ss,rs,device_id=dev,device_id_type=MESH)

def when(cond,fn):
    if cond is True: fn()
    else: pl.when(cond)(fn)

class Place:
    def __init__(self,D,F):
        self.D,self.F=D,F; self.A=4; self.B=F//4; self.O=D//4
        d=self.d=lax.axis_index("dp"); f=self.f=lax.axis_index("fsdp")
        self.a=f//self.B; self.b=f%self.B; self.o=d//4; self.x=(d//2)%2; self.c=d%2
        self.xd=d+2-4*self.x; self.cd=d+1-2*self.c
        self.N=D*F; self.me=d*F+f
    def peer(self,s):
        p=(self.me+s)%self.N
        return p,(p//self.F,p%self.F)

class Gather:
    def __init__(self,pos,g,chunks,ready,sems):
        self.p,self.g,self.chunks,self.ready=pos,g,chunks,ready
        self.zs,self.zr,self.ys,self.yr,self.xs,self.xr,self.cs,self.cr,self.ks,self.kr=sems
    def rows(self,q,t0,n):
        return pl.ds(pl.multiple_of(self.chunks[q][1]+t0*16,16),n*16)
    def parts(self,q):
        p=self.p; half=self.chunks[q][2]//32; nx=(half*13+18)//36; nyz=half-nx
        h=p.c*half; hc=(1-p.c)*half
        R=lambda t0,n: self.rows(q,t0,n)
        return dict(yz=R(h+p.x*nx,nyz),xs=R(h+p.x*nyz,nx),xr=R(h+(1-p.x)*nyz,nx),oyz=R(hc+p.x*nx,nyz),oxr=R(hc+(1-p.x)*nyz,nx))
    def at(self,q,fs,part): return self.g.at[self.chunks[q][0],fs,self.parts(q)[part]]
    def src_a(self,hd): return self.p.a-hd[0] if hd[1]==0 else self.p.a+hd[0]
    def has(self,hd):
        if hd[0]==0: return True
        return (self.p.a>=hd[0]) if hd[1]==0 else (self.p.a+hd[0]<self.p.A)
    def canpass(self,dr): return (self.p.a+1<self.p.A) if dr==0 else (self.p.a>0)
    def z(self,q,hd,fs):
        na=self.p.a+1 if hd[1]==0 else self.p.a-1
        r=self.at(q,fs,"yz")
        return remote(r,r,self.zs.at[q,hd[1],hd[0]],self.zr.at[q,hd[1],hd[0]],(self.p.d,na*self.p.B+self.p.b))
    def slot(self,hd): return hd[0]*2+hd[1]
    def y(self,q,hd,fs,t):
        r=self.at(q,fs,"yz"); s=self.slot(hd)
        return remote(r,r,self.ys.at[q,s,t],self.yr.at[q,s,t],(self.p.d,self.p.a*self.p.B+(self.p.b+t)%self.p.B))
    def xc(self,q,fs,i,part="xs"):
        r=self.at(q,fs,part); return remote(r,r,self.xs.at[q,i],self.xr.at[q,i],(self.p.xd,self.p.f))
    def cc(self,q,fs,i,part="yz"):
        r=self.at(q,fs,part); return remote(r,r,self.cs.at[q,i],self.cr.at[q,i],(self.p.cd,self.p.f))
    def kc(self,q,fs,i,part="xr"):
        r=self.at(q,fs,part); return remote(r,r,self.ks.at[q,i],self.kr.at[q,i],(self.p.cd,self.p.f))
    def shard(self,hd,t=0): return self.src_a(hd)*self.p.B+(self.p.b-t)%self.p.B
    def hds(self,hh): return [(0,0)] if hh==0 else [(hh,0),(hh,1)]
    def start(self,q):
        self.ready(q)
        f=self.p.f
        for dr in (0,1): when(self.canpass(dr),lambda dr=dr: self.z(q,(1,dr),f).start())
        for t in range(1,self.p.B): self.y(q,(0,0),f,t).start()
    def on_z(self,q,hh):
        for hd in self.hds(hh):
            def go(hd=hd):
                fs=self.shard(hd); dr=hd[1]
                self.z(q,hd,fs).wait_recv()
                if hh+1<self.p.A: when(self.canpass(dr),lambda: self.z(q,(hh+1,dr),fs).start())
                for t in range(1,self.p.B): self.y(q,hd,fs,t).start()
                i=self.slot(hd)*self.p.B
                self.xc(q,fs,i).start(); self.cc(q,fs,i).start()
            when(self.has(hd),go)
    def on_y(self,q,hh):
        for hd in self.hds(hh):
            for t in range(1,self.p.B):
                def go(hd=hd,t=t):
                    fs=self.shard(hd,t); i=self.slot(hd)*self.p.B+t
                    self.y(q,hd,fs,t).wait_recv()
                    self.xc(q,fs,i).start(); self.cc(q,fs,i).start()
                when(self.has(hd),go)
    def each(self,hh,fn):
        for hd in self.hds(hh):
            for t in range(self.p.B):
                if hh==0 and t==0: continue
                when(self.has(hd),lambda hd=hd,t=t: fn(self.shard(hd,t),self.slot(hd)*self.p.B+t))
    def on_x(self,q,hh):
        def go(fs,i):
            self.xc(q,fs,i,"xr").wait_recv(); self.kc(q,fs,i).start()
        self.each(hh,go)
    def on_c(self,q):
        def go(fs,i):
            self.cc(q,fs,i,"oyz").wait_recv(); self.kc(q,fs,i,"oxr").wait_recv()
        for hh in range(self.p.A): self.each(hh,go)
    def finish(self):
        f=self.p.f
        for q in range(len(self.chunks)):
            def go(fs,i):
                self.xc(q,fs,i).wait_send(); self.cc(q,fs,i).wait_send(); self.kc(q,fs,i).wait_send()
            for hh in range(self.p.A):
                self.each(hh,go)
                for hd in self.hds(hh):
                    for t in range(1,self.p.B): when(self.has(hd),lambda hd=hd,t=t: self.y(q,hd,f,t).wait_send())
            for dr in (0,1):
                for hh in range(1,self.p.A):
                    cond=self.canpass(dr)
                    if hh>1: cond=jnp.logical_and(cond,self.has((hh-1,dr)))
                    pl.when(cond)(lambda hh=hh,dr=dr: self.z(q,(hh,dr),f).wait_send())

SAVED=("qkv","pb","ctx","xh1","rs1","h1","act","der","xh2","rs2")
def saved_shapes():
    sd=jax.ShapeDtypeStruct
    return [sd((512,2304),bf16),sd((24,256,256),bf16),sd((512,768),bf16),sd((512,768),f32),sd((512,128),f32),sd((512,768),bf16),sd((512,3072),bf16),sd((512,3072),bf16),sd((512,768),f32),sd((512,128),f32)]

class Forward:
    def __init__(self,g,vecs,lens,R):
        self.g,self.vecs,self.lens=g,vecs,lens
        self.__dict__.update(R)
    def W(self,j): return self.wv[j].reshape(768,768)
    def S(self,j): return self.sv[j].reshape(768,768)
    def load(self,l,js):
        for j in js: self.wcp(l,j).start()
    def wcp(self,l,j):
        F=self.g.shape[1]; r=768//F; rs=3072//F
        if j<8: return pltpu.make_async_copy(self.g.at[l,:,pl.ds(j*r,r),:],self.wv.at[j],self.wsem.at[j])
        j-=8
        return pltpu.make_async_copy(self.g.at[l,pl.ds(j*(F//4),F//4),pl.ds(8*r,rs),:],self.sv.at[j],self.wsem.at[8+j])
    def ocp(self,l,i): return pltpu.make_async_copy(self.__dict__[SAVED[i]],self.outs[l][i],self.osem.at[l,i])
    def out(self,l,*names):
        for n in names: self.ocp(l,SAVED.index(n)).start()
    def drain(self,l):
        for i in range(len(SAVED)): self.ocp(l,i).wait()
    def ln(self,z,gain,shift):
        mu=jnp.mean(z,-1,keepdims=True); cz=z-mu
        rstd=lax.rsqrt(jnp.mean(cz*cz,-1,keepdims=True)+1e-12)
        xh=cz*rstd
        return xh,rstd,xh*gain+shift
    def attn_steps(self,l,save,x,lens,before=None):
        V=lambda i: self.vecs[l,i:i+1,:]
        def proj_in(j):
            if j==0 and before: before()
            if j==0: self.load(l,range(4))
            self.wcp(l,j).wait()
            r=dot(x[...],self.W(j))
            if j==0: r=r+V(0)
            if j==2: r=r+V(1)
            self.qkv[:,j*768:(j+1)*768]=r.astype(bf16)
            if save and j==2: self.out(l,"qkv")
        lane=lax.broadcasted_iota(jnp.int32,(256,128),1); low_half=lane<64
        kpos=lax.broadcasted_iota(jnp.int32,(256,256),1)
        def pair(i,_):
            c=i//6; p=i-c*6
            rows=pl.ds(pl.multiple_of(c*256,256),256); o=pl.multiple_of(p*128,128)
            q2=self.qkv[rows,pl.ds(o,128)]*jnp.asarray(0.125,bf16)
            k2=self.qkv[rows,pl.ds(pl.multiple_of(768+o,128),128)]; v2=self.qkv[rows,pl.ds(pl.multiple_of(1536+o,128),128)]
            ok=kpos<lens[c]
            res=[]
            for hh in range(2):
                qm=jnp.where(low_half if hh==0 else jnp.logical_not(low_half),q2,jnp.zeros_like(q2))
                s=jnp.where(ok,dot_t(qm,k2),-1e9)
                e=jnp.exp(s-jnp.max(s,-1,keepdims=True))
                pr=(e*(1.0/jnp.sum(e,-1,keepdims=True))).astype(bf16)
                if save: self.pb[i*2+hh]=pr
                res.append(dot(pr,v2))
            self.ctx[rows,pl.ds(o,128)]=jnp.where(low_half,res[0],res[1]).astype(bf16)
            return 0
        def attend(s):
            lax.fori_loop(6*s,6*s+6,pair,0,unroll=3)
            if save and s==1: self.out(l,"pb","ctx")
        def proj_out():
            self.wcp(l,3).wait()
            z=dot(self.ctx[...],self.W(3))+V(2)+x[...].astype(f32)
            xh,rstd,h=self.ln(z,V(3),V(4))
            if save: self.xh1[...]=xh; self.rs1[...]=jnp.broadcast_to(rstd,(512,128))
            self.h1[...]=h.astype(bf16)
            self.acc[...]=h+V(5)
            if save: self.out(l,"xh1","rs1","h1")
        return [functools.partial(proj_in,j) for j in range(3)]+[functools.partial(attend,s) for s in range(2)]+[proj_out]
    def ffn_steps(self,l,save,y,lens,pooled):
        V=lambda i: self.vecs[l,i:i+1,:]
        def part(j):
            if j==0: self.load(l,[4,8,5,9,6,10,7,11])
            self.wcp(l,4+j).wait(); self.wcp(l,8+j).wait()
            u=dot(self.h1[...],self.W(4+j))+V(8+j)
            cdf,pdf=phi_parts(u)
            gb=(u*cdf).astype(bf16)
            if save:
                self.act[:,j*768:(j+1)*768]=gb
                self.der[:,j*768:(j+1)*768]=(cdf+u*pdf).astype(bf16)
            self.acc[...]+=dot(gb,self.S(j))
            if save and j==3: self.out(l,"act","der")
        def end():
            xh,rstd,yy=self.ln(self.acc[...],V(6),V(7))
            if save:
                self.xh2[...]=xh; self.rs2[...]=jnp.broadcast_to(rstd,(512,128)); self.out(l,"xh2","rs2")
            y[...]=yy.astype(bf16)
            if pooled is not None:
                tpos=lax.broadcasted_iota(jnp.int32,(256,768),0)
                for c in range(2):
                    pooled[c:c+1,:]=jnp.sum(jnp.where(tpos<lens[c],yy[c*256:(c+1)*256],0.0),0,keepdims=True)/lens[c].astype(f32)
        return [functools.partial(part,j) for j in range(4)]+[end]

def unit_scale(p): return lax.rsqrt(jnp.sum(p*p,-1,keepdims=True)+1e-6)

class Contrast:
    def __init__(self,pos,queue,lens,R):
        self.p,self.queue,self.lens=pos,queue,lens
        self.__dict__.update(R)
    def ucp(self,s):
        _,dev=self.p.peer(s)
        return remote(self.units.at[self.p.me],self.units.at[self.p.me],self.us.at[s],self.ur.at[s],dev)
    def gcp(self,s):
        j,dev=self.p.peer(s)
        return remote(self.sends.at[j],self.gets.at[self.p.me],self.gs.at[s],self.gr.at[s],dev)
    def loop(self,fn): lax.fori_loop(1,self.p.N,lambda s,_: (fn(s),0)[1],0)
    def send_units(self):
        p=self.pool_q[...]
        self.units[self.p.me]=(p*unit_scale(p)).astype(bf16).astype(f32)
        self.loop(lambda s: self.ucp(s).start())
    def share(self):
        self.loop(lambda s: self.ucp(s).wait_recv())
        N=self.p.N
        for i in range(N): self.q_all[2*i:2*i+2,:]=self.units[i]
        lg=dot_t(self.q_all[...].astype(bf16),self.queue[...])*(1.0/SHARP)
        m=jnp.max(lg,-1,keepdims=True)
        e=jnp.exp(lg-m)
        self.part[:,0:768]=dot(e.astype(bf16),self.queue[...])
        self.part[:,768:896]=jnp.broadcast_to(m,(2*N,128))
        self.part[:,896:1024]=jnp.broadcast_to(jnp.sum(e,-1,keepdims=True),(2*N,128))
        for i in range(N): self.sends[i]=self.part[2*i:2*i+2,:]
        self.gets[self.p.me]=self.sends[self.p.me]
        self.loop(lambda s: self.gcp(s).start())
    def end(self,loss,grad):
        pk=self.pool_k[...]; pq=self.pool_q[...]
        ku=(pk*unit_scale(pk)).astype(bf16).astype(f32)
        rs=unit_scale(pq)
        qu=(pq*rs).astype(bf16).astype(f32)
        pos=jnp.sum(qu*ku,-1,keepdims=True)/SHARP
        self.loop(lambda s: self.gcp(s).wait_recv())
        mi=self.gets[:,:,768:896]
        top=jnp.maximum(jnp.max(mi,0),pos)
        w=jnp.exp(mi-top[None])
        pe=jnp.exp(pos-top)
        total=jnp.sum(w*self.gets[:,:,896:1024],0)+pe
        loss[...]=top+jnp.log(total)-pos
        scale=FACTOR/SHARP
        inv=scale/total
        cp=scale*(pe/total-1.0)
        for k in range(6):
            cols=slice(k*128,(k+1)*128)
            grad[:,cols]=jnp.sum(w*self.gets[:,:,cols],0)*inv+cp*ku[:,cols]
        g=grad[...]
        d=rs*g-pq*(rs*rs*rs)*jnp.sum(pq*g,-1,keepdims=True)
        for c in range(2): grad[c:c+1,:]=d[c:c+1]/self.lens[c].astype(f32)
    def finish(self):
        self.loop(lambda s: self.ucp(s).wait_send())
        self.loop(lambda s: self.gcp(s).wait_send())

def forward_kernel(D,F,order,names,lenq,lenk,xq,xk,queue,msg,qw,pw,ew,sw,kqw,kpw,kew,ksw,
                   g,vecs,y0,y1,loss,gp,*rest):
    outs=(rest[:10],rest[10:20]); R=dict(zip(names,rest[20:]))
    pos=Place(D,F); r=768//F; rs=3072//F; f=pos.f
    bar=pltpu.get_barrier_semaphore()
    def hello(s,_):
        _,dev=pos.peer(s)
        pl.semaphore_signal(bar,inc=1,device_id=dev,device_id_type=MESH); return 0
    lax.fori_loop(1,pos.N,hello,0)
    def own(l,j):
        dst=lambda j,n: R["pk"].at[l,pl.ds(j*r,n)]
        if j<3: s,d=qw.at[l,:,pl.ds(j*768,768)],dst(j,r)
        elif j==3: s,d=pw.at[l],dst(3,r)
        elif j<8: s,d=ew.at[l,:,pl.ds((j-4)*768,768)],dst(j,r)
        else: s,d=sw.at[l],dst(8,rs)
        return pltpu.make_async_copy(s,d,R["lsem"].at[l,j])
    groups={0:range(4),1:range(4,9)}
    for l in range(2):
        for j in range(9): own(l,j).start()
    def kload(l):
        pairs=[(kqw,"kq"),(kpw,"kp"),(kew,"ke"),(ksw,"ks"),(qw,"qq"),(pw,"qp"),(ew,"qe"),(sw,"qs")]
        return [pltpu.make_async_copy(a.at[l],R[b],R["ksem"].at[i]) for i,(a,b) in enumerate(pairs)]
    def mcp(l): return pltpu.make_async_copy(R["mo"].at[l],g.at[2+l,f],R["msem"].at[l])
    for c in kload(0): c.start()
    def mirror(l):
        for c in kload(l): c.wait()
        mo=R["mo"]
        mix=lambda k,q: (MOM*k+(1.0-MOM)*q.astype(f32)).astype(bf16)
        for j in range(3):
            cols=slice(j*768,(j+1)*768); mo[l,j*r:(j+1)*r,:]=mix(R["kq"][:,cols],R["qq"][:,cols])
        mo[l,3*r:4*r,:]=mix(R["kp"][...],R["qp"][...])
        for j in range(4):
            cols=slice(j*768,(j+1)*768); mo[l,(4+j)*r:(5+j)*r,:]=mix(R["ke"][:,cols],R["qe"][:,cols])
        mo[l,8*r:8*r+rs,:]=mix(R["ks"][...],R["qs"][...])
        mcp(l).start()
        if l==0:
            for c in kload(1): c.start()
    def packed(q):
        l,r0,n=chunks[q]
        return pltpu.make_async_copy(R["pk"].at[l,pl.ds(r0,n)],g.at[l,f,pl.ds(r0,n)],R["psem"].at[q])
    waited=set()
    def ready(q):
        l=q//2
        if l<2:
            for j in groups[q%2]: own(l,j).wait()
            cp=packed(q); cp.start(); cp.wait()
        elif l not in waited:
            waited.add(l); mcp(l-2).wait()
    chunks=[(l,r0,n) for l in range(4) for r0,n in ((0,4*r),(4*r,8*r))]
    G=Gather(pos,g,chunks,ready,[R[k] for k in ("zs","zr","ys","yr","xs","xr","cs","cr","ks_","kr_")])
    vmsg=R["vmsg"]
    def vcp(s): return remote(msg,vmsg.at[f],R["vs"].at[s],R["vr"].at[s],(pos.d,(f+s)%F))
    vmsg[f]=msg[...]
    pl.semaphore_wait(bar,pos.N-1)
    for s in range(1,F): vcp(s).start()
    def vectors():
        for s in range(1,F): vcp(s).wait_recv()
        row=lax.broadcasted_iota(jnp.int32,(128,768),0); col=lax.broadcasted_iota(jnp.int32,(128,768),1)
        v=jnp.zeros((32,768),f32)
        for i in range(F):
            hot=jnp.logical_and(col==row+i*r,row<r)
            v=v+dot(vmsg[i,:,0:128],jnp.where(hot,1.0,0.0).astype(bf16))
        row=lax.broadcasted_iota(jnp.int32,(384,768),0); col=lax.broadcasted_iota(jnp.int32,(384,768),1)
        for l in range(4): vecs[l,0:8,:]=v[8*l:8*l+8]; vecs[l,8:16,:]=jnp.zeros((8,768),f32)
        for j in range(4):
            e=jnp.zeros((32,768),f32)
            for i in range(F//4):
                hot=jnp.logical_and(col==row+i*rs,row<rs)
                e=e+dot(vmsg[j*(F//4)+i,:,128:512],jnp.where(hot,1.0,0.0).astype(bf16))
            for l in range(4): vecs[l,8+j:9+j,:]=e[8*l:8*l+1]
    Fw=Forward(g,vecs,None,R); Fw.outs=outs
    Ct=Contrast(pos,queue,lenq,R)
    yk=R["yk"]
    work=[]
    for l,(save,x,y,lens,pool) in enumerate([(True,xq,y0,lenq,None),(True,y0,y1,lenq,R["pool_q"]),(False,xk,yk,lenk,None),(False,yk,R["yl"],lenk,R["pool_k"])]):
        work.append(Fw.attn_steps(l,save,x,lens,(lambda k=l-1: Fw.drain(k)) if l in (1,2) else None))
        work.append(Fw.ffn_steps(l,save,y,lens,pool))
    work[3].append(Ct.send_units)
    work[4].append(Ct.share)
    pre=[vectors,lambda: mirror(0),lambda: mirror(1)]
    act=[G.start,G.on_z,G.on_y,G.on_x,G.on_c,lambda q,i: work[q][i](),lambda q,i: pre[i]()]
    for kind,q,i in order:
        if kind in (0,4): act[kind](q)
        else: act[kind](q,i)
    Ct.end(loss,gp)
    G.finish(); Ct.finish()
    for s in range(1,F): vcp(s).wait_send()

def forward(D,F,lenq,lenk,xq,xk,queue,msg,mats,kmats,cid,order=None):
    sd=jax.ShapeDtypeStruct; S=pltpu.SemaphoreType.DMA; VM=pltpu.VMEM
    V=pl.BlockSpec(memory_space=pltpu.VMEM); ANY=pl.BlockSpec(memory_space=pl.ANY); SM=pl.BlockSpec(memory_space=pltpu.SMEM)
    A=4;B=F//4;Q=8;N=D*F; r=768//F; rs=3072//F; M=2*A*B
    buf=dict(zip(SAVED,[VM(s.shape,s.dtype) for s in saved_shapes()]))
    buf.update(acc=VM((512,768),f32),yk=VM((512,768),bf16),yl=VM((512,768),bf16),wv=VM((8,F,r,768),bf16),sv=VM((4,F//4,rs,768),bf16),
        pool_q=VM((2,768),f32),pool_k=VM((2,768),f32),units=VM((N,2,768),f32),q_all=VM((2*N,768),f32),part=VM((2*N,1024),f32),
        sends=VM((N,2,1024),f32),gets=VM((N,2,1024),f32),vmsg=VM((F,32,512),bf16),
        kq=VM((r,2304),f32),kp=VM((r,768),f32),ke=VM((r,3072),f32),ks=VM((rs,768),f32),qq=VM((r,2304),bf16),qp=VM((r,768),bf16),qe=VM((r,3072),bf16),qs=VM((rs,768),bf16),
        mo=VM((2,12*r,768),bf16),pk=VM((2,12*r,768),bf16),psem=S((4,)),
        wsem=S((12,)),osem=S((2,10)),lsem=S((2,9)),ksem=S((8,)),msem=S((2,)),us=S((N,)),ur=S((N,)),gs=S((N,)),gr=S((N,)),vs=S((F,)),vr=S((F,)),
        zs=S((Q,2,A)),zr=S((Q,2,A)),ys=S((Q,2*A,B)),yr=S((Q,2*A,B)),xs=S((Q,M)),xr=S((Q,M)),cs=S((Q,M)),cr=S((Q,M)),ks_=S((Q,M)),kr_=S((Q,M)))
    saved=saved_shapes()
    outs=[sd((4,F,12*r,768),bf16),sd((4,16,768),f32),sd((512,768),bf16),sd((512,768),bf16),sd((2,128),f32),sd((2,768),f32)]+saved*2
    res=pl.pallas_call(functools.partial(forward_kernel,D,F,ORDER if order is None else order,list(buf)),out_shape=outs,
        in_specs=[SM,SM,V,V,V,V]+[ANY]*8,out_specs=[ANY,V,V,V,V,V]+[ANY]*20,scratch_shapes=list(buf.values()),
        compiler_params=pltpu.CompilerParams(collective_id=cid,has_side_effects=True,vmem_limit_bytes=61<<20),name="forward")(lenq,lenk,xq,xk,queue,msg,*mats,*kmats)
    return res[:6],res[6:16],res[16:26]
ORDER = (
    (0, 0, 0), (1, 0, 1), (6, 0, 0), (1, 0, 2), (2, 0, 0), (6, 0, 1), (0, 1, 0), (6, 0, 2), (1, 0, 3), (2, 0, 1),
    (3, 0, 0), (2, 0, 2), (1, 1, 1), (2, 0, 3), (3, 0, 1), (2, 1, 0), (3, 0, 2), (1, 1, 2), (3, 0, 3), (4, 0, 0),
    (5, 0, 0), (5, 0, 1), (1, 1, 3), (5, 0, 2), (5, 0, 3), (3, 1, 0), (2, 1, 1), (0, 2, 0), (5, 0, 4), (2, 1, 2),
    (1, 2, 1), (5, 0, 5), (1, 2, 2), (2, 2, 0), (0, 3, 0), (2, 1, 3), (1, 2, 3), (3, 1, 1), (2, 2, 1), (3, 1, 2),
    (3, 2, 0), (2, 2, 2), (1, 3, 1), (3, 1, 3), (4, 1, 0), (5, 1, 0), (2, 2, 3), (3, 2, 1), (2, 3, 0), (3, 2, 2),
    (1, 3, 2), (5, 1, 1), (3, 2, 3), (5, 1, 2), (4, 2, 0), (5, 1, 3), (1, 3, 3), (5, 1, 4), (3, 3, 0), (2, 3, 1),
    (5, 2, 0), (0, 4, 0), (5, 2, 1), (2, 3, 2), (1, 4, 1), (5, 2, 2), (5, 2, 3), (1, 4, 2), (2, 4, 0), (0, 5, 0),
    (5, 2, 4), (2, 3, 3), (1, 4, 3), (3, 3, 1), (2, 4, 1), (3, 3, 2), (5, 2, 5), (3, 4, 0), (2, 4, 2), (1, 5, 1),
    (3, 3, 3), (4, 3, 0), (5, 3, 0), (2, 4, 3), (3, 4, 1), (2, 5, 0), (3, 4, 2), (1, 5, 2), (5, 3, 1), (3, 4, 3),
    (5, 3, 2), (4, 4, 0), (5, 3, 3), (1, 5, 3), (5, 3, 4), (3, 5, 0), (2, 5, 1), (5, 3, 5), (0, 6, 0), (5, 4, 0),
    (2, 5, 2), (5, 4, 1), (1, 6, 1), (5, 4, 2), (5, 4, 3), (1, 6, 2), (2, 6, 0), (0, 7, 0), (2, 5, 3), (5, 4, 4),
    (1, 6, 3), (3, 5, 1), (2, 6, 1), (3, 5, 2), (3, 6, 0), (5, 4, 5), (2, 6, 2), (1, 7, 1), (3, 5, 3), (4, 5, 0),
    (5, 4, 6), (2, 6, 3), (3, 6, 1), (2, 7, 0), (3, 6, 2), (1, 7, 2), (3, 6, 3), (4, 6, 0), (5, 5, 0), (1, 7, 3),
    (5, 5, 1), (3, 7, 0), (2, 7, 1), (5, 5, 2), (5, 5, 3), (2, 7, 2), (5, 5, 4), (5, 6, 0), (5, 6, 1), (2, 7, 3),
    (5, 6, 2), (3, 7, 1), (5, 6, 3), (3, 7, 2), (5, 6, 4), (3, 7, 3), (4, 7, 0), (5, 6, 5), (5, 7, 0), (5, 7, 1),
    (5, 7, 2), (5, 7, 3), (5, 7, 4),
)
def bwd_kernel(l,first,lens,dyin,x,vec,g,qkv_i,pb_i,ctx_i,xh1_i,rs1_i,h1_i,act_i,der_i,xh2_i,rs2_i,
               dx,dg,vg,wv,sv,qkv,pb,ctx,xh1,rs1,h1,act,der,xh2,rs2,dmix,dacc,dr2,dctx,dv,ds,sem,isem,osem):
    F=g.shape[1]; r=768//F; rs_=3072//F
    cps=load_weights(l,g,wv,sv,sem)
    ins=[pltpu.make_async_copy(s,d,isem.at[i]) for i,(s,d) in enumerate([(qkv_i,qkv),(pb_i,pb),(ctx_i,ctx),(xh1_i,xh1),(rs1_i,rs1),(h1_i,h1),(act_i,act),(der_i,der),(xh2_i,xh2),(rs2_i,rs2)])]
    QKV,PB,CTX,XH1,RS1,H1,ACT,DER,XH2,RS2=range(10)
    for i in (XH2,RS2): ins[i].start()
    for j in range(4):
        cps[8+j].start()
        if j==0: ins[ACT].start(); ins[DER].start(); ins[H1].start()
        cps[4+j].start()
    for i in (XH1,RS1,CTX): ins[i].start()
    cps[3].start(); ins[QKV].start(); ins[PB].start()
    for j in range(3): cps[j].start()
    def W(j): return wv[j].reshape(768,768)
    def S(j): return sv[j].reshape(768,768)
    outs=[]
    def outw(j,val):
        if j<8:
            dv[j]=val.astype(bf16).reshape(F,r,768)
            cp=pltpu.make_async_copy(dv.at[j],dg.at[:,pl.ds(j*r,r),:],osem.at[j])
        else:
            q=j-8
            ds[q]=val.astype(bf16).reshape(F//4,rs_,768)
            cp=pltpu.make_async_copy(ds.at[q],dg.at[pl.ds(q*(F//4),F//4),pl.ds(8*r,rs_),:],osem.at[j])
        cp.start(); outs.append(cp)
    vg[...]=jnp.zeros_like(vg)
    tpos=lax.broadcasted_iota(jnp.int32,(256,768),0)
    if first:
        dy=jnp.concatenate([jnp.where(tpos<lens[c],dyin[c:c+1,:],0.0) for c in range(2)],0)
    else: dy=dyin[...]
    def ln_back(dy,xh,rstd,gain):
        t=dy*gain
        return rstd*(t-jnp.mean(t,-1,keepdims=True)-xh*jnp.mean(t*xh,-1,keepdims=True))
    def colsum(v): return jnp.sum(v,0,keepdims=True)
    ins[XH2].wait(); ins[RS2].wait()
    xh=xh2[...]
    vg[6:7,:]=colsum(dy*xh); vg[7:8,:]=colsum(dy)
    d2=ln_back(dy,xh,rs2[:,0:1],vec[6:7,:])
    dacc[...]=d2
    dfb=d2.astype(bf16)
    dr2[...]=dfb
    vg[5:6,:]=colsum(dfb.astype(f32))
    for i in (ACT,DER,H1): ins[i].wait()
    for j in range(4):
        cps[8+j].wait(); cps[4+j].wait()
        a=act[:,j*768:(j+1)*768]
        outw(8+j,tdot(a,dr2[...]))
        du=(dot_t(dr2[...],S(j))*der[:,j*768:(j+1)*768].astype(f32)).astype(bf16)
        vg[8+j:9+j,:]=colsum(du.astype(f32))
        outw(4+j,tdot(h1[...],du))
        dacc[...]+=dot_t(du,W(4+j))
    for i in (XH1,RS1,CTX): ins[i].wait()
    dh=dacc[...]; xh=xh1[...]
    vg[3:4,:]=colsum(dh*xh); vg[4:5,:]=colsum(dh)
    d1=ln_back(dh,xh,rs1[:,0:1],vec[3:4,:])
    dacc[...]=d1
    dr2[...]=d1.astype(bf16)
    vg[2:3,:]=colsum(dr2[...].astype(f32))
    cps[3].wait()
    outw(3,tdot(ctx[...],dr2[...]))
    dctx[...]=dot_t(dr2[...],W(3)).astype(bf16)
    ins[QKV].wait(); ins[PB].wait()
    lane=lax.broadcasted_iota(jnp.int32,(256,128),1); low_half=lane<64
    def pair(i,_):
        c=i//6; p=i-c*6
        rows=pl.ds(pl.multiple_of(c*256,256),256); o=pl.multiple_of(p*128,128)
        o1=pl.multiple_of(768+o,128); o2=pl.multiple_of(1536+o,128)
        q2=qkv[rows,pl.ds(o,128)]; k2=qkv[rows,pl.ds(o1,128)]; v2=qkv[rows,pl.ds(o2,128)]
        dc=dctx[rows,pl.ds(o,128)]
        res=[]
        for hh in range(2):
            m=low_half if hh==0 else jnp.logical_not(low_half)
            P=pb[i*2+hh]; pf=P.astype(f32)
            dP=dot_t(jnp.where(m,dc,jnp.zeros_like(dc)),v2)
            pd=pf*dP
            dS=(pd-pf*jnp.sum(pd,-1,keepdims=True)).astype(bf16)
            res.append((dot(dS,k2),tdot(dS,q2),tdot(P,dc)))
        sel=lambda t: jnp.where(low_half,res[0][t],res[1][t])
        dmix[rows,pl.ds(o,128)]=(sel(0)*0.125).astype(bf16)
        dmix[rows,pl.ds(o1,128)]=(sel(1)*0.125).astype(bf16)
        dmix[rows,pl.ds(o2,128)]=sel(2).astype(bf16)
        return 0
    lax.fori_loop(0,12,pair,0,unroll=3)
    for j in range(3):
        cps[j].wait()
        dm=dmix[:,j*768:(j+1)*768]
        if j==0: vg[0:1,:]=colsum(dm.astype(f32))
        if j==2: vg[1:2,:]=colsum(dm.astype(f32))
        outw(j,tdot(x[...],dm))
        dacc[...]+=dot_t(dm,W(j))
    dx[...]=dacc[...].astype(dx.dtype)
    for c in outs: c.wait()

def layer_bwd(l,first,lens,dy,x,vec,g,saved,dxt):
    F=g.shape[1]; sd=jax.ShapeDtypeStruct
    V=pl.BlockSpec(memory_space=pltpu.VMEM); ANY=pl.BlockSpec(memory_space=pl.ANY)
    S=pltpu.SemaphoreType.DMA
    w=[pltpu.VMEM((8,F,768//F,768),bf16),pltpu.VMEM((4,F//4,3072//F,768),bf16)]
    scr=w+[pltpu.VMEM(s.shape,s.dtype) for s in saved]+[pltpu.VMEM((512,2304),bf16),pltpu.VMEM((512,768),f32),pltpu.VMEM((512,768),bf16),pltpu.VMEM((512,768),bf16)]+w+[S((12,)),S((10,)),S((12,))]
    return pl.pallas_call(functools.partial(bwd_kernel,l,first),out_shape=[sd((512,768),dxt),sd((F,12*768//F,768),bf16),sd((16,768),f32)],
        in_specs=[pl.BlockSpec(memory_space=pltpu.SMEM),V,V,V]+[ANY]*11,out_specs=[V,ANY,V],scratch_shapes=scr,
        compiler_params=pltpu.CompilerParams(vmem_limit_bytes=61<<20),name="layer_bwd")(lens,dy,x,vec,g,*saved)

def sizes(F):
    n=4*(768//F); np_=n//3; nq=n-np_
    return n,np_,nq
def rs_scratch(D,F,NP):
    A=4;B=F//4;O=D//4; n,np_,nq=sizes(F); nh=n//2; Sm=pltpu.SemaphoreType.DMA
    V=pltpu.VMEM
    return dict(T=V((NP,F,n,384),bf16),RC=V((NP,F,n,384),bf16),RPX=V((NP,F,np_//2,384),bf16),RPY=V((NP,B-1,A,np_//2,384),bf16),
      RQY=V((NP,B-1,A,nq,384),bf16),RQX=V((NP,A,nq//2,384),bf16),T3=V((NP,A,nh,384),bf16),RZ=V((NP,A-1,nh,384),bf16),
      **(dict(RO=V((NP,O-1,nh,384),bf16),TO=V((NP,nh,384),bf16)) if O>1 else {}),
      VS=V((5,32,768),f32),VRC=V((1,32,768),f32),VRX=V((1,32,768),f32),VRY=V((B-1,32,768),f32),VRZ=V((A-1,32,768),f32),
      **(dict(VRO=V((O-1,32,768),f32)) if O>1 else {}),
      LS=Sm((NP,)),SS=Sm((NP,8+B+A+B+A+O,)),RS=Sm((NP,8+B+A+B+A+O)),VSS=Sm((8+B+A+O,)),VRS=Sm((8+B+A+O,)))
class Reduce:
    def __init__(self,D,F,src,fin,vin,vout,buf):
        self.D,self.F=D,F; self.A=4; self.B=F//4; self.O=D//4
        d=lax.axis_index("dp"); f=lax.axis_index("fsdp")
        self.d,self.f=d,f; self.a=f//self.B; self.b=f%self.B; self.x=(d//2)%2; self.c=d%2; self.o=d//4
        self.xd=d+2-4*self.x; self.cd=d+1-2*self.c
        self.src,self.fin,self.vin,self.vout=src,fin,vin,vout
        self.__dict__.update(buf); self.n,self.np,self.nq=sizes(F)
        self.hp=self.np//2; self.hq=self.nq//2
        self.pending=[]
        m=pl.multiple_of
        self.mycols=pl.ds(m(self.c*384,128),384); self.ocols=pl.ds(m((1-self.c)*384,128),384)
        self.Pown=pl.ds(m(self.x*self.hp,16),self.hp); self.Poth=pl.ds(m((1-self.x)*self.hp,16),self.hp)
        self.Qown=pl.ds(m(self.np+self.x*self.hq,16),self.hq); self.Qoth=pl.ds(m(self.np+(1-self.x)*self.hq,16),self.hq)
        self.Qall=pl.ds(self.np,self.nq)
    def peers(self):
        out=[(self.d,(self.f+s)%self.F) for s in range(1,self.F)]
        out+=[(self.xd,self.f),(self.cd,self.f)]+[((self.d+4*s)%self.D,self.f) for s in range(1,self.O)]
        return out
    def rc(self,i,k,src,dst,dev):
        cp=pltpu.make_async_remote_copy(src,dst,self.SS.at[i,k],self.RS.at[i,k],device_id=dev,device_id_type=MESH)
        return cp
    def go(self,cp): cp.start(); self.pending.append(cp)
    def kPy(self,t): return 8+t
    def kQy(self,t): return 8+self.B+t
    def kZ(self,s): return 8+2*self.B+s
    def kO(self,s): return 8+2*self.B+self.A+s
    def Yd(self,t): return (self.d,self.a*self.B+(self.b+t)%self.B)
    def Zd(self,s): return (self.d,((self.a+s)%self.A)*self.B+self.b)
    def s0(self,i):
        s=self.src(i)
        self.cC=lambda i: self.rc(i,0,self.src(i).at[:,:,self.ocols],self.RC.at[i],(self.cd,self.f))
        self.go(self.cC(i))
        self.lc=lambda i: pltpu.make_async_copy(self.src(i).at[:,:,self.mycols],self.T.at[i],self.LS.at[i])
        self.lc(i).start()
    def s1(self,i):
        self.lc(i).wait(); self.cC(i).wait_recv()
        T,RC=self.T,self.RC
        def body(f,_):
            T[i,f]=(T[i,f].astype(f32)+RC[i,f].astype(f32)).astype(bf16); return 0
        lax.fori_loop(0,self.F,body,0)
        self.go(self.cPx(i))
        for t in range(1,self.B):
            for a in range(self.A): pass
        for t in range(1,self.B):
            fb=(self.b+t)%self.B
            for a in range(self.A):
                pass
        self.startQy(i)
    def cPx(self,i): return self.rc(i,1,self.T.at[i,:,self.Poth],self.RPX.at[i],(self.xd,self.f))
    def Tab(self,i):
        return self.T.at[i].reshape(self.A,self.B,self.n,384)
    def cQy(self,i,t): return self.rc(i,self.kQy(t),self.Tab(i).at[:,(self.b+t)%self.B,self.Qall],self.RQY.at[i,t-1],self.Yd(t))
    def cPy(self,i,t): return self.rc(i,self.kPy(t),self.Tab(i).at[:,(self.b+t)%self.B,self.Pown],self.RPY.at[i,t-1],self.Yd(t))
    def startQy(self,i):
        for t in range(1,self.B): self.go(self.cQy(i,t))
    def s2(self,i):
        T=self.T
        self.cPx(i).wait_recv()
        def body(f,_):
            T[i,f,self.Pown]=(T[i,f,self.Pown].astype(f32)+self.RPX[i,f].astype(f32)).astype(bf16); return 0
        lax.fori_loop(0,self.F,body,0)
        for t in range(1,self.B): self.go(self.cPy(i,t))
        for t in range(1,self.B): self.cQy(i,t).wait_recv()
        def bodyq(a,_):
            fo=a*self.B+self.b
            v=T[i,fo,self.Qall].astype(f32)
            for t in range(1,self.B): v=v+self.RQY[i,t-1,a].astype(f32)
            T[i,fo,self.Qall]=v.astype(bf16); return 0
        lax.fori_loop(0,self.A,bodyq,0)
        self.go(self.cQx(i))
    def cQx(self,i): return self.rc(i,2,self.Tab(i).at[:,self.b,self.Qoth],self.RQX.at[i],(self.xd,self.f))
    def s3(self,i):
        for t in range(1,self.B): self.cPy(i,t).wait_recv()
        self.cQx(i).wait_recv()
        def body(a,_):
            fo=a*self.B+self.b
            v=self.T[i,fo,self.Pown].astype(f32)
            for t in range(1,self.B): v=v+self.RPY[i,t-1,a].astype(f32)
            self.T3[i,a,0:self.hp]=v.astype(bf16)
            self.T3[i,a,self.hp:self.hp+self.hq]=(self.T[i,fo,self.Qown].astype(f32)+self.RQX[i,a].astype(f32)).astype(bf16)
            return 0
        lax.fori_loop(0,self.A,body,0)
        for s in range(1,self.A): self.go(self.cZ(i,s))
    def cZ(self,i,s): return self.rc(i,self.kZ(s),self.T3.at[i,(self.a+s)%self.A],self.RZ.at[i,s-1],self.Zd(s))
    def cO(self,i,s): return self.rc(i,self.kO(s),self.TO.at[i],self.RO.at[i,s-1],((self.d+4*s)%self.D,self.f))
    def put(self,i,v):
        v=v.astype(bf16)
        self.fin[i,self.Pown,self.mycols]=v[:self.hp]; self.fin[i,self.Qown,self.mycols]=v[self.hp:]
        self.go(self.cFX(i,0)); self.go(self.cFX(i,1))
    def cFX(self,i,w):
        r=(self.Pown,self.Qown)[w]; v=self.fin.at[i,r,self.mycols]
        return self.rc(i,3+w,v,v,(self.xd,self.f))
    def rFX(self,i,w):
        r=(self.Poth,self.Qoth)[w]; v=self.fin.at[i,r,self.mycols]
        return self.rc(i,3+w,v,v,(self.xd,self.f))
    def s4(self,i):
        v=self.T3[i,self.a].astype(f32)
        for s in range(1,self.A):
            self.cZ(i,s).wait_recv()
            v=v+self.RZ[i,s-1].astype(f32)
        if self.O>1:
            self.TO[i]=v.astype(bf16)
            for s in range(1,self.O): self.go(self.cO(i,s))
            for s in range(1,self.O):
                self.cO(i,s).wait_recv(); v=v+self.RO[i,s-1].astype(f32)
        self.put(i,v)
    def s5(self,i):
        for w in (0,1): self.rFX(i,w).wait_recv()
        v=self.fin.at[i,:,self.mycols]; self.go(self.rc(i,5,v,v,(self.cd,self.f)))
    def s6(self,i):
        v=self.fin.at[i,:,self.ocols]; self.rc(i,5,v,v,(self.cd,self.f)).wait_recv()
    def vstage(self,k):
        st=[(self.VRC,[(self.cd,self.f)],0),(self.VRX,[(self.xd,self.f)],1),(self.VRY,[self.Yd(t) for t in range(1,self.B)],8),(self.VRZ,[self.Zd(s) for s in range(1,self.A)],8+self.B)]
        if self.O>1: st.append((self.VRO,[((self.d+4*s)%self.D,self.f) for s in range(1,self.O)],8+self.B+self.A))
        def cps(k):
            buf,devs,k0=st[k]
            return [pltpu.make_async_remote_copy(self.VS.at[k],buf.at[q],self.VSS.at[k0+q],self.VRS.at[k0+q],device_id=dv,device_id_type=MESH) for q,dv in enumerate(devs)]
        if k==0: self.VS[0]=self.vin[...]
        elif k<=len(st):
            v=self.VS[k-1]
            for q,cp in enumerate(cps(k-1)):
                cp.wait_recv(); v=v+st[k-1][0][q]
            if k<len(st): self.VS[k]=v
            else: self.vout[...]=v
        if k<len(st):
            for cp in cps(k): self.go(cp)
    def finish(self):
        for cp in self.pending: cp.wait_send()

def rs_kernel(D,F,names,dgs,vin,fin,vout,*scr):
    buf=dict(zip(names,scr))
    n=4*(768//F)
    NP=3*len(dgs)
    src=lambda i: dgs[i//3].at[:,pl.ds((2-i%3)*n,n),:]
    R=Reduce(D,F,src,fin,vin,vout,buf)
    bar=pltpu.get_barrier_semaphore(); ps=R.peers()
    for p in ps: pl.semaphore_signal(bar,inc=1,device_id=p,device_id_type=MESH)
    pl.semaphore_wait(bar,len(ps))
    stages=[R.s0,R.s1,R.s2,R.s3,R.s4,R.s5,R.s6]
    for t in range(NP+6):
        if t<6: R.vstage(t)
        for i in range(NP):
            if 0<=t-i<=6: stages[t-i](i)
    R.finish()

def reduce_grads(D,F,dgs,vin,cid):
    n,np_,nq=sizes(F); NP=3*len(dgs)
    buf=rs_scratch(D,F,NP); sd=jax.ShapeDtypeStruct
    V=pl.BlockSpec(memory_space=pltpu.VMEM); ANY=pl.BlockSpec(memory_space=pl.ANY)
    def k(*refs):
        nd=len(dgs)
        rs_kernel(D,F,list(buf),refs[:nd],refs[nd],refs[nd+1],refs[nd+2],*refs[nd+3:])
    return pl.pallas_call(k,out_shape=[sd((NP,n,768),bf16),sd((32,768),f32)],in_specs=[ANY]*len(dgs)+[V],out_specs=[V,V],
        scratch_shapes=list(buf.values()),compiler_params=pltpu.CompilerParams(collective_id=cid,has_side_effects=True,vmem_limit_bytes=61<<20),name="reduce_grads")(*dgs,vin)


def on_device(dp, fsdp, x_query, x_key, len_query, len_key, queue, *params):
    query_params, key_params = params[:13], params[13:]
    num_crops, seq_len, width = x_query.shape
    r = width // fsdp
    order = (1, 2, 4, 5, 6, 10, 11, 12)
    small_q = jnp.stack([query_params[i] for i in order], 1)
    small_k = jnp.stack([key_params[i] for i in order], 1)
    bias_q, bias_k = query_params[8], key_params[8]
    mix = lambda k, q: (MOM * k + (1.0 - MOM) * q.astype(f32)).astype(bf16)
    small = jnp.concatenate([small_q, mix(small_k, small_q)], 0).reshape(32, r)
    wide = jnp.concatenate([bias_q, mix(bias_k, bias_q)], 0)
    wide = jnp.pad(wide[:, None, :], ((0, 0), (0, 7), (0, 384 - wide.shape[1]))).reshape(32, 384)
    msg = jnp.concatenate([jnp.pad(small, ((0, 0), (0, 128 - r))), wide], 1)
    big = (0, 3, 7, 9)
    x0 = x_query.reshape(num_crops * seq_len, width)
    xk = x_key.reshape(num_crops * seq_len, width)
    (gathered, vecs, y0, y1, loss, grad_pooled), saved0, saved1 = forward(
        dp, fsdp, len_query, len_key, x0, xk, queue, msg,
        [query_params[i] for i in big], [key_params[i] for i in big], 1)
    dx1, d1, v1 = layer_bwd(1, True, len_query, grad_pooled, y0, vecs[1], gathered, saved1, f32)
    dx0, d0, v0 = layer_bwd(0, False, len_query, dx1, x0, vecs[0], gathered, saved0, bf16)
    fin, vsum = reduce_grads(dp, fsdp, [d1, d0], jnp.concatenate([v1, v0], 0), 2)
    me = lax.axis_index("fsdp")
    n = fin.shape[1]
    fin = fin.astype(f32).reshape(2, 3, n, width)[::-1]
    sh_g, ex_g, at_g = fin[:, 0], fin[:, 1], fin[:, 2]
    grad_qkv = jnp.concatenate([at_g[:, i * r : (i + 1) * r] for i in range(3)], 2)
    grad_proj = at_g[:, 3 * r :]
    grad_expand = jnp.concatenate([ex_g[:, i * r : (i + 1) * r] for i in range(4)], 2)
    vsum = vsum.reshape(2, 16, width)[::-1]
    mine = lax.dynamic_slice_in_dim(vsum[:, :8], me * r, r, 2)
    ebg = lax.dynamic_slice_in_dim(vsum[:, 8:12].reshape(2, 4 * width), me * 4 * r, 4 * r, 1)
    qb, vb, pb, g1, b1, sb, g2, b2 = [mine[:, i] for i in range(8)]
    hidden = y1.reshape(num_crops, seq_len, width)
    grad_input = dx0.reshape(num_crops, seq_len, width)
    return (hidden, grad_input, grad_qkv, qb, vb, grad_proj, pb, g1, b1, grad_expand, ebg, sh_g, sb, g2, b2, loss[:, 0])


def solution(mesh):
    in_specs = (
        P(("dp", "fsdp"), None, None),
        P(("dp", "fsdp"), None, None),
        P(("dp", "fsdp")),
        P(("dp", "fsdp")),
        P(("dp", "fsdp"), None),
        P(None, "fsdp", None),
        P(None, "fsdp"),
        P(None, "fsdp"),
        P(None, "fsdp", None),
        P(None, "fsdp"),
        P(None, "fsdp"),
        P(None, "fsdp"),
        P(None, "fsdp", None),
        P(None, "fsdp"),
        P(None, "fsdp", None),
        P(None, "fsdp"),
        P(None, "fsdp"),
        P(None, "fsdp"),
        P(None, "fsdp", None),
        P(None, "fsdp"),
        P(None, "fsdp"),
        P(None, "fsdp", None),
        P(None, "fsdp"),
        P(None, "fsdp"),
        P(None, "fsdp"),
        P(None, "fsdp", None),
        P(None, "fsdp"),
        P(None, "fsdp", None),
        P(None, "fsdp"),
        P(None, "fsdp"),
        P(None, "fsdp"),
    )
    out_specs = (
        P(("dp", "fsdp"), None, None),
        P(("dp", "fsdp"), None, None),
        P(None, "fsdp", None),
        P(None, "fsdp"),
        P(None, "fsdp"),
        P(None, "fsdp", None),
        P(None, "fsdp"),
        P(None, "fsdp"),
        P(None, "fsdp"),
        P(None, "fsdp", None),
        P(None, "fsdp"),
        P(None, "fsdp", None),
        P(None, "fsdp"),
        P(None, "fsdp"),
        P(None, "fsdp"),
        P(("dp", "fsdp")),
    )
    return jax.shard_map(
        functools.partial(on_device, mesh.shape["dp"], mesh.shape["fsdp"]), mesh=mesh, in_specs=in_specs, out_specs=out_specs, check_vma=False
    )
```

```python
import functools

import jax
import jax.numpy as jnp
from jax import lax
from jax.experimental import pallas as pl
from jax.experimental.pallas import tpu as pltpu
from jax.sharding import PartitionSpec as P

f32=jnp.float32; bf16=jnp.bfloat16
HEADS=12
def dot(a,b): return lax.dot_general(a,b,(((1,),(0,)),((),())),preferred_element_type=f32)
def dot_t(a,b): return lax.dot_general(a,b,(((1,),(1,)),((),())),preferred_element_type=f32)
def tdot(a,b): return lax.dot_general(a,b,(((0,),(0,)),((),())),preferred_element_type=f32)

def phi_parts(u):
    z=jnp.abs(u)*0.7071067811865476
    t=1.0/(1.0+0.3275911*z)
    e=jnp.exp(-z*z)
    poly=t*(0.254829592+t*(-0.284496736+t*(1.421413741+t*(-1.453152027+t*1.061405429))))
    half=0.5*poly*e
    cdf=jnp.where(u>=0,1.0-half,half)
    return cdf,e*0.3989422804014327

def load_weights(l,g,wv,sv,sem):
    F=g.shape[1]; r=768//F; rs=3072//F
    cps=[]
    for j in range(8):
        cps.append(pltpu.make_async_copy(g.at[l,:,pl.ds(j*r,r),:],wv.at[j],sem.at[j]))
    for j in range(4):
        cps.append(pltpu.make_async_copy(g.at[l,pl.ds(j*(F//4),F//4),pl.ds(8*r,rs),:],sv.at[j],sem.at[8+j]))
    return cps

MESH=pl.DeviceIdType.MESH
SHARP=0.05
FACTOR=512.0
MOM=0.9995

def remote(src,dst,ss,rs,dev):
    return pltpu.make_async_remote_copy(src,dst,ss,rs,device_id=dev,device_id_type=MESH)

def when(cond,fn):
    if cond is True: fn()
    else: pl.when(cond)(fn)

class Place:
    def __init__(self,D,F):
        self.D,self.F=D,F; self.A=4; self.B=F//4; self.O=D//4
        d=self.d=lax.axis_index("dp"); f=self.f=lax.axis_index("fsdp")
        self.a=f//self.B; self.b=f%self.B; self.o=d//4; self.x=(d//2)%2; self.c=d%2
        self.xd=d+2-4*self.x; self.cd=d+1-2*self.c
        self.N=D*F; self.me=d*F+f
    def peer(self,s):
        p=(self.me+s)%self.N
        return p,(p//self.F,p%self.F)

class Gather:
    def __init__(self,pos,g,chunks,ready,sems):
        self.p,self.g,self.chunks,self.ready=pos,g,chunks,ready
        self.zs,self.zr,self.ys,self.yr,self.xs,self.xr,self.cs,self.cr,self.ks,self.kr=sems
    def rows(self,q,t0,n):
        return pl.ds(pl.multiple_of(self.chunks[q][1]+t0*16,16),n*16)
    def parts(self,q):
        p=self.p; half=self.chunks[q][2]//32; nx=(half*13+18)//36; nyz=half-nx
        h=p.c*half; hc=(1-p.c)*half
        R=lambda t0,n: self.rows(q,t0,n)
        return dict(yz=R(h+p.x*nx,nyz),xs=R(h+p.x*nyz,nx),xr=R(h+(1-p.x)*nyz,nx),oyz=R(hc+p.x*nx,nyz),oxr=R(hc+(1-p.x)*nyz,nx))
    def at(self,q,fs,part): return self.g.at[self.chunks[q][0],fs,self.parts(q)[part]]
    def src_a(self,hd): return self.p.a-hd[0] if hd[1]==0 else self.p.a+hd[0]
    def has(self,hd):
        if hd[0]==0: return True
        return (self.p.a>=hd[0]) if hd[1]==0 else (self.p.a+hd[0]<self.p.A)
    def canpass(self,dr): return (self.p.a+1<self.p.A) if dr==0 else (self.p.a>0)
    def z(self,q,hd,fs):
        na=self.p.a+1 if hd[1]==0 else self.p.a-1
        r=self.at(q,fs,"yz")
        return remote(r,r,self.zs.at[q,hd[1],hd[0]],self.zr.at[q,hd[1],hd[0]],(self.p.d,na*self.p.B+self.p.b))
    def slot(self,hd): return hd[0]*2+hd[1]
    def y(self,q,hd,fs,t):
        r=self.at(q,fs,"yz"); s=self.slot(hd)
        return remote(r,r,self.ys.at[q,s,t],self.yr.at[q,s,t],(self.p.d,self.p.a*self.p.B+(self.p.b+t)%self.p.B))
    def xc(self,q,fs,i,part="xs"):
        r=self.at(q,fs,part); return remote(r,r,self.xs.at[q,i],self.xr.at[q,i],(self.p.xd,self.p.f))
    def cc(self,q,fs,i,part="yz"):
        r=self.at(q,fs,part); return remote(r,r,self.cs.at[q,i],self.cr.at[q,i],(self.p.cd,self.p.f))
    def kc(self,q,fs,i,part="xr"):
        r=self.at(q,fs,part); return remote(r,r,self.ks.at[q,i],self.kr.at[q,i],(self.p.cd,self.p.f))
    def shard(self,hd,t=0): return self.src_a(hd)*self.p.B+(self.p.b-t)%self.p.B
    def hds(self,hh): return [(0,0)] if hh==0 else [(hh,0),(hh,1)]
    def start(self,q):
        self.ready(q)
        f=self.p.f
        for dr in (0,1): when(self.canpass(dr),lambda dr=dr: self.z(q,(1,dr),f).start())
        for t in range(1,self.p.B): self.y(q,(0,0),f,t).start()
    def on_z(self,q,hh):
        for hd in self.hds(hh):
            def go(hd=hd):
                fs=self.shard(hd); dr=hd[1]
                self.z(q,hd,fs).wait_recv()
                if hh+1<self.p.A: when(self.canpass(dr),lambda: self.z(q,(hh+1,dr),fs).start())
                for t in range(1,self.p.B): self.y(q,hd,fs,t).start()
                i=self.slot(hd)*self.p.B
                self.xc(q,fs,i).start(); self.cc(q,fs,i).start()
            when(self.has(hd),go)
    def on_y(self,q,hh):
        for hd in self.hds(hh):
            for t in range(1,self.p.B):
                def go(hd=hd,t=t):
                    fs=self.shard(hd,t); i=self.slot(hd)*self.p.B+t
                    self.y(q,hd,fs,t).wait_recv()
                    self.xc(q,fs,i).start(); self.cc(q,fs,i).start()
                when(self.has(hd),go)
    def each(self,hh,fn):
        for hd in self.hds(hh):
            for t in range(self.p.B):
                if hh==0 and t==0: continue
                when(self.has(hd),lambda hd=hd,t=t: fn(self.shard(hd,t),self.slot(hd)*self.p.B+t))
    def on_x(self,q,hh):
        def go(fs,i):
            self.xc(q,fs,i,"xr").wait_recv(); self.kc(q,fs,i).start()
        self.each(hh,go)
    def on_c(self,q):
        def go(fs,i):
            self.cc(q,fs,i,"oyz").wait_recv(); self.kc(q,fs,i,"oxr").wait_recv()
        for hh in range(self.p.A): self.each(hh,go)
    def finish(self):
        f=self.p.f
        for q in range(len(self.chunks)):
            def go(fs,i):
                self.xc(q,fs,i).wait_send(); self.cc(q,fs,i).wait_send(); self.kc(q,fs,i).wait_send()
            for hh in range(self.p.A):
                self.each(hh,go)
                for hd in self.hds(hh):
                    for t in range(1,self.p.B): when(self.has(hd),lambda hd=hd,t=t: self.y(q,hd,f,t).wait_send())
            for dr in (0,1):
                for hh in range(1,self.p.A):
                    cond=self.canpass(dr)
                    if hh>1: cond=jnp.logical_and(cond,self.has((hh-1,dr)))
                    pl.when(cond)(lambda hh=hh,dr=dr: self.z(q,(hh,dr),f).wait_send())

SAVED=("qkv","pb","ctx","xh1","rs1","h1","act","der","xh2","rs2")
def saved_shapes():
    sd=jax.ShapeDtypeStruct
    return [sd((512,2304),bf16),sd((24,256,256),bf16),sd((512,768),bf16),sd((512,768),f32),sd((512,128),f32),sd((512,768),bf16),sd((512,3072),bf16),sd((512,3072),bf16),sd((512,768),f32),sd((512,128),f32)]

class Forward:
    def __init__(self,g,vecs,lens,R):
        self.g,self.vecs,self.lens=g,vecs,lens
        self.__dict__.update(R)
    def W(self,j): return self.wv[j].reshape(768,768)
    def S(self,j): return self.sv[j].reshape(768,768)
    def load(self,l,js):
        for j in js: self.wcp(l,j).start()
    def wcp(self,l,j):
        F=self.g.shape[1]; r=768//F; rs=3072//F
        if j<8: return pltpu.make_async_copy(self.g.at[l,:,pl.ds(j*r,r),:],self.wv.at[j],self.wsem.at[j])
        j-=8
        return pltpu.make_async_copy(self.g.at[l,pl.ds(j*(F//4),F//4),pl.ds(8*r,rs),:],self.sv.at[j],self.wsem.at[8+j])
    def ocp(self,l,i): return pltpu.make_async_copy(self.__dict__[SAVED[i]],self.outs[l][i],self.osem.at[l,i])
    def out(self,l,*names):
        for n in names: self.ocp(l,SAVED.index(n)).start()
    def drain(self,l):
        for i in range(len(SAVED)): self.ocp(l,i).wait()
    def ln(self,z,gain,shift):
        mu=jnp.mean(z,-1,keepdims=True); cz=z-mu
        rstd=lax.rsqrt(jnp.mean(cz*cz,-1,keepdims=True)+1e-12)
        xh=cz*rstd
        return xh,rstd,xh*gain+shift
    def attn_steps(self,l,save,x,lens,before=None):
        V=lambda i: self.vecs[l,i:i+1,:]
        def proj_in(j):
            if j==0 and before: before()
            if j==0: self.load(l,range(4))
            self.wcp(l,j).wait()
            r=dot(x[...],self.W(j))
            if j==0: r=r+V(0)
            if j==2: r=r+V(1)
            self.qkv[:,j*768:(j+1)*768]=r.astype(bf16)
            if save and j==2: self.out(l,"qkv")
        lane=lax.broadcasted_iota(jnp.int32,(256,128),1); low_half=lane<64
        kpos=lax.broadcasted_iota(jnp.int32,(256,256),1)
        def pair(i,_):
            c=i//6; p=i-c*6
            rows=pl.ds(pl.multiple_of(c*256,256),256); o=pl.multiple_of(p*128,128)
            q2=self.qkv[rows,pl.ds(o,128)]*jnp.asarray(0.125,bf16)
            k2=self.qkv[rows,pl.ds(pl.multiple_of(768+o,128),128)]; v2=self.qkv[rows,pl.ds(pl.multiple_of(1536+o,128),128)]
            ok=kpos<lens[c]
            res=[]
            for hh in range(2):
                qm=jnp.where(low_half if hh==0 else jnp.logical_not(low_half),q2,jnp.zeros_like(q2))
                s=jnp.where(ok,dot_t(qm,k2),-1e9)
                e=jnp.exp(s-jnp.max(s,-1,keepdims=True))
                pr=(e*(1.0/jnp.sum(e,-1,keepdims=True))).astype(bf16)
                if save: self.pb[i*2+hh]=pr
                res.append(dot(pr,v2))
            self.ctx[rows,pl.ds(o,128)]=jnp.where(low_half,res[0],res[1]).astype(bf16)
            return 0
        def attend(s):
            lax.fori_loop(6*s,6*s+6,pair,0,unroll=3)
            if save and s==1: self.out(l,"pb","ctx")
        def proj_out():
            self.wcp(l,3).wait()
            z=dot(self.ctx[...],self.W(3))+V(2)+x[...].astype(f32)
            xh,rstd,h=self.ln(z,V(3),V(4))
            if save: self.xh1[...]=xh; self.rs1[...]=jnp.broadcast_to(rstd,(512,128))
            self.h1[...]=h.astype(bf16)
            self.acc[...]=h+V(5)
            if save: self.out(l,"xh1","rs1","h1")
        return [functools.partial(proj_in,j) for j in range(3)]+[functools.partial(attend,s) for s in range(2)]+[proj_out]
    def ffn_steps(self,l,save,y,lens,pooled):
        V=lambda i: self.vecs[l,i:i+1,:]
        def part(j):
            if j==0: self.load(l,[4,8,5,9,6,10,7,11])
            self.wcp(l,4+j).wait(); self.wcp(l,8+j).wait()
            u=dot(self.h1[...],self.W(4+j))+V(8+j)
            cdf,pdf=phi_parts(u)
            gb=(u*cdf).astype(bf16)
            if save:
                self.act[:,j*768:(j+1)*768]=gb
                self.der[:,j*768:(j+1)*768]=(cdf+u*pdf).astype(bf16)
            self.acc[...]+=dot(gb,self.S(j))
            if save and j==3: self.out(l,"act","der")
        def end():
            xh,rstd,yy=self.ln(self.acc[...],V(6),V(7))
            if save:
                self.xh2[...]=xh; self.rs2[...]=jnp.broadcast_to(rstd,(512,128)); self.out(l,"xh2","rs2")
            y[...]=yy.astype(bf16)
            if pooled is not None:
                tpos=lax.broadcasted_iota(jnp.int32,(256,768),0)
                for c in range(2):
                    pooled[c:c+1,:]=jnp.sum(jnp.where(tpos<lens[c],yy[c*256:(c+1)*256],0.0),0,keepdims=True)/lens[c].astype(f32)
        return [functools.partial(part,j) for j in range(4)]+[end]

def unit_scale(p): return lax.rsqrt(jnp.sum(p*p,-1,keepdims=True)+1e-6)

class Contrast:
    def __init__(self,pos,queue,lens,R):
        self.p,self.queue,self.lens=pos,queue,lens
        self.__dict__.update(R)
    def ucp(self,s):
        _,dev=self.p.peer(s)
        return remote(self.units.at[self.p.me],self.units.at[self.p.me],self.us.at[s],self.ur.at[s],dev)
    def gcp(self,s):
        j,dev=self.p.peer(s)
        return remote(self.sends.at[j],self.gets.at[self.p.me],self.gs.at[s],self.gr.at[s],dev)
    def loop(self,fn): lax.fori_loop(1,self.p.N,lambda s,_: (fn(s),0)[1],0)
    def send_units(self):
        p=self.pool_q[...]
        self.units[self.p.me]=(p*unit_scale(p)).astype(bf16).astype(f32)
        self.loop(lambda s: self.ucp(s).start())
    def share(self):
        self.loop(lambda s: self.ucp(s).wait_recv())
        N=self.p.N
        for i in range(N): self.q_all[2*i:2*i+2,:]=self.units[i]
        lg=dot_t(self.q_all[...].astype(bf16),self.queue[...])*(1.0/SHARP)
        m=jnp.max(lg,-1,keepdims=True)
        e=jnp.exp(lg-m)
        self.part[:,0:768]=dot(e.astype(bf16),self.queue[...])
        self.part[:,768:896]=jnp.broadcast_to(m,(2*N,128))
        self.part[:,896:1024]=jnp.broadcast_to(jnp.sum(e,-1,keepdims=True),(2*N,128))
        for i in range(N): self.sends[i]=self.part[2*i:2*i+2,:]
        self.gets[self.p.me]=self.sends[self.p.me]
        self.loop(lambda s: self.gcp(s).start())
    def end(self,loss,grad):
        pk=self.pool_k[...]; pq=self.pool_q[...]
        ku=(pk*unit_scale(pk)).astype(bf16).astype(f32)
        rs=unit_scale(pq)
        qu=(pq*rs).astype(bf16).astype(f32)
        pos=jnp.sum(qu*ku,-1,keepdims=True)/SHARP
        self.loop(lambda s: self.gcp(s).wait_recv())
        mi=self.gets[:,:,768:896]
        top=jnp.maximum(jnp.max(mi,0),pos)
        w=jnp.exp(mi-top[None])
        pe=jnp.exp(pos-top)
        total=jnp.sum(w*self.gets[:,:,896:1024],0)+pe
        loss[...]=top+jnp.log(total)-pos
        scale=FACTOR/SHARP
        inv=scale/total
        cp=scale*(pe/total-1.0)
        for k in range(6):
            cols=slice(k*128,(k+1)*128)
            grad[:,cols]=jnp.sum(w*self.gets[:,:,cols],0)*inv+cp*ku[:,cols]
        g=grad[...]
        d=rs*g-pq*(rs*rs*rs)*jnp.sum(pq*g,-1,keepdims=True)
        for c in range(2): grad[c:c+1,:]=d[c:c+1]/self.lens[c].astype(f32)
    def finish(self):
        self.loop(lambda s: self.ucp(s).wait_send())
        self.loop(lambda s: self.gcp(s).wait_send())

def forward_kernel(D,F,order,names,lenq,lenk,xq,xk,queue,msg,qw,pw,ew,sw,kqw,kpw,kew,ksw,
                   g,vecs,y0,y1,loss,gp,*rest):
    outs=(rest[:10],rest[10:20]); R=dict(zip(names,rest[20:]))
    pos=Place(D,F); r=768//F; rs=3072//F; f=pos.f
    bar=pltpu.get_barrier_semaphore()
    def hello(s,_):
        _,dev=pos.peer(s)
        pl.semaphore_signal(bar,inc=1,device_id=dev,device_id_type=MESH); return 0
    lax.fori_loop(1,pos.N,hello,0)
    def own(l,j):
        dst=lambda j,n: R["pk"].at[l,pl.ds(j*r,n)]
        if j<3: s,d=qw.at[l,:,pl.ds(j*768,768)],dst(j,r)
        elif j==3: s,d=pw.at[l],dst(3,r)
        elif j<8: s,d=ew.at[l,:,pl.ds((j-4)*768,768)],dst(j,r)
        else: s,d=sw.at[l],dst(8,rs)
        return pltpu.make_async_copy(s,d,R["lsem"].at[l,j])
    groups={0:range(4),1:range(4,9)}
    for l in range(2):
        for j in range(9): own(l,j).start()
    def kload(l):
        pairs=[(kqw,"kq"),(kpw,"kp"),(kew,"ke"),(ksw,"ks"),(qw,"qq"),(pw,"qp"),(ew,"qe"),(sw,"qs")]
        return [pltpu.make_async_copy(a.at[l],R[b],R["ksem"].at[i]) for i,(a,b) in enumerate(pairs)]
    def mcp(l): return pltpu.make_async_copy(R["mo"].at[l],g.at[2+l,f],R["msem"].at[l])
    for c in kload(0): c.start()
    def mirror(l):
        for c in kload(l): c.wait()
        mo=R["mo"]
        mix=lambda k,q: (MOM*k+(1.0-MOM)*q.astype(f32)).astype(bf16)
        for j in range(3):
            cols=slice(j*768,(j+1)*768); mo[l,j*r:(j+1)*r,:]=mix(R["kq"][:,cols],R["qq"][:,cols])
        mo[l,3*r:4*r,:]=mix(R["kp"][...],R["qp"][...])
        for j in range(4):
            cols=slice(j*768,(j+1)*768); mo[l,(4+j)*r:(5+j)*r,:]=mix(R["ke"][:,cols],R["qe"][:,cols])
        mo[l,8*r:8*r+rs,:]=mix(R["ks"][...],R["qs"][...])
        mcp(l).start()
        if l==0:
            for c in kload(1): c.start()
    def packed(q):
        l,r0,n=chunks[q]
        return pltpu.make_async_copy(R["pk"].at[l,pl.ds(r0,n)],g.at[l,f,pl.ds(r0,n)],R["psem"].at[q])
    waited=set()
    def ready(q):
        l=q//2
        if l<2:
            for j in groups[q%2]: own(l,j).wait()
            cp=packed(q); cp.start(); cp.wait()
        elif l not in waited:
            waited.add(l); mcp(l-2).wait()
    chunks=[(l,r0,n) for l in range(4) for r0,n in ((0,4*r),(4*r,8*r))]
    G=Gather(pos,g,chunks,ready,[R[k] for k in ("zs","zr","ys","yr","xs","xr","cs","cr","ks_","kr_")])
    vmsg=R["vmsg"]
    def vcp(s): return remote(msg,vmsg.at[f],R["vs"].at[s],R["vr"].at[s],(pos.d,(f+s)%F))
    vmsg[f]=msg[...]
    pl.semaphore_wait(bar,pos.N-1)
    for s in range(1,F): vcp(s).start()
    def vectors():
        for s in range(1,F): vcp(s).wait_recv()
        row=lax.broadcasted_iota(jnp.int32,(128,768),0); col=lax.broadcasted_iota(jnp.int32,(128,768),1)
        v=jnp.zeros((32,768),f32)
        for i in range(F):
            hot=jnp.logical_and(col==row+i*r,row<r)
            v=v+dot(vmsg[i,:,0:128],jnp.where(hot,1.0,0.0).astype(bf16))
        row=lax.broadcasted_iota(jnp.int32,(384,768),0); col=lax.broadcasted_iota(jnp.int32,(384,768),1)
        for l in range(4): vecs[l,0:8,:]=v[8*l:8*l+8]; vecs[l,8:16,:]=jnp.zeros((8,768),f32)
        for j in range(4):
            e=jnp.zeros((32,768),f32)
            for i in range(F//4):
                hot=jnp.logical_and(col==row+i*rs,row<rs)
                e=e+dot(vmsg[j*(F//4)+i,:,128:512],jnp.where(hot,1.0,0.0).astype(bf16))
            for l in range(4): vecs[l,8+j:9+j,:]=e[8*l:8*l+1]
    Fw=Forward(g,vecs,None,R); Fw.outs=outs
    Ct=Contrast(pos,queue,lenq,R)
    yk=R["yk"]
    work=[]
    for l,(save,x,y,lens,pool) in enumerate([(True,xq,y0,lenq,None),(True,y0,y1,lenq,R["pool_q"]),(False,xk,yk,lenk,None),(False,yk,R["yl"],lenk,R["pool_k"])]):
        work.append(Fw.attn_steps(l,save,x,lens,(lambda k=l-1: Fw.drain(k)) if l in (1,2) else None))
        work.append(Fw.ffn_steps(l,save,y,lens,pool))
    work[3].append(Ct.send_units)
    work[4].append(Ct.share)
    pre=[vectors,lambda: mirror(0),lambda: mirror(1)]
    act=[G.start,G.on_z,G.on_y,G.on_x,G.on_c,lambda q,i: work[q][i](),lambda q,i: pre[i]()]
    for kind,q,i in order:
        if kind in (0,4): act[kind](q)
        else: act[kind](q,i)
    Ct.end(loss,gp)
    G.finish(); Ct.finish()
    for s in range(1,F): vcp(s).wait_send()

def forward(D,F,lenq,lenk,xq,xk,queue,msg,mats,kmats,cid,order=None):
    sd=jax.ShapeDtypeStruct; S=pltpu.SemaphoreType.DMA; VM=pltpu.VMEM
    V=pl.BlockSpec(memory_space=pltpu.VMEM); ANY=pl.BlockSpec(memory_space=pl.ANY); SM=pl.BlockSpec(memory_space=pltpu.SMEM)
    A=4;B=F//4;Q=8;N=D*F; r=768//F; rs=3072//F; M=2*A*B
    buf=dict(zip(SAVED,[VM(s.shape,s.dtype) for s in saved_shapes()]))
    buf.update(acc=VM((512,768),f32),yk=VM((512,768),bf16),yl=VM((512,768),bf16),wv=VM((8,F,r,768),bf16),sv=VM((4,F//4,rs,768),bf16),
        pool_q=VM((2,768),f32),pool_k=VM((2,768),f32),units=VM((N,2,768),f32),q_all=VM((2*N,768),f32),part=VM((2*N,1024),f32),
        sends=VM((N,2,1024),f32),gets=VM((N,2,1024),f32),vmsg=VM((F,32,512),bf16),
        kq=VM((r,2304),f32),kp=VM((r,768),f32),ke=VM((r,3072),f32),ks=VM((rs,768),f32),qq=VM((r,2304),bf16),qp=VM((r,768),bf16),qe=VM((r,3072),bf16),qs=VM((rs,768),bf16),
        mo=VM((2,12*r,768),bf16),pk=VM((2,12*r,768),bf16),psem=S((4,)),
        wsem=S((12,)),osem=S((2,10)),lsem=S((2,9)),ksem=S((8,)),msem=S((2,)),us=S((N,)),ur=S((N,)),gs=S((N,)),gr=S((N,)),vs=S((F,)),vr=S((F,)),
        zs=S((Q,2,A)),zr=S((Q,2,A)),ys=S((Q,2*A,B)),yr=S((Q,2*A,B)),xs=S((Q,M)),xr=S((Q,M)),cs=S((Q,M)),cr=S((Q,M)),ks_=S((Q,M)),kr_=S((Q,M)))
    saved=saved_shapes()
    outs=[sd((4,F,12*r,768),bf16),sd((4,16,768),f32),sd((512,768),bf16),sd((512,768),bf16),sd((2,128),f32),sd((2,768),f32)]+saved*2
    res=pl.pallas_call(functools.partial(forward_kernel,D,F,ORDER if order is None else order,list(buf)),out_shape=outs,
        in_specs=[SM,SM,V,V,V,V]+[ANY]*8,out_specs=[ANY,V,V,V,V,V]+[ANY]*20,scratch_shapes=list(buf.values()),
        compiler_params=pltpu.CompilerParams(collective_id=cid,has_side_effects=True,vmem_limit_bytes=61<<20),name="forward")(lenq,lenk,xq,xk,queue,msg,*mats,*kmats)
    return res[:6],res[6:16],res[16:26]
ORDER = (
    (0, 0, 0), (1, 0, 1), (6, 0, 0), (1, 0, 2), (2, 0, 0), (6, 0, 1), (0, 1, 0), (6, 0, 2), (1, 0, 3), (2, 0, 1),
    (3, 0, 0), (2, 0, 2), (1, 1, 1), (2, 0, 3), (3, 0, 1), (2, 1, 0), (3, 0, 2), (1, 1, 2), (3, 0, 3), (4, 0, 0),
    (5, 0, 0), (5, 0, 1), (1, 1, 3), (5, 0, 2), (5, 0, 3), (3, 1, 0), (2, 1, 1), (0, 2, 0), (5, 0, 4), (2, 1, 2),
    (1, 2, 1), (5, 0, 5), (1, 2, 2), (2, 2, 0), (0, 3, 0), (2, 1, 3), (1, 2, 3), (3, 1, 1), (2, 2, 1), (3, 1, 2),
    (3, 2, 0), (2, 2, 2), (1, 3, 1), (3, 1, 3), (4, 1, 0), (5, 1, 0), (2, 2, 3), (3, 2, 1), (2, 3, 0), (3, 2, 2),
    (1, 3, 2), (5, 1, 1), (3, 2, 3), (5, 1, 2), (4, 2, 0), (5, 1, 3), (1, 3, 3), (5, 1, 4), (3, 3, 0), (2, 3, 1),
    (5, 2, 0), (0, 4, 0), (5, 2, 1), (2, 3, 2), (1, 4, 1), (5, 2, 2), (5, 2, 3), (1, 4, 2), (2, 4, 0), (0, 5, 0),
    (5, 2, 4), (2, 3, 3), (1, 4, 3), (3, 3, 1), (2, 4, 1), (3, 3, 2), (5, 2, 5), (3, 4, 0), (2, 4, 2), (1, 5, 1),
    (3, 3, 3), (4, 3, 0), (5, 3, 0), (2, 4, 3), (3, 4, 1), (2, 5, 0), (3, 4, 2), (1, 5, 2), (5, 3, 1), (3, 4, 3),
    (5, 3, 2), (4, 4, 0), (5, 3, 3), (1, 5, 3), (5, 3, 4), (3, 5, 0), (2, 5, 1), (5, 3, 5), (0, 6, 0), (5, 4, 0),
    (2, 5, 2), (5, 4, 1), (1, 6, 1), (5, 4, 2), (5, 4, 3), (1, 6, 2), (2, 6, 0), (0, 7, 0), (2, 5, 3), (5, 4, 4),
    (1, 6, 3), (3, 5, 1), (2, 6, 1), (3, 5, 2), (3, 6, 0), (5, 4, 5), (2, 6, 2), (1, 7, 1), (3, 5, 3), (4, 5, 0),
    (5, 4, 6), (2, 6, 3), (3, 6, 1), (2, 7, 0), (3, 6, 2), (1, 7, 2), (3, 6, 3), (4, 6, 0), (5, 5, 0), (1, 7, 3),
    (5, 5, 1), (3, 7, 0), (2, 7, 1), (5, 5, 2), (5, 5, 3), (2, 7, 2), (5, 5, 4), (5, 6, 0), (5, 6, 1), (2, 7, 3),
    (5, 6, 2), (3, 7, 1), (5, 6, 3), (3, 7, 2), (5, 6, 4), (3, 7, 3), (4, 7, 0), (5, 6, 5), (5, 7, 0), (5, 7, 1),
    (5, 7, 2), (5, 7, 3), (5, 7, 4),
)

def piece_sizes(F):
    n=4*(768//F); np_=n//3
    return n,np_,n-np_

class Reduce:
    def __init__(self,pos,src,flush,R,outs,r):
        self.p,self.src,self.flush,self.outs,self.r=pos,src,flush,outs,r
        self.__dict__.update(R)
        self.n,self.np,self.nq=piece_sizes(pos.F); self.hp=self.np//2; self.hq=self.nq//2
        m=pl.multiple_of; c,x=pos.c,pos.x
        self.mycols=pl.ds(m(c*384,128),384); self.ocols=pl.ds(m((1-c)*384,128),384)
        self.Pown=pl.ds(m(x*self.hp,16),self.hp); self.Poth=pl.ds(m((1-x)*self.hp,16),self.hp)
        self.Qown=pl.ds(m(self.np+x*self.hq,16),self.hq); self.Qoth=pl.ds(m(self.np+(1-x)*self.hq,16),self.hq)
        self.Qall=pl.ds(self.np,self.nq)
        self.X=(pos.xd,pos.f); self.C=(pos.cd,pos.f)
        self.busy={}
        self.rest=[]
    def Y(self,t): return (self.p.d,self.p.a*self.p.B+(self.p.b+t)%self.p.B)
    def Z(self,s): return (self.p.d,((self.p.a+s)%self.p.A)*self.p.B+self.p.b)
    def Oo(self,s): return ((self.p.d+4*s)%self.p.D,self.p.f)
    def rc(self,i,k,src,dst,dev): return remote(src,dst,self.SS.at[i,k],self.RS.at[i,k],dev)
    def go(self,cp,key=None):
        cp.start()
        if key is None: self.rest.append(cp)
        else: self.busy.setdefault(key,[]).append(cp)
    def free(self,key):
        for cp in self.busy.pop(key,[]): cp.wait_send()
    def ky(self,t): return 5+t
    def kq(self,t): return 5+self.p.B+t
    def kz(self,s): return 5+2*self.p.B+s
    def ko(self,s): return 5+2*self.p.B+self.p.A+s
    def Tv(self,i): return self.T.at[i%3].reshape(self.p.A,self.p.B,self.n,384)
    def cC(self,i): return self.rc(i,0,self.src(i).at[:,:,self.ocols],self.RC.at[i],self.C)
    def cPx(self,i): return self.rc(i,1,self.T.at[i%3,:,self.Poth],self.RPX.at[i],self.X)
    def cPy(self,i,t): return self.rc(i,self.ky(t),self.Tv(i).at[:,(self.p.b+t)%self.p.B,self.Pown],self.RPY.at[i,t-1],self.Y(t))
    def cQy(self,i,t): return self.rc(i,self.kq(t),self.Tv(i).at[:,(self.p.b+t)%self.p.B,self.Qall],self.RQY.at[i,t-1],self.Y(t))
    def cQx(self,i): return self.rc(i,2,self.Tv(i).at[:,self.p.b,self.Qoth],self.RQX.at[i],self.X)
    def cZ(self,i,s): return self.rc(i,self.kz(s),self.T3.at[i%3,(self.p.a+s)%self.p.A],self.RZ.at[i,s-1],self.Z(s))
    def cO(self,i,s): return self.rc(i,self.ko(s),self.TO.at[i],self.RO.at[i,s-1],self.Oo(s))
    def cFX(self,i,w,mine=True):
        r=((self.Pown,self.Qown) if mine else (self.Poth,self.Qoth))[w]; v=self.FIN.at[i,r,self.mycols]
        return self.rc(i,3+w,v,v,self.X)
    def cFC(self,i,mine=True):
        v=self.FIN.at[i,:,self.mycols if mine else self.ocols]
        return self.rc(i,5,v,v,self.C)
    def s0(self,i):
        self.flush(i)
        self.go(self.cC(i))
    def loads(self,i):
        return [pltpu.make_async_copy(self.src(i).at[:,:,self.mycols],self.T.at[i%3],self.LS.at[i,0]),
                pltpu.make_async_copy(self.RC.at[i],self.RCV,self.LS.at[i,1])]
    def s1(self,i):
        self.free(("T",i%3))
        self.cC(i).wait_recv()
        for cp in self.loads(i): cp.start()
    def s2(self,i):
        T,k=self.T,i%3
        for cp in self.loads(i): cp.wait()
        def body(f,_):
            T[k,f]=(T[k,f].astype(f32)+self.RCV[f].astype(f32)).astype(bf16); return 0
        lax.fori_loop(0,self.p.F,body,0)
        self.go(self.cPx(i),("T",k))
        for t in range(1,self.p.B): self.go(self.cQy(i,t),("T",k))
    def s3(self,i):
        T,k=self.T,i%3
        self.cPx(i).wait_recv()
        def body(f,_):
            T[k,f,self.Pown]=(T[k,f,self.Pown].astype(f32)+self.RPX[i,f].astype(f32)).astype(bf16); return 0
        lax.fori_loop(0,self.p.F,body,0)
        for t in range(1,self.p.B): self.go(self.cPy(i,t),("T",k))
    def s4(self,i):
        T,k=self.T,i%3
        for t in range(1,self.p.B): self.cQy(i,t).wait_recv()
        def body(a,_):
            fo=a*self.p.B+self.p.b
            v=T[k,fo,self.Qall].astype(f32)
            for t in range(1,self.p.B): v=v+self.RQY[i,t-1,a].astype(f32)
            T[k,fo,self.Qall]=v.astype(bf16); return 0
        lax.fori_loop(0,self.p.A,body,0)
        self.go(self.cQx(i),("T",k))
    def s5(self,i):
        T,k,k3=self.T,i%3,i%3
        self.free(("T3",k3))
        for t in range(1,self.p.B): self.cPy(i,t).wait_recv()
        self.cQx(i).wait_recv()
        def body(a,_):
            fo=a*self.p.B+self.p.b
            v=T[k,fo,self.Pown].astype(f32)
            for t in range(1,self.p.B): v=v+self.RPY[i,t-1,a].astype(f32)
            self.T3[k3,a,0:self.hp]=v.astype(bf16)
            self.T3[k3,a,self.hp:self.hp+self.hq]=(T[k,fo,self.Qown].astype(f32)+self.RQX[i,a].astype(f32)).astype(bf16)
            return 0
        lax.fori_loop(0,self.p.A,body,0)
        for s in range(1,self.p.A): self.go(self.cZ(i,s),("T3",k3))
    def s6(self,i):
        v=self.T3[i%3,self.p.a].astype(f32)
        for s in range(1,self.p.A):
            self.cZ(i,s).wait_recv()
            v=v+self.RZ[i,s-1].astype(f32)
        if self.p.O>1:
            self.TO[i]=v.astype(bf16)
            for s in range(1,self.p.O): self.go(self.cO(i,s))
            for s in range(1,self.p.O):
                self.cO(i,s).wait_recv(); v=v+self.RO[i,s-1].astype(f32)
        v=v.astype(bf16)
        self.FIN[i,self.Pown,self.mycols]=v[:self.hp]; self.FIN[i,self.Qown,self.mycols]=v[self.hp:]
        for w in (0,1): self.go(self.cFX(i,w))
    def s7(self,i):
        for w in (0,1): self.cFX(i,w,False).wait_recv()
        self.go(self.cFC(i))
    def outcps(self,i):
        l=1-i//3; kind=i%3; r=self.r; oq,op,oe,os=self.outs; F=self.FIN.at[i]
        if kind==0: pairs=[(F,os.at[l])]
        elif kind==1: pairs=[(F.at[pl.ds(j*r,r)],oe.at[l,:,pl.ds(j*768,768)]) for j in range(4)]
        else: pairs=[(F.at[pl.ds(j*r,r)],oq.at[l,:,pl.ds(j*768,768)]) for j in range(3)]+[(F.at[pl.ds(3*r,r)],op.at[l])]
        return [pltpu.make_async_copy(s,d,self.OS.at[i,j]) for j,(s,d) in enumerate(pairs)]
    def s8(self,i):
        self.cFC(i,False).wait_recv()
        for cp in self.outcps(i): cp.start()
    def vstage(self,k):
        B,A,O=self.p.B,self.p.A,self.p.O
        st=[(self.VRC,[self.C],0),(self.VRX,[self.X],1),(self.VRY,[self.Y(t) for t in range(1,B)],2),(self.VRZ,[self.Z(s) for s in range(1,A)],2+B)]
        if O>1: st.append((self.VRO,[self.Oo(s) for s in range(1,O)],2+B+A))
        def cps(k):
            buf,devs,k0=st[k]
            return [remote(self.VS.at[k],buf.at[q],self.VSS.at[k0+q],self.VRS.at[k0+q],dv) for q,dv in enumerate(devs)]
        if k>len(st): return
        if k>0:
            v=self.VS[k-1]
            for q,cp in enumerate(cps(k-1)):
                cp.wait_recv(); v=v+st[k-1][0][q]
            if k<len(st): self.VS[k]=v
            else: self.vout[...]=v
        if k<len(st):
            for cp in cps(k): self.go(cp)
    def finish(self):
        for key in list(self.busy): self.free(key)
        for cp in self.rest: cp.wait_send()
        for i in range(6):
            for cp in self.outcps(i): cp.wait()

class Backward:
    NAMES=("qkv","pb","ctx","xh1","rs1","h1","xh2","rs2","x")
    SAME={"xh1":"xh","xh2":"xh","rs1":"rsd","rs2":"rsd"}
    def __init__(self,lens,gp,vecs,g,dg,saved,xs,R,dx):
        self.lens,self.gp,self.vecs,self.g,self.dg,self.saved,self.xs,self.dx=lens,gp,vecs,g,dg,saved,xs,dx
        self.__dict__.update(R)
        self.F=g.shape[1]; self.r=768//self.F; self.rs=3072//self.F
        self.slot=0; self.stage={}; self.blocks={}
        self.chunkno=0
    def cp(self,l,name):
        src=self.xs[l] if name=="x" else self.saved[l][SAVED.index(name)]
        return pltpu.make_async_copy(src,self.__dict__[self.SAME.get(name,name)],self.isem.at[self.NAMES.index(name)])
    def fetch(self,l,*names):
        if l<0: return
        for n in names: self.cp(l,n).start()
    def need(self,l,*names):
        for n in names: self.cp(l,n).wait()
    def wcp(self,l,j): return pltpu.make_async_copy(self.g.at[l,:,pl.ds(j*self.r,self.r),:],self.wa.at[j],self.wsem.at[j])
    def ccps(self,l,j):
        s=j%2; F=self.F; cols=pl.ds(j*768,768)
        srcs=[(self.g.at[l,:,pl.ds((4+j)*self.r,self.r),:],self.we.at[s]),(self.g.at[l,pl.ds(j*(F//4),F//4),pl.ds(8*self.r,self.rs),:],self.wsx.at[s]),
              (self.saved[l][SAVED.index("act")].at[:,cols],self.act.at[s]),(self.saved[l][SAVED.index("der")].at[:,cols],self.der.at[s])]
        return [pltpu.make_async_copy(a,b,self.csem.at[s,k]) for k,(a,b) in enumerate(srcs)]
    def fetch_chunk(self,l,j):
        if j>=4: l,j=l-1,j-4
        if l<0: return
        for c in self.ccps(l,j): c.start()
    def fetch_w(self,l,*js):
        if l<0: return
        for j in js: self.wcp(l,j).start()
    def put(self,l,j,val):
        k=self.slot; self.slot=(k+1)%3
        if k in self.stage: self.stage.pop(k).wait()
        self.st[k]=val.astype(bf16)
        if j<8: src,dst=self.st.at[k].reshape(self.F,self.r,768),self.dg.at[l,:,pl.ds(j*self.r,self.r)]
        else:
            q=j-8; n=self.F//4
            src,dst=self.st.at[k].reshape(n,self.rs,768),self.dg.at[l,pl.ds(q*n,n),pl.ds(8*self.r,self.rs)]
        cp=pltpu.make_async_copy(src,dst,self.ssem.at[k]); cp.start()
        self.stage[k]=cp; self.blocks[k]=(l,j)
    def flush(self,i):
        l=1-i//3; lo={0:8,1:4,2:0}[i%3]
        for k in list(self.stage):
            bl,bj=self.blocks[k]
            if bl==l and lo<=bj<lo+4: self.stage.pop(k).wait()
    def first(self):
        l=1
        self.fetch(l,"xh2","rs2"); self.fetch_chunk(l,0); self.fetch(l,"h1"); self.fetch_chunk(l,1)
        self.fetch(l,"ctx"); self.fetch_w(l,3); self.fetch(l,"qkv","pb"); self.fetch_w(l,0,1,2); self.fetch(l,"x")
        self.VS[0]=jnp.zeros(self.VS.shape[1:],f32)
    def vrow(self,l,k,val): self.VS[0,l*12+k:l*12+k+1,:]=jnp.sum(val,0,keepdims=True)
    def steps(self,l):
        V=lambda i: self.vecs[l,i:i+1,:]
        r=self.r
        def ln_back(dy,xh,rstd,gain):
            t=dy*gain
            return rstd*(t-jnp.mean(t,-1,keepdims=True)-xh*jnp.mean(t*xh,-1,keepdims=True))
        def second():
            if l==1:
                tpos=lax.broadcasted_iota(jnp.int32,(256,768),0)
                for c in range(2): self.acc[c*256:(c+1)*256,:]=jnp.where(tpos<self.lens[c],self.gp[c:c+1,:],0.0)
            dy=self.acc[...]
            self.need(l,"xh2","rs2")
            xh=self.xh[...]
            self.vrow(l,6,dy*xh); self.vrow(l,7,dy)
            d2=ln_back(dy,xh,self.rsd[:,0:1],V(6))
            self.acc[...]=d2
            self.dr[...]=d2.astype(bf16)
            self.vrow(l,5,self.dr[...].astype(f32))
            self.fetch(l,"xh1","rs1")
        def ffn(j):
            s=j%2
            for c in self.ccps(l,j): c.wait()
            if j==0: self.need(l,"h1")
            E=self.we[s].reshape(768,768); S=self.wsx[s].reshape(768,768)
            self.put(l,8+j,tdot(self.act[s],self.dr[...]))
            du=(dot_t(self.dr[...],S)*self.der[s].astype(f32)).astype(bf16)
            self.vrow(l,8+j,du.astype(f32))
            self.put(l,4+j,tdot(self.h1[...],du))
            self.acc[...]+=dot_t(du,E)
            self.fetch_chunk(l,j+2)
            if j==3: self.fetch(l-1,"h1")
        def middle():
            self.need(l,"xh1","rs1","ctx")
            dh=self.acc[...]; xh=self.xh[...]
            self.vrow(l,3,dh*xh); self.vrow(l,4,dh)
            d1=ln_back(dh,xh,self.rsd[:,0:1],V(3))
            self.acc[...]=d1
            self.dr[...]=d1.astype(bf16)
            self.vrow(l,2,self.dr[...].astype(f32))
            self.wcp(l,3).wait()
            self.put(l,3,tdot(self.ctx[...],self.dr[...]))
            self.ctx[...]=dot_t(self.dr[...],self.wa[3].reshape(768,768)).astype(bf16)
            self.fetch(l-1,"xh2","rs2"); self.fetch_w(l-1,3)
        lane=lax.broadcasted_iota(jnp.int32,(256,128),1); low_half=lane<64
        def pair(i,_):
            c=i//6; p=i-c*6; qkv=self.qkv
            rows=pl.ds(pl.multiple_of(c*256,256),256); o=pl.multiple_of(p*128,128)
            o1=pl.multiple_of(768+o,128); o2=pl.multiple_of(1536+o,128)
            q2=qkv[rows,pl.ds(o,128)]; k2=qkv[rows,pl.ds(o1,128)]; v2=qkv[rows,pl.ds(o2,128)]
            dc=self.ctx[rows,pl.ds(o,128)]
            res=[]
            for hh in range(2):
                m=low_half if hh==0 else jnp.logical_not(low_half)
                P=self.pb[i*2+hh]; pf=P.astype(f32)
                dP=dot_t(jnp.where(m,dc,jnp.zeros_like(dc)),v2)
                pd=pf*dP
                dS=(pd-pf*jnp.sum(pd,-1,keepdims=True)).astype(bf16)
                res.append((dot(dS,k2),tdot(dS,q2),tdot(P,dc)))
            sel=lambda t: jnp.where(low_half,res[0][t],res[1][t])
            qkv[rows,pl.ds(o,128)]=(sel(0)*0.125).astype(bf16)
            qkv[rows,pl.ds(o1,128)]=(sel(1)*0.125).astype(bf16)
            qkv[rows,pl.ds(o2,128)]=sel(2).astype(bf16)
            return 0
        def attend(s):
            if s==0: self.need(l,"qkv","pb")
            lax.fori_loop(4*s,4*s+4,pair,0,unroll=2)
            if s==2: self.fetch(l-1,"pb","ctx")
        def mixed(j):
            self.wcp(l,j).wait()
            if j==0: self.need(l,"x")
            dm=self.qkv[:,j*768:(j+1)*768]
            if j!=1: self.vrow(l,0 if j==0 else 1,dm.astype(f32))
            self.put(l,j,tdot(self.x[...],dm))
            self.acc[...]+=dot_t(dm,self.wa[j].reshape(768,768))
            self.fetch_w(l-1,j)
            if j==2:
                self.fetch(l-1,"qkv","x")
                if l==0: self.dx[...]=self.acc[...].astype(bf16)
        P=functools.partial
        return [second]+[P(ffn,j) for j in range(4)]+[middle]+[P(attend,s) for s in range(3)]+[P(mixed,j) for j in range(3)]

def backward_kernel(D,F,order,names,lens,gp,vecs,g,x0,y0,*rest):
    saved=(rest[0:10],rest[10:20]); dg,dx,oq,op,oe,os,vout,rcv=rest[20:28]; R=dict(zip(names,rest[28:])); R["RC"]=rcv
    pos=Place(D,F); n=4*(768//F)
    bar=pltpu.get_barrier_semaphore()
    peers=[(pos.xd,pos.f),(pos.cd,pos.f)]+[(pos.d,(pos.f+s)%F) for s in range(1,F)]+[((pos.d+4*s)%D,pos.f) for s in range(1,pos.O)]
    for dev in peers: pl.semaphore_signal(bar,inc=1,device_id=dev,device_id_type=MESH)
    Bw=Backward(lens,gp,vecs,g,dg,saved,(x0,y0),R,dx)
    Bw.first()
    src=lambda i: dg.at[1-i//3,:,pl.ds((2-i%3)*n,n),:]
    Rd=Reduce(pos,src,Bw.flush,R,(oq,op,oe,os),768//F); Rd.vout=vout
    work={1:Bw.steps(1),0:Bw.steps(0)}
    stages=[Rd.s0,Rd.s1,Rd.s2,Rd.s3,Rd.s4,Rd.s5,Rd.s6,Rd.s7,Rd.s8]
    pl.semaphore_wait(bar,len(peers))
    for kind,i,k in order:
        if kind==0: work[i][k]()
        elif kind==1: stages[k](i)
        else: Rd.vstage(k)
    Rd.finish()

def backward(D,F,lens,gp,vecs,g,x0,y0,saved0,saved1,cid,order=None):
    sd=jax.ShapeDtypeStruct; S=pltpu.SemaphoreType.DMA; VM=pltpu.VMEM
    V=pl.BlockSpec(memory_space=pltpu.VMEM); ANY=pl.BlockSpec(memory_space=pl.ANY); SM=pl.BlockSpec(memory_space=pltpu.SMEM)
    A=4;B=F//4;O=D//4; r=768//F; rs=3072//F; n,np_,nq=piece_sizes(F); nh=n//2; K=8+2*B+A+O
    shp=dict(zip(SAVED,saved_shapes()))
    buf={k:VM(shp[k].shape,shp[k].dtype) for k in ("qkv","pb","ctx","h1")}
    buf.update(xh=VM((512,768),f32),rsd=VM((512,128),f32))
    buf.update(x=VM((512,768),bf16),act=VM((2,512,768),bf16),der=VM((2,512,768),bf16),wa=VM((4,F,r,768),bf16),we=VM((2,F,r,768),bf16),wsx=VM((2,F//4,rs,768),bf16),
        acc=VM((512,768),f32),dr=VM((512,768),bf16),st=VM((3,768,768),bf16),
        T=VM((3,F,n,384),bf16),RCV=VM((F,n,384),bf16),RPX=VM((6,F,np_//2,384),bf16),RPY=VM((6,B-1,A,np_//2,384),bf16),RQY=VM((6,B-1,A,nq,384),bf16),
        RQX=VM((6,A,nq//2,384),bf16),T3=VM((3,A,nh,384),bf16),RZ=VM((6,A-1,nh,384),bf16),FIN=VM((6,n,768),bf16),
        VS=VM((5,24,768),f32),VRC=VM((1,24,768),f32),VRX=VM((1,24,768),f32),VRY=VM((B-1,24,768),f32),VRZ=VM((A-1,24,768),f32),
        isem=S((9,)),wsem=S((4,)),csem=S((2,4)),ssem=S((3,)),LS=S((6,2)),OS=S((6,4)),SS=S((6,K)),RS=S((6,K)),VSS=S((K,)),VRS=S((K,)))
    if O>1: buf.update(RO=VM((6,O-1,nh,384),bf16),TO=VM((6,nh,384),bf16),VRO=VM((O-1,24,768),f32))
    outs=[sd((2,F,12*r,768),bf16),sd((512,768),bf16),sd((2,r,2304),bf16),sd((2,r,768),bf16),sd((2,r,3072),bf16),sd((2,rs,768),bf16),sd((24,768),f32),sd((6,F,n,384),bf16)]
    res=pl.pallas_call(functools.partial(backward_kernel,D,F,BORDER if order is None else order,list(buf)),out_shape=outs,
        in_specs=[SM,V,V]+[ANY]*23,out_specs=[ANY,V,ANY,ANY,ANY,ANY,V,ANY],scratch_shapes=list(buf.values()),
        compiler_params=pltpu.CompilerParams(collective_id=cid,has_side_effects=True,vmem_limit_bytes=62<<20),name="backward")(lens,gp,vecs,g,x0,y0,*saved0,*saved1)
    return res[1:7]
BORDER = (
    (0, 1, 0), (0, 1, 1), (0, 1, 2), (0, 1, 3), (0, 1, 4), (1, 0, 0), (1, 1, 0), (0, 1, 5), (0, 1, 6), (1, 0, 1),
    (0, 1, 7), (1, 0, 2), (1, 1, 1), (0, 1, 8), (1, 1, 2), (0, 1, 9), (0, 1, 10), (1, 0, 3), (0, 1, 11), (1, 2, 0),
    (0, 0, 0), (0, 0, 1), (1, 0, 4), (1, 1, 3), (1, 2, 1), (0, 0, 2), (1, 2, 2), (0, 0, 3), (1, 1, 4), (0, 0, 4),
    (1, 0, 5), (1, 2, 3), (1, 3, 0), (1, 4, 0), (0, 0, 5), (0, 0, 6), (1, 1, 5), (1, 3, 1), (0, 0, 7), (1, 0, 6),
    (1, 3, 2), (1, 4, 1), (0, 0, 8), (1, 0, 7), (1, 2, 4), (1, 4, 2), (1, 0, 8), (0, 0, 9), (1, 1, 6), (0, 0, 10),
    (1, 3, 3), (0, 0, 11), (1, 5, 0), (2, 0, 0), (2, 0, 1), (1, 2, 5), (1, 3, 4), (1, 5, 1), (2, 0, 2), (1, 5, 2),
    (2, 0, 3), (1, 4, 3), (2, 0, 4), (1, 1, 7), (2, 0, 5), (1, 1, 8), (1, 2, 6), (1, 4, 4), (1, 3, 5), (1, 5, 3),
    (1, 2, 7), (1, 2, 8), (1, 3, 6), (1, 5, 4), (1, 3, 7), (1, 4, 5), (1, 3, 8), (1, 5, 5), (1, 4, 6), (1, 4, 7),
    (1, 4, 8), (1, 5, 6), (1, 5, 7), (1, 5, 8),
)


def on_device(dp, fsdp, x_query, x_key, len_query, len_key, queue, *params):
    query_params, key_params = params[:13], params[13:]
    num_crops, seq_len, width = x_query.shape
    r = width // fsdp
    order = (1, 2, 4, 5, 6, 10, 11, 12)
    small_q = jnp.stack([query_params[i] for i in order], 1)
    small_k = jnp.stack([key_params[i] for i in order], 1)
    bias_q, bias_k = query_params[8], key_params[8]
    mix = lambda k, q: (MOM * k + (1.0 - MOM) * q.astype(f32)).astype(bf16)
    small = jnp.concatenate([small_q, mix(small_k, small_q)], 0).reshape(32, r)
    wide = jnp.concatenate([bias_q, mix(bias_k, bias_q)], 0)
    wide = jnp.pad(wide[:, None, :], ((0, 0), (0, 7), (0, 384 - wide.shape[1]))).reshape(32, 384)
    msg = jnp.concatenate([jnp.pad(small, ((0, 0), (0, 128 - r))), wide], 1)
    big = (0, 3, 7, 9)
    x0 = x_query.reshape(num_crops * seq_len, width)
    xk = x_key.reshape(num_crops * seq_len, width)
    (gathered, vecs, y0, y1, loss, grad_pooled), saved0, saved1 = forward(
        dp, fsdp, len_query, len_key, x0, xk, queue, msg,
        [query_params[i] for i in big], [key_params[i] for i in big], 1)
    dx0, *grads, vsum = backward(dp, fsdp, len_query, grad_pooled, vecs, gathered, x0, y0, saved0, saved1, 2)
    grad_qkv, grad_proj, grad_expand, sh_g = [v.astype(f32) for v in grads]
    me = lax.axis_index("fsdp")
    vsum = vsum.reshape(2, 12, width)
    mine = lax.dynamic_slice_in_dim(vsum[:, :8], me * r, r, 2)
    ebg = lax.dynamic_slice_in_dim(vsum[:, 8:12].reshape(2, 4 * width), me * 4 * r, 4 * r, 1)
    qb, vb, pb, g1, b1, sb, g2, b2 = [mine[:, i] for i in range(8)]
    hidden = y1.reshape(num_crops, seq_len, width)
    grad_input = dx0.reshape(num_crops, seq_len, width)
    return (hidden, grad_input, grad_qkv, qb, vb, grad_proj, pb, g1, b1, grad_expand, ebg, sh_g, sb, g2, b2, loss[:, 0])


def solution(mesh):
    in_specs = (
        P(("dp", "fsdp"), None, None),
        P(("dp", "fsdp"), None, None),
        P(("dp", "fsdp")),
        P(("dp", "fsdp")),
        P(("dp", "fsdp"), None),
        P(None, "fsdp", None),
        P(None, "fsdp"),
        P(None, "fsdp"),
        P(None, "fsdp", None),
        P(None, "fsdp"),
        P(None, "fsdp"),
        P(None, "fsdp"),
        P(None, "fsdp", None),
        P(None, "fsdp"),
        P(None, "fsdp", None),
        P(None, "fsdp"),
        P(None, "fsdp"),
        P(None, "fsdp"),
        P(None, "fsdp", None),
        P(None, "fsdp"),
        P(None, "fsdp"),
        P(None, "fsdp", None),
        P(None, "fsdp"),
        P(None, "fsdp"),
        P(None, "fsdp"),
        P(None, "fsdp", None),
        P(None, "fsdp"),
        P(None, "fsdp", None),
        P(None, "fsdp"),
        P(None, "fsdp"),
        P(None, "fsdp"),
    )
    out_specs = (
        P(("dp", "fsdp"), None, None),
        P(("dp", "fsdp"), None, None),
        P(None, "fsdp", None),
        P(None, "fsdp"),
        P(None, "fsdp"),
        P(None, "fsdp", None),
        P(None, "fsdp"),
        P(None, "fsdp"),
        P(None, "fsdp"),
        P(None, "fsdp", None),
        P(None, "fsdp"),
        P(None, "fsdp", None),
        P(None, "fsdp"),
        P(None, "fsdp"),
        P(None, "fsdp"),
        P(("dp", "fsdp")),
    )
    return jax.shard_map(
        functools.partial(on_device, mesh.shape["dp"], mesh.shape["fsdp"]), mesh=mesh, in_specs=in_specs, out_specs=out_specs, check_vma=False
    )
```

```python
import functools

import jax
import jax.numpy as jnp
from jax import lax
from jax.experimental import pallas as pl
from jax.experimental.pallas import tpu as pltpu
from jax.sharding import PartitionSpec as P

f32=jnp.float32; bf16=jnp.bfloat16
HEADS=12
def dot(a,b): return lax.dot_general(a,b,(((1,),(0,)),((),())),preferred_element_type=f32)
def dot_t(a,b): return lax.dot_general(a,b,(((1,),(1,)),((),())),preferred_element_type=f32)
def tdot(a,b): return lax.dot_general(a,b,(((0,),(0,)),((),())),preferred_element_type=f32)

def phi_parts(u):
    z=jnp.abs(u)*0.7071067811865476
    t=1.0/(1.0+0.3275911*z)
    e=jnp.exp(-z*z)
    poly=t*(0.254829592+t*(-0.284496736+t*(1.421413741+t*(-1.453152027+t*1.061405429))))
    half=0.5*poly*e
    cdf=jnp.where(u>=0,1.0-half,half)
    return cdf,e*0.3989422804014327

def load_weights(l,g,wv,sv,sem):
    F=g.shape[1]; r=768//F; rs=3072//F
    cps=[]
    for j in range(8):
        cps.append(pltpu.make_async_copy(g.at[l,:,pl.ds(j*r,r),:],wv.at[j],sem.at[j]))
    for j in range(4):
        cps.append(pltpu.make_async_copy(g.at[l,pl.ds(j*(F//4),F//4),pl.ds(8*r,rs),:],sv.at[j],sem.at[8+j]))
    return cps

MESH=pl.DeviceIdType.MESH
SHARP=0.05
FACTOR=512.0
MOM=0.9995

def remote(src,dst,ss,rs,dev):
    return pltpu.make_async_remote_copy(src,dst,ss,rs,device_id=dev,device_id_type=MESH)

def when(cond,fn):
    if cond is True: fn()
    else: pl.when(cond)(fn)

class Place:
    def __init__(self,D,F):
        self.D,self.F=D,F; self.A=4; self.B=F//4; self.O=D//4
        d=self.d=lax.axis_index("dp"); f=self.f=lax.axis_index("fsdp")
        self.a=f//self.B; self.b=f%self.B; self.o=d//4; self.x=(d//2)%2; self.c=d%2
        self.xd=d+2-4*self.x; self.cd=d+1-2*self.c
        self.N=D*F; self.me=d*F+f
    def peer(self,s):
        p=(self.me+s)%self.N
        return p,(p//self.F,p%self.F)

class Gather:
    def __init__(self,pos,g,chunks,ready,sems):
        self.p,self.g,self.chunks,self.ready=pos,g,chunks,ready
        self.zs,self.zr,self.ys,self.yr,self.xs,self.xr,self.cs,self.cr,self.ks,self.kr=sems
    def rows(self,q,t0,n):
        return pl.ds(pl.multiple_of(self.chunks[q][1]+t0*16,16),n*16)
    def parts(self,q):
        p=self.p; half=self.chunks[q][2]//32; nx=(half*13+18)//36; nyz=half-nx
        h=p.c*half; hc=(1-p.c)*half
        R=lambda t0,n: self.rows(q,t0,n)
        return dict(yz=R(h+p.x*nx,nyz),xs=R(h+p.x*nyz,nx),xr=R(h+(1-p.x)*nyz,nx),oyz=R(hc+p.x*nx,nyz),oxr=R(hc+(1-p.x)*nyz,nx))
    def at(self,q,fs,part): return self.g.at[self.chunks[q][0],fs,self.parts(q)[part]]
    def src_a(self,hd): return self.p.a-hd[0] if hd[1]==0 else self.p.a+hd[0]
    def has(self,hd):
        if hd[0]==0: return True
        return (self.p.a>=hd[0]) if hd[1]==0 else (self.p.a+hd[0]<self.p.A)
    def canpass(self,dr): return (self.p.a+1<self.p.A) if dr==0 else (self.p.a>0)
    def z(self,q,hd,fs):
        na=self.p.a+1 if hd[1]==0 else self.p.a-1
        r=self.at(q,fs,"yz")
        return remote(r,r,self.zs.at[q,hd[1],hd[0]],self.zr.at[q,hd[1],hd[0]],(self.p.d,na*self.p.B+self.p.b))
    def slot(self,hd): return hd[0]*2+hd[1]
    def y(self,q,hd,fs,t):
        r=self.at(q,fs,"yz"); s=self.slot(hd)
        return remote(r,r,self.ys.at[q,s,t],self.yr.at[q,s,t],(self.p.d,self.p.a*self.p.B+(self.p.b+t)%self.p.B))
    def xc(self,q,fs,i,part="xs"):
        r=self.at(q,fs,part); return remote(r,r,self.xs.at[q,i],self.xr.at[q,i],(self.p.xd,self.p.f))
    def cc(self,q,fs,i,part="yz"):
        r=self.at(q,fs,part); return remote(r,r,self.cs.at[q,i],self.cr.at[q,i],(self.p.cd,self.p.f))
    def kc(self,q,fs,i,part="xr"):
        r=self.at(q,fs,part); return remote(r,r,self.ks.at[q,i],self.kr.at[q,i],(self.p.cd,self.p.f))
    def shard(self,hd,t=0): return self.src_a(hd)*self.p.B+(self.p.b-t)%self.p.B
    def hds(self,hh): return [(0,0)] if hh==0 else [(hh,0),(hh,1)]
    def start(self,q):
        self.ready(q)
        f=self.p.f
        for dr in (0,1): when(self.canpass(dr),lambda dr=dr: self.z(q,(1,dr),f).start())
        for t in range(1,self.p.B): self.y(q,(0,0),f,t).start()
    def on_z(self,q,hh):
        for hd in self.hds(hh):
            def go(hd=hd):
                fs=self.shard(hd); dr=hd[1]
                self.z(q,hd,fs).wait_recv()
                if hh+1<self.p.A: when(self.canpass(dr),lambda: self.z(q,(hh+1,dr),fs).start())
                for t in range(1,self.p.B): self.y(q,hd,fs,t).start()
                i=self.slot(hd)*self.p.B
                self.xc(q,fs,i).start(); self.cc(q,fs,i).start()
            when(self.has(hd),go)
    def on_y(self,q,hh):
        for hd in self.hds(hh):
            for t in range(1,self.p.B):
                def go(hd=hd,t=t):
                    fs=self.shard(hd,t); i=self.slot(hd)*self.p.B+t
                    self.y(q,hd,fs,t).wait_recv()
                    self.xc(q,fs,i).start(); self.cc(q,fs,i).start()
                when(self.has(hd),go)
    def each(self,hh,fn):
        for hd in self.hds(hh):
            for t in range(self.p.B):
                if hh==0 and t==0: continue
                when(self.has(hd),lambda hd=hd,t=t: fn(self.shard(hd,t),self.slot(hd)*self.p.B+t))
    def on_x(self,q,hh):
        def go(fs,i):
            self.xc(q,fs,i,"xr").wait_recv(); self.kc(q,fs,i).start()
        self.each(hh,go)
    def on_c(self,q):
        def go(fs,i):
            self.cc(q,fs,i,"oyz").wait_recv(); self.kc(q,fs,i,"oxr").wait_recv()
        for hh in range(self.p.A): self.each(hh,go)
    def finish(self):
        f=self.p.f
        for q in range(len(self.chunks)):
            def go(fs,i):
                self.xc(q,fs,i).wait_send(); self.cc(q,fs,i).wait_send(); self.kc(q,fs,i).wait_send()
            for hh in range(self.p.A):
                self.each(hh,go)
                for hd in self.hds(hh):
                    for t in range(1,self.p.B): when(self.has(hd),lambda hd=hd,t=t: self.y(q,hd,f,t).wait_send())
            for dr in (0,1):
                for hh in range(1,self.p.A):
                    cond=self.canpass(dr)
                    if hh>1: cond=jnp.logical_and(cond,self.has((hh-1,dr)))
                    pl.when(cond)(lambda hh=hh,dr=dr: self.z(q,(hh,dr),f).wait_send())

SAVED=("qkv","pb","ctx","xh1","rs1","h1","act","der","xh2","rs2")
def saved_shapes():
    sd=jax.ShapeDtypeStruct
    return [sd((512,2304),bf16),sd((24,256,256),bf16),sd((512,768),bf16),sd((512,768),f32),sd((512,128),f32),sd((512,768),bf16),sd((512,3072),bf16),sd((512,3072),bf16),sd((512,768),f32),sd((512,128),f32)]

class Forward:
    def __init__(self,g,vecs,lens,R):
        self.g,self.vecs,self.lens=g,vecs,lens
        self.__dict__.update(R)
    def W(self,j): return self.wv[j].reshape(768,768)
    def S(self,j): return self.sv[j].reshape(768,768)
    def load(self,l,js):
        for j in js: self.wcp(l,j).start()
    def wcp(self,l,j):
        F=self.g.shape[1]; r=768//F; rs=3072//F
        if j<8: return pltpu.make_async_copy(self.g.at[l,:,pl.ds(j*r,r),:],self.wv.at[j],self.wsem.at[j])
        j-=8
        return pltpu.make_async_copy(self.g.at[l,pl.ds(j*(F//4),F//4),pl.ds(8*r,rs),:],self.sv.at[j],self.wsem.at[8+j])
    def ocp(self,l,i): return pltpu.make_async_copy(self.__dict__[SAVED[i]],self.outs[l][i],self.osem.at[l,i])
    def out(self,l,*names):
        for n in names: self.ocp(l,SAVED.index(n)).start()
    def drain(self,l):
        for i in range(len(SAVED)): self.ocp(l,i).wait()
    def ln(self,z,gain,shift):
        mu=jnp.mean(z,-1,keepdims=True); cz=z-mu
        rstd=lax.rsqrt(jnp.mean(cz*cz,-1,keepdims=True)+1e-12)
        xh=cz*rstd
        return xh,rstd,xh*gain+shift
    def attn_steps(self,l,save,x,lens,before=None):
        V=lambda i: self.vecs[l,i:i+1,:]
        def proj_in(j):
            if j==0 and before: before()
            if j==0: self.load(l,range(4))
            self.wcp(l,j).wait()
            r=dot(x[...],self.W(j))
            if j==0: r=r+V(0)
            if j==2: r=r+V(1)
            self.qkv[:,j*768:(j+1)*768]=r.astype(bf16)
            if save and j==2: self.out(l,"qkv")
        lane=lax.broadcasted_iota(jnp.int32,(256,128),1); low_half=lane<64
        kpos=lax.broadcasted_iota(jnp.int32,(256,256),1)
        def pair(i,_):
            c=i//6; p=i-c*6
            rows=pl.ds(pl.multiple_of(c*256,256),256); o=pl.multiple_of(p*128,128)
            q2=self.qkv[rows,pl.ds(o,128)]*jnp.asarray(0.125,bf16)
            k2=self.qkv[rows,pl.ds(pl.multiple_of(768+o,128),128)]; v2=self.qkv[rows,pl.ds(pl.multiple_of(1536+o,128),128)]
            ok=kpos<lens[c]
            res=[]
            for hh in range(2):
                qm=jnp.where(low_half if hh==0 else jnp.logical_not(low_half),q2,jnp.zeros_like(q2))
                s=jnp.where(ok,dot_t(qm,k2),-1e9)
                e=jnp.exp(s-jnp.max(s,-1,keepdims=True))
                pr=(e*(1.0/jnp.sum(e,-1,keepdims=True))).astype(bf16)
                if save: self.pb[i*2+hh]=pr
                res.append(dot(pr,v2))
            self.ctx[rows,pl.ds(o,128)]=jnp.where(low_half,res[0],res[1]).astype(bf16)
            return 0
        def attend(s):
            lax.fori_loop(6*s,6*s+6,pair,0,unroll=3)
            if save and s==1: self.out(l,"pb","ctx")
        def proj_out():
            self.wcp(l,3).wait()
            z=dot(self.ctx[...],self.W(3))+V(2)+x[...].astype(f32)
            xh,rstd,h=self.ln(z,V(3),V(4))
            if save: self.xh1[...]=xh; self.rs1[...]=jnp.broadcast_to(rstd,(512,128))
            self.h1[...]=h.astype(bf16)
            self.acc[...]=h+V(5)
            if save: self.out(l,"xh1","rs1","h1")
        return [functools.partial(proj_in,j) for j in range(3)]+[functools.partial(attend,s) for s in range(2)]+[proj_out]
    def ffn_steps(self,l,save,y,lens,pooled):
        V=lambda i: self.vecs[l,i:i+1,:]
        def part(j):
            if j==0: self.load(l,[4,8,5,9,6,10,7,11])
            self.wcp(l,4+j).wait(); self.wcp(l,8+j).wait()
            u=dot(self.h1[...],self.W(4+j))+V(8+j)
            cdf,pdf=phi_parts(u)
            gb=(u*cdf).astype(bf16)
            if save:
                self.act[:,j*768:(j+1)*768]=gb
                self.der[:,j*768:(j+1)*768]=(cdf+u*pdf).astype(bf16)
            self.acc[...]+=dot(gb,self.S(j))
            if save and j==3: self.out(l,"act","der")
        def end():
            xh,rstd,yy=self.ln(self.acc[...],V(6),V(7))
            if save:
                self.xh2[...]=xh; self.rs2[...]=jnp.broadcast_to(rstd,(512,128)); self.out(l,"xh2","rs2")
            y[...]=yy.astype(bf16)
            if pooled is not None:
                tpos=lax.broadcasted_iota(jnp.int32,(256,768),0)
                for c in range(2):
                    pooled[c:c+1,:]=jnp.sum(jnp.where(tpos<lens[c],yy[c*256:(c+1)*256],0.0),0,keepdims=True)/lens[c].astype(f32)
        return [functools.partial(part,j) for j in range(4)]+[end]

def unit_scale(p): return lax.rsqrt(jnp.sum(p*p,-1,keepdims=True)+1e-6)

class Contrast:
    def __init__(self,pos,queue,lens,R):
        self.p,self.queue,self.lens=pos,queue,lens
        self.__dict__.update(R)
    def ucp(self,s):
        _,dev=self.p.peer(s)
        return remote(self.units.at[self.p.me],self.units.at[self.p.me],self.us.at[s],self.ur.at[s],dev)
    def gcp(self,s):
        j,dev=self.p.peer(s)
        return remote(self.sends.at[j],self.gets.at[self.p.me],self.gs.at[s],self.gr.at[s],dev)
    def loop(self,fn): lax.fori_loop(1,self.p.N,lambda s,_: (fn(s),0)[1],0)
    def send_units(self):
        p=self.pool_q[...]
        self.units[self.p.me]=(p*unit_scale(p)).astype(bf16).astype(f32)
        self.loop(lambda s: self.ucp(s).start())
    def share(self):
        self.loop(lambda s: self.ucp(s).wait_recv())
        N=self.p.N
        for i in range(N): self.q_all[2*i:2*i+2,:]=self.units[i]
        lg=dot_t(self.q_all[...].astype(bf16),self.queue[...])*(1.0/SHARP)
        m=jnp.max(lg,-1,keepdims=True)
        e=jnp.exp(lg-m)
        self.part[:,0:768]=dot(e.astype(bf16),self.queue[...])
        self.part[:,768:896]=jnp.broadcast_to(m,(2*N,128))
        self.part[:,896:1024]=jnp.broadcast_to(jnp.sum(e,-1,keepdims=True),(2*N,128))
        for i in range(N): self.sends[i]=self.part[2*i:2*i+2,:]
        self.gets[self.p.me]=self.sends[self.p.me]
        self.loop(lambda s: self.gcp(s).start())
    def end(self,loss,grad):
        pk=self.pool_k[...]; pq=self.pool_q[...]
        ku=(pk*unit_scale(pk)).astype(bf16).astype(f32)
        rs=unit_scale(pq)
        qu=(pq*rs).astype(bf16).astype(f32)
        pos=jnp.sum(qu*ku,-1,keepdims=True)/SHARP
        self.loop(lambda s: self.gcp(s).wait_recv())
        mi=self.gets[:,:,768:896]
        top=jnp.maximum(jnp.max(mi,0),pos)
        w=jnp.exp(mi-top[None])
        pe=jnp.exp(pos-top)
        total=jnp.sum(w*self.gets[:,:,896:1024],0)+pe
        loss[...]=top+jnp.log(total)-pos
        scale=FACTOR/SHARP
        inv=scale/total
        cp=scale*(pe/total-1.0)
        for k in range(6):
            cols=slice(k*128,(k+1)*128)
            grad[:,cols]=jnp.sum(w*self.gets[:,:,cols],0)*inv+cp*ku[:,cols]
        g=grad[...]
        d=rs*g-pq*(rs*rs*rs)*jnp.sum(pq*g,-1,keepdims=True)
        for c in range(2): grad[c:c+1,:]=d[c:c+1]/self.lens[c].astype(f32)
    def finish(self):
        self.loop(lambda s: self.ucp(s).wait_send())
        self.loop(lambda s: self.gcp(s).wait_send())

def forward_kernel(D,F,order,names,lenq,lenk,xq,xk,queue,msg,qw,pw,ew,sw,kqw,kpw,kew,ksw,
                   g,vecs,y0,y1,loss,gp,*rest):
    outs=(rest[:10],rest[10:20]); R=dict(zip(names,rest[20:]))
    pos=Place(D,F); r=768//F; rs=3072//F; f=pos.f
    bar=pltpu.get_barrier_semaphore()
    def hello(s,_):
        _,dev=pos.peer(s)
        pl.semaphore_signal(bar,inc=1,device_id=dev,device_id_type=MESH); return 0
    lax.fori_loop(1,pos.N,hello,0)
    def own(l,j):
        dst=lambda j,n: R["pk"].at[l,pl.ds(j*r,n)]
        if j<3: s,d=qw.at[l,:,pl.ds(j*768,768)],dst(j,r)
        elif j==3: s,d=pw.at[l],dst(3,r)
        elif j<8: s,d=ew.at[l,:,pl.ds((j-4)*768,768)],dst(j,r)
        else: s,d=sw.at[l],dst(8,rs)
        return pltpu.make_async_copy(s,d,R["lsem"].at[l,j])
    groups={0:range(4),1:range(4,9)}
    for l in range(2):
        for j in range(9): own(l,j).start()
    def kload(l):
        pairs=[(kqw,"kq"),(kpw,"kp"),(kew,"ke"),(ksw,"ks"),(qw,"qq"),(pw,"qp"),(ew,"qe"),(sw,"qs")]
        return [pltpu.make_async_copy(a.at[l],R[b],R["ksem"].at[i]) for i,(a,b) in enumerate(pairs)]
    def mcp(l): return pltpu.make_async_copy(R["mo"].at[l],g.at[2+l,f],R["msem"].at[l])
    for c in kload(0): c.start()
    def mirror(l):
        for c in kload(l): c.wait()
        mo=R["mo"]
        mix=lambda k,q: (MOM*k+(1.0-MOM)*q.astype(f32)).astype(bf16)
        for j in range(3):
            cols=slice(j*768,(j+1)*768); mo[l,j*r:(j+1)*r,:]=mix(R["kq"][:,cols],R["qq"][:,cols])
        mo[l,3*r:4*r,:]=mix(R["kp"][...],R["qp"][...])
        for j in range(4):
            cols=slice(j*768,(j+1)*768); mo[l,(4+j)*r:(5+j)*r,:]=mix(R["ke"][:,cols],R["qe"][:,cols])
        mo[l,8*r:8*r+rs,:]=mix(R["ks"][...],R["qs"][...])
        mcp(l).start()
        if l==0:
            for c in kload(1): c.start()
    def packed(q):
        l,r0,n=chunks[q]
        return pltpu.make_async_copy(R["pk"].at[l,pl.ds(r0,n)],g.at[l,f,pl.ds(r0,n)],R["psem"].at[q])
    waited=set()
    def ready(q):
        l=q//2
        if l<2:
            for j in groups[q%2]: own(l,j).wait()
            cp=packed(q); cp.start(); cp.wait()
        elif l not in waited:
            waited.add(l); mcp(l-2).wait()
    chunks=[(l,r0,n) for l in range(4) for r0,n in ((0,4*r),(4*r,8*r))]
    G=Gather(pos,g,chunks,ready,[R[k] for k in ("zs","zr","ys","yr","xs","xr","cs","cr","ks_","kr_")])
    vmsg=R["vmsg"]
    def vcp(s): return remote(msg,vmsg.at[f],R["vs"].at[s],R["vr"].at[s],(pos.d,(f+s)%F))
    vmsg[f]=msg[...]
    pl.semaphore_wait(bar,pos.N-1)
    for s in range(1,F): vcp(s).start()
    def vectors():
        for s in range(1,F): vcp(s).wait_recv()
        row=lax.broadcasted_iota(jnp.int32,(128,768),0); col=lax.broadcasted_iota(jnp.int32,(128,768),1)
        v=jnp.zeros((32,768),f32)
        for i in range(F):
            hot=jnp.logical_and(col==row+i*r,row<r)
            v=v+dot(vmsg[i,:,0:128],jnp.where(hot,1.0,0.0).astype(bf16))
        row=lax.broadcasted_iota(jnp.int32,(384,768),0); col=lax.broadcasted_iota(jnp.int32,(384,768),1)
        for l in range(4): vecs[l,0:8,:]=v[8*l:8*l+8]; vecs[l,8:16,:]=jnp.zeros((8,768),f32)
        for j in range(4):
            e=jnp.zeros((32,768),f32)
            for i in range(F//4):
                hot=jnp.logical_and(col==row+i*rs,row<rs)
                e=e+dot(vmsg[j*(F//4)+i,:,128:512],jnp.where(hot,1.0,0.0).astype(bf16))
            for l in range(4): vecs[l,8+j:9+j,:]=e[8*l:8*l+1]
    Fw=Forward(g,vecs,None,R); Fw.outs=outs
    Ct=Contrast(pos,queue,lenq,R)
    yk=R["yk"]
    work=[]
    for l,(save,x,y,lens,pool) in enumerate([(True,xq,y0,lenq,None),(True,y0,y1,lenq,R["pool_q"]),(False,xk,yk,lenk,None),(False,yk,R["yl"],lenk,R["pool_k"])]):
        work.append(Fw.attn_steps(l,save,x,lens,(lambda k=l-1: Fw.drain(k)) if l in (1,2) else None))
        work.append(Fw.ffn_steps(l,save,y,lens,pool))
    work[3].append(Ct.send_units)
    work[4].append(Ct.share)
    pre=[vectors,lambda: mirror(0),lambda: mirror(1)]
    act=[G.start,G.on_z,G.on_y,G.on_x,G.on_c,lambda q,i: work[q][i](),lambda q,i: pre[i]()]
    for kind,q,i in order:
        if kind in (0,4): act[kind](q)
        else: act[kind](q,i)
    Ct.end(loss,gp)
    G.finish(); Ct.finish()
    for s in range(1,F): vcp(s).wait_send()

def forward(D,F,lenq,lenk,xq,xk,queue,msg,mats,kmats,cid,order=None):
    sd=jax.ShapeDtypeStruct; S=pltpu.SemaphoreType.DMA; VM=pltpu.VMEM
    V=pl.BlockSpec(memory_space=pltpu.VMEM); ANY=pl.BlockSpec(memory_space=pl.ANY); SM=pl.BlockSpec(memory_space=pltpu.SMEM)
    A=4;B=F//4;Q=8;N=D*F; r=768//F; rs=3072//F; M=2*A*B
    buf=dict(zip(SAVED,[VM(s.shape,s.dtype) for s in saved_shapes()]))
    buf.update(acc=VM((512,768),f32),yk=VM((512,768),bf16),yl=VM((512,768),bf16),wv=VM((8,F,r,768),bf16),sv=VM((4,F//4,rs,768),bf16),
        pool_q=VM((2,768),f32),pool_k=VM((2,768),f32),units=VM((N,2,768),f32),q_all=VM((2*N,768),f32),part=VM((2*N,1024),f32),
        sends=VM((N,2,1024),f32),gets=VM((N,2,1024),f32),vmsg=VM((F,32,512),bf16),
        kq=VM((r,2304),f32),kp=VM((r,768),f32),ke=VM((r,3072),f32),ks=VM((rs,768),f32),qq=VM((r,2304),bf16),qp=VM((r,768),bf16),qe=VM((r,3072),bf16),qs=VM((rs,768),bf16),
        mo=VM((2,12*r,768),bf16),pk=VM((2,12*r,768),bf16),psem=S((4,)),
        wsem=S((12,)),osem=S((2,10)),lsem=S((2,9)),ksem=S((8,)),msem=S((2,)),us=S((N,)),ur=S((N,)),gs=S((N,)),gr=S((N,)),vs=S((F,)),vr=S((F,)),
        zs=S((Q,2,A)),zr=S((Q,2,A)),ys=S((Q,2*A,B)),yr=S((Q,2*A,B)),xs=S((Q,M)),xr=S((Q,M)),cs=S((Q,M)),cr=S((Q,M)),ks_=S((Q,M)),kr_=S((Q,M)))
    saved=saved_shapes()
    outs=[sd((4,F,12*r,768),bf16),sd((4,16,768),f32),sd((512,768),bf16),sd((512,768),bf16),sd((2,128),f32),sd((2,768),f32)]+saved*2
    res=pl.pallas_call(functools.partial(forward_kernel,D,F,ORDER if order is None else order,list(buf)),out_shape=outs,
        in_specs=[SM,SM,V,V,V,V]+[ANY]*8,out_specs=[ANY,V,V,V,V,V]+[ANY]*20,scratch_shapes=list(buf.values()),
        compiler_params=pltpu.CompilerParams(collective_id=cid,has_side_effects=True,vmem_limit_bytes=61<<20),name="forward")(lenq,lenk,xq,xk,queue,msg,*mats,*kmats)
    return res[:6],res[6:16],res[16:26]
ORDER = (
    (0, 0, 0), (1, 0, 1), (6, 0, 0), (1, 0, 2), (2, 0, 0), (6, 0, 1), (0, 1, 0), (6, 0, 2), (1, 0, 3), (2, 0, 1),
    (3, 0, 0), (2, 0, 2), (1, 1, 1), (2, 0, 3), (3, 0, 1), (2, 1, 0), (3, 0, 2), (1, 1, 2), (3, 0, 3), (4, 0, 0),
    (5, 0, 0), (5, 0, 1), (1, 1, 3), (5, 0, 2), (5, 0, 3), (3, 1, 0), (2, 1, 1), (0, 2, 0), (5, 0, 4), (2, 1, 2),
    (1, 2, 1), (5, 0, 5), (1, 2, 2), (2, 2, 0), (0, 3, 0), (2, 1, 3), (1, 2, 3), (3, 1, 1), (2, 2, 1), (3, 1, 2),
    (3, 2, 0), (2, 2, 2), (1, 3, 1), (3, 1, 3), (4, 1, 0), (5, 1, 0), (2, 2, 3), (3, 2, 1), (2, 3, 0), (3, 2, 2),
    (1, 3, 2), (5, 1, 1), (3, 2, 3), (5, 1, 2), (4, 2, 0), (5, 1, 3), (1, 3, 3), (5, 1, 4), (3, 3, 0), (2, 3, 1),
    (5, 2, 0), (0, 4, 0), (5, 2, 1), (2, 3, 2), (1, 4, 1), (5, 2, 2), (5, 2, 3), (1, 4, 2), (2, 4, 0), (0, 5, 0),
    (5, 2, 4), (2, 3, 3), (1, 4, 3), (3, 3, 1), (2, 4, 1), (3, 3, 2), (5, 2, 5), (3, 4, 0), (2, 4, 2), (1, 5, 1),
    (3, 3, 3), (4, 3, 0), (5, 3, 0), (2, 4, 3), (3, 4, 1), (2, 5, 0), (3, 4, 2), (1, 5, 2), (5, 3, 1), (3, 4, 3),
    (5, 3, 2), (4, 4, 0), (5, 3, 3), (1, 5, 3), (5, 3, 4), (3, 5, 0), (2, 5, 1), (5, 3, 5), (0, 6, 0), (5, 4, 0),
    (2, 5, 2), (5, 4, 1), (1, 6, 1), (5, 4, 2), (5, 4, 3), (1, 6, 2), (2, 6, 0), (0, 7, 0), (2, 5, 3), (5, 4, 4),
    (1, 6, 3), (3, 5, 1), (2, 6, 1), (3, 5, 2), (3, 6, 0), (5, 4, 5), (2, 6, 2), (1, 7, 1), (3, 5, 3), (4, 5, 0),
    (5, 4, 6), (2, 6, 3), (3, 6, 1), (2, 7, 0), (3, 6, 2), (1, 7, 2), (3, 6, 3), (4, 6, 0), (5, 5, 0), (1, 7, 3),
    (5, 5, 1), (3, 7, 0), (2, 7, 1), (5, 5, 2), (5, 5, 3), (2, 7, 2), (5, 5, 4), (5, 6, 0), (5, 6, 1), (2, 7, 3),
    (5, 6, 2), (3, 7, 1), (5, 6, 3), (3, 7, 2), (5, 6, 4), (3, 7, 3), (4, 7, 0), (5, 6, 5), (5, 7, 0), (5, 7, 1),
    (5, 7, 2), (5, 7, 3), (5, 7, 4),
)

PROWS=(32,64,192,192,64,64,160,32,128)
class Piece:
    pass
def pieces(F):
    r=768//F; fine=r%32==0
    ffn=[range(4,6),range(6,8),range(8,12)]
    attn=[range(3,4),range(0,3)] if fine else [range(0,4)]
    out=[]; o=dict(n=0,hp=0,q=0,hq=0,h=0)
    for l,parts in ((1,ffn+[range(0,4)]),(0,ffn+attn)):
        for blocks in parts:
            p=Piece(); p.l,p.blocks,p.row,p.n=l,blocks,blocks[0]*r,len(blocks)*r
            p.np=PROWS[len(out)]*r//96 if fine else p.n//96*32
            p.nq=p.n-p.np; p.hp,p.hq=p.np//2,p.nq//2; p.h=p.hp+p.hq
            p.on,p.ohp,p.oq,p.ohq,p.oh=o["n"],o["hp"],o["q"],o["hq"],o["h"]
            o["n"]+=p.n; o["hp"]+=p.hp; o["q"]+=p.nq; o["hq"]+=p.hq; o["h"]+=p.h
            out.append(p)
    return out,o
class Reduce:
    def __init__(self,pos,dg,flush,R,outs,r):
        self.p,self.dg,self.flush,self.outs,self.r=pos,dg,flush,outs,r
        self.__dict__.update(R)
        self.pc,_=pieces(pos.F)
        m=pl.multiple_of; c=pos.c
        self.mycols=pl.ds(m(c*384,128),384); self.ocols=pl.ds(m((1-c)*384,128),384)
        self.X=(pos.xd,pos.f); self.C=(pos.cd,pos.f)
        self.busy={}
        self.rest=[]
    def Y(self,t): return (self.p.d,self.p.a*self.p.B+(self.p.b+t)%self.p.B)
    def Z(self,s): return (self.p.d,((self.p.a+s)%self.p.A)*self.p.B+self.p.b)
    def Oo(self,s): return ((self.p.d+4*s)%self.p.D,self.p.f)
    def rc(self,i,k,src,dst,dev): return remote(src,dst,self.SS.at[i,k],self.RS.at[i,k],dev)
    def go(self,cp,key=None):
        cp.start()
        if key is None: self.rest.append(cp)
        else: self.busy.setdefault(key,[]).append(cp)
    def free(self,key):
        for cp in self.busy.pop(key,[]): cp.wait_send()
    def ky(self,t): return 5+t
    def kq(self,t): return 5+self.p.B+t
    def kz(self,s): return 5+2*self.p.B+s
    def ko(self,s): return 5+2*self.p.B+self.p.A+s
    def Prow(self,i,mine):
        q=self.pc[i]; x=self.p.x if mine else 1-self.p.x
        return pl.ds(pl.multiple_of(x*q.hp,16),q.hp)
    def Qrow(self,i,mine):
        q=self.pc[i]; x=self.p.x if mine else 1-self.p.x
        return pl.ds(pl.multiple_of(q.np+x*q.hq,16),q.hq)
    def Qall(self,i): return pl.ds(self.pc[i].np,self.pc[i].nq)
    def src(self,i): q=self.pc[i]; return self.dg.at[q.l,:,pl.ds(q.row,q.n)]
    def Tv(self,i): return self.T.at[i%3].reshape(self.p.A,self.p.B,self.T.shape[2],384)
    def bhp(self,i): return pl.ds(self.pc[i].ohp,self.pc[i].hp)
    def bq(self,i): return pl.ds(self.pc[i].oq,self.pc[i].nq)
    def bhq(self,i): return pl.ds(self.pc[i].ohq,self.pc[i].hq)
    def bh(self,i): return pl.ds(self.pc[i].oh,self.pc[i].h)
    def bn(self,i): return pl.ds(self.pc[i].on,self.pc[i].n)
    def cC(self,i): return self.rc(i,0,self.src(i).at[:,:,self.ocols],self.RC.at[:,self.bn(i)],self.C)
    def cPx(self,i): return self.rc(i,1,self.T.at[i%3,:,self.Prow(i,False)],self.RPX.at[:,self.bhp(i)],self.X)
    def cPy(self,i,t): return self.rc(i,self.ky(t),self.Tv(i).at[:,(self.p.b+t)%self.p.B,self.Prow(i,True)],self.RPY.at[t-1,:,self.bhp(i)],self.Y(t))
    def cQy(self,i,t): return self.rc(i,self.kq(t),self.Tv(i).at[:,(self.p.b+t)%self.p.B,self.Qall(i)],self.RQY.at[t-1,:,self.bq(i)],self.Y(t))
    def cQx(self,i): return self.rc(i,2,self.Tv(i).at[:,self.p.b,self.Qrow(i,False)],self.RQX.at[:,self.bhq(i)],self.X)
    def cZ(self,i,s): return self.rc(i,self.kz(s),self.T3.at[i%3,(self.p.a+s)%self.p.A,0:self.pc[i].h],self.RZ.at[s-1,self.bh(i)],self.Z(s))
    def cO(self,i,s): return self.rc(i,self.ko(s),self.TO.at[self.bh(i)],self.RO.at[s-1,self.bh(i)],self.Oo(s))
    def fin(self,i,rows): return pl.ds(pl.multiple_of(self.pc[i].on+rows.start,16),rows.size)
    def cFX(self,i,w,mine=True):
        r=(self.Prow,self.Qrow)[w](i,mine); v=self.FIN.at[self.fin(i,r),self.mycols]
        return self.rc(i,3+w,v,v,self.X)
    def cFC(self,i,mine=True):
        v=self.FIN.at[self.bn(i),self.mycols if mine else self.ocols]
        return self.rc(i,5,v,v,self.C)
    def s0(self,i):
        self.flush(self.pc[i])
        self.go(self.cC(i))
    def loads(self,i):
        n=self.pc[i].n
        return [pltpu.make_async_copy(self.src(i).at[:,:,self.mycols],self.T.at[i%3,:,0:n],self.LS.at[i,0]),
                pltpu.make_async_copy(self.RC.at[:,self.bn(i)],self.RCV.at[:,0:n],self.LS.at[i,1])]
    def s1(self,i):
        self.free(("T",i%3))
        self.cC(i).wait_recv()
        for cp in self.loads(i): cp.start()
    def s2(self,i):
        T,k,n=self.T,i%3,self.pc[i].n
        for cp in self.loads(i): cp.wait()
        def body(f,_):
            T[k,f,0:n]=(T[k,f,0:n].astype(f32)+self.RCV[f,0:n].astype(f32)).astype(bf16); return 0
        lax.fori_loop(0,self.p.F,body,0)
        self.go(self.cPx(i),("T",k))
        for t in range(1,self.p.B): self.go(self.cQy(i,t),("T",k))
    def s3(self,i):
        T,k=self.T,i%3; own=self.Prow(i,True)
        self.cPx(i).wait_recv()
        def body(f,_):
            T[k,f,own]=(T[k,f,own].astype(f32)+self.RPX[f,self.bhp(i)].astype(f32)).astype(bf16); return 0
        lax.fori_loop(0,self.p.F,body,0)
        for t in range(1,self.p.B): self.go(self.cPy(i,t),("T",k))
    def s4(self,i):
        T,k=self.T,i%3; al=self.Qall(i)
        for t in range(1,self.p.B): self.cQy(i,t).wait_recv()
        def body(a,_):
            fo=a*self.p.B+self.p.b
            v=T[k,fo,al].astype(f32)
            for t in range(1,self.p.B): v=v+self.RQY[t-1,a,self.bq(i)].astype(f32)
            T[k,fo,al]=v.astype(bf16); return 0
        lax.fori_loop(0,self.p.A,body,0)
        self.go(self.cQx(i),("T",k))
    def s5(self,i):
        T,k=self.T,i%3; q=self.pc[i]
        self.free(("T3",k))
        for t in range(1,self.p.B): self.cPy(i,t).wait_recv()
        self.cQx(i).wait_recv()
        def body(a,_):
            fo=a*self.p.B+self.p.b
            v=T[k,fo,self.Prow(i,True)].astype(f32)
            for t in range(1,self.p.B): v=v+self.RPY[t-1,a,self.bhp(i)].astype(f32)
            self.T3[k,a,0:q.hp]=v.astype(bf16)
            self.T3[k,a,q.hp:q.h]=(T[k,fo,self.Qrow(i,True)].astype(f32)+self.RQX[a,self.bhq(i)].astype(f32)).astype(bf16)
            return 0
        lax.fori_loop(0,self.p.A,body,0)
        for s in range(1,self.p.A): self.go(self.cZ(i,s),("T3",k))
    def s6(self,i):
        q=self.pc[i]
        v=self.T3[i%3,self.p.a,0:q.h].astype(f32)
        for s in range(1,self.p.A):
            self.cZ(i,s).wait_recv()
            v=v+self.RZ[s-1,self.bh(i)].astype(f32)
        if self.p.O>1:
            self.TO[self.bh(i)]=v.astype(bf16)
            for s in range(1,self.p.O): self.go(self.cO(i,s))
            for s in range(1,self.p.O):
                self.cO(i,s).wait_recv(); v=v+self.RO[s-1,self.bh(i)].astype(f32)
        v=v.astype(bf16)
        self.FIN[self.fin(i,self.Prow(i,True)),self.mycols]=v[:q.hp]; self.FIN[self.fin(i,self.Qrow(i,True)),self.mycols]=v[q.hp:]
        for w in (0,1): self.go(self.cFX(i,w))
    def s7(self,i):
        for w in (0,1): self.cFX(i,w,False).wait_recv()
        self.go(self.cFC(i))
    def outcps(self,i):
        q=self.pc[i]; r=self.r; oq,op,oe,os=self.outs
        if q.blocks[0]==8: pairs=[(self.FIN.at[self.bn(i)],os.at[q.l])]
        else:
            pairs=[]
            for k,b in enumerate(q.blocks):
                v=self.FIN.at[pl.ds(q.on+k*r,r)]
                if b<3: pairs.append((v,oq.at[q.l,:,pl.ds(b*768,768)]))
                elif b==3: pairs.append((v,op.at[q.l]))
                else: pairs.append((v,oe.at[q.l,:,pl.ds((b-4)*768,768)]))
        return [pltpu.make_async_copy(s,d,self.OS.at[i,j]) for j,(s,d) in enumerate(pairs)]
    def s8(self,i):
        self.cFC(i,False).wait_recv()
        for cp in self.outcps(i): cp.start()
    def vstage(self,k):
        B,A,O=self.p.B,self.p.A,self.p.O
        st=[(self.VRC,[self.C],0),(self.VRX,[self.X],1),(self.VRY,[self.Y(t) for t in range(1,B)],2),(self.VRZ,[self.Z(s) for s in range(1,A)],2+B)]
        if O>1: st.append((self.VRO,[self.Oo(s) for s in range(1,O)],2+B+A))
        def cps(k):
            buf,devs,k0=st[k]
            return [remote(self.VS.at[k],buf.at[q],self.VSS.at[k0+q],self.VRS.at[k0+q],dv) for q,dv in enumerate(devs)]
        if k>len(st): return
        if k>0:
            v=self.VS[k-1]
            for q,cp in enumerate(cps(k-1)):
                cp.wait_recv(); v=v+st[k-1][0][q]
            if k<len(st): self.VS[k]=v
            else: self.vout[...]=v
        if k<len(st):
            for cp in cps(k): self.go(cp)
    def finish(self):
        for key in list(self.busy): self.free(key)
        for cp in self.rest: cp.wait_send()
        for i in range(len(self.pc)):
            for cp in self.outcps(i): cp.wait()

class Backward:
    NAMES=("qkv","pb","ctx","xh1","rs1","h1","xh2","rs2","x")
    SAME={"xh1":"xh","xh2":"xh","rs1":"rsd","rs2":"rsd"}
    def __init__(self,lens,gp,vecs,g,dg,saved,xs,R,dx):
        self.lens,self.gp,self.vecs,self.g,self.dg,self.saved,self.xs,self.dx=lens,gp,vecs,g,dg,saved,xs,dx
        self.__dict__.update(R)
        self.F=g.shape[1]; self.r=768//self.F; self.rs=3072//self.F
        self.slot=0; self.stage={}; self.blocks={}
        self.chunkno=0
    def cp(self,l,name):
        src=self.xs[l] if name=="x" else self.saved[l][SAVED.index(name)]
        return pltpu.make_async_copy(src,self.__dict__[self.SAME.get(name,name)],self.isem.at[self.NAMES.index(name)])
    def fetch(self,l,*names):
        if l<0: return
        for n in names: self.cp(l,n).start()
    def need(self,l,*names):
        for n in names: self.cp(l,n).wait()
    def wcp(self,l,j): return pltpu.make_async_copy(self.g.at[l,:,pl.ds(j*self.r,self.r),:],self.wa.at[j],self.wsem.at[j])
    def ccps(self,l,j):
        s=j%2; F=self.F; cols=pl.ds(j*768,768)
        srcs=[(self.g.at[l,:,pl.ds((4+j)*self.r,self.r),:],self.we.at[s]),(self.g.at[l,pl.ds(j*(F//4),F//4),pl.ds(8*self.r,self.rs),:],self.wsx.at[s]),
              (self.saved[l][SAVED.index("act")].at[:,cols],self.act.at[s]),(self.saved[l][SAVED.index("der")].at[:,cols],self.der.at[s])]
        return [pltpu.make_async_copy(a,b,self.csem.at[s,k]) for k,(a,b) in enumerate(srcs)]
    def fetch_chunk(self,l,j):
        if j>=4: l,j=l-1,j-4
        if l<0: return
        for c in self.ccps(l,j): c.start()
    def fetch_w(self,l,*js):
        if l<0: return
        for j in js: self.wcp(l,j).start()
    def put(self,l,j,val):
        k=self.slot; self.slot=(k+1)%3
        if k in self.stage: self.stage.pop(k).wait()
        self.st[k]=val.astype(bf16)
        if j<8: src,dst=self.st.at[k].reshape(self.F,self.r,768),self.dg.at[l,:,pl.ds(j*self.r,self.r)]
        else:
            q=j-8; n=self.F//4
            src,dst=self.st.at[k].reshape(n,self.rs,768),self.dg.at[l,pl.ds(q*n,n),pl.ds(8*self.r,self.rs)]
        cp=pltpu.make_async_copy(src,dst,self.ssem.at[k]); cp.start()
        self.stage[k]=cp; self.blocks[k]=(l,j)
    def flush(self,piece):
        for k in list(self.stage):
            l,j=self.blocks[k]
            if l==piece.l and j in piece.blocks: self.stage.pop(k).wait()
    def first(self):
        l=1
        self.fetch(l,"xh2","rs2"); self.fetch_chunk(l,0); self.fetch(l,"h1"); self.fetch_chunk(l,1)
        self.fetch(l,"ctx"); self.fetch_w(l,3); self.fetch(l,"qkv","pb"); self.fetch_w(l,0,1,2); self.fetch(l,"x")
        self.VS[0]=jnp.zeros(self.VS.shape[1:],f32)
    def vrow(self,l,k,val): self.VS[0,l*12+k:l*12+k+1,:]=jnp.sum(val,0,keepdims=True)
    def steps(self,l):
        V=lambda i: self.vecs[l,i:i+1,:]
        r=self.r
        def ln_back(dy,xh,rstd,gain):
            t=dy*gain
            return rstd*(t-jnp.mean(t,-1,keepdims=True)-xh*jnp.mean(t*xh,-1,keepdims=True))
        def second():
            if l==1:
                tpos=lax.broadcasted_iota(jnp.int32,(256,768),0)
                for c in range(2): self.acc[c*256:(c+1)*256,:]=jnp.where(tpos<self.lens[c],self.gp[c:c+1,:],0.0)
            dy=self.acc[...]
            self.need(l,"xh2","rs2")
            xh=self.xh[...]
            self.vrow(l,6,dy*xh); self.vrow(l,7,dy)
            d2=ln_back(dy,xh,self.rsd[:,0:1],V(6))
            self.acc[...]=d2
            self.dr[...]=d2.astype(bf16)
            self.vrow(l,5,self.dr[...].astype(f32))
            self.fetch(l,"xh1","rs1")
        def ffn(j):
            s=j%2
            for c in self.ccps(l,j): c.wait()
            if j==0: self.need(l,"h1")
            E=self.we[s].reshape(768,768); S=self.wsx[s].reshape(768,768)
            self.put(l,8+j,tdot(self.act[s],self.dr[...]))
            du=(dot_t(self.dr[...],S)*self.der[s].astype(f32)).astype(bf16)
            self.vrow(l,8+j,du.astype(f32))
            self.put(l,4+j,tdot(self.h1[...],du))
            self.acc[...]+=dot_t(du,E)
            self.fetch_chunk(l,j+2)
            if j==3: self.fetch(l-1,"h1")
        def middle():
            self.need(l,"xh1","rs1","ctx")
            dh=self.acc[...]; xh=self.xh[...]
            self.vrow(l,3,dh*xh); self.vrow(l,4,dh)
            d1=ln_back(dh,xh,self.rsd[:,0:1],V(3))
            self.acc[...]=d1
            self.dr[...]=d1.astype(bf16)
            self.vrow(l,2,self.dr[...].astype(f32))
            self.wcp(l,3).wait()
            self.put(l,3,tdot(self.ctx[...],self.dr[...]))
            self.ctx[...]=dot_t(self.dr[...],self.wa[3].reshape(768,768)).astype(bf16)
            self.fetch(l-1,"xh2","rs2"); self.fetch_w(l-1,3)
        lane=lax.broadcasted_iota(jnp.int32,(256,128),1); low_half=lane<64
        def pair(i,_):
            c=i//6; p=i-c*6; qkv=self.qkv
            rows=pl.ds(pl.multiple_of(c*256,256),256); o=pl.multiple_of(p*128,128)
            o1=pl.multiple_of(768+o,128); o2=pl.multiple_of(1536+o,128)
            q2=qkv[rows,pl.ds(o,128)]; k2=qkv[rows,pl.ds(o1,128)]; v2=qkv[rows,pl.ds(o2,128)]
            dc=self.ctx[rows,pl.ds(o,128)]
            res=[]
            for hh in range(2):
                m=low_half if hh==0 else jnp.logical_not(low_half)
                P=self.pb[i*2+hh]; pf=P.astype(f32)
                dP=dot_t(jnp.where(m,dc,jnp.zeros_like(dc)),v2)
                pd=pf*dP
                dS=(pd-pf*jnp.sum(pd,-1,keepdims=True)).astype(bf16)
                res.append((dot(dS,k2),tdot(dS,q2),tdot(P,dc)))
            sel=lambda t: jnp.where(low_half,res[0][t],res[1][t])
            qkv[rows,pl.ds(o,128)]=(sel(0)*0.125).astype(bf16)
            qkv[rows,pl.ds(o1,128)]=(sel(1)*0.125).astype(bf16)
            qkv[rows,pl.ds(o2,128)]=sel(2).astype(bf16)
            return 0
        def attend(s):
            if s==0: self.need(l,"qkv","pb")
            lax.fori_loop(4*s,4*s+4,pair,0,unroll=2)
            if s==2: self.fetch(l-1,"pb","ctx")
        def mixed(j):
            self.wcp(l,j).wait()
            if j==0: self.need(l,"x")
            dm=self.qkv[:,j*768:(j+1)*768]
            if j!=1: self.vrow(l,0 if j==0 else 1,dm.astype(f32))
            self.put(l,j,tdot(self.x[...],dm))
            self.acc[...]+=dot_t(dm,self.wa[j].reshape(768,768))
            self.fetch_w(l-1,j)
            if j==2:
                self.fetch(l-1,"qkv","x")
                if l==0: self.dx[...]=self.acc[...].astype(bf16)
        P=functools.partial
        return [second]+[P(ffn,j) for j in range(4)]+[middle]+[P(attend,s) for s in range(3)]+[P(mixed,j) for j in range(3)]

def backward_kernel(D,F,order,names,lens,gp,vecs,g,x0,y0,*rest):
    saved=(rest[0:10],rest[10:20]); dg,dx,oq,op,oe,os,vout,rcv=rest[20:28]; R=dict(zip(names,rest[28:])); R["RC"]=rcv
    pos=Place(D,F)
    bar=pltpu.get_barrier_semaphore()
    peers=[(pos.xd,pos.f),(pos.cd,pos.f)]+[(pos.d,(pos.f+s)%F) for s in range(1,F)]+[((pos.d+4*s)%D,pos.f) for s in range(1,pos.O)]
    for dev in peers: pl.semaphore_signal(bar,inc=1,device_id=dev,device_id_type=MESH)
    Bw=Backward(lens,gp,vecs,g,dg,saved,(x0,y0),R,dx)
    Bw.first()
    Rd=Reduce(pos,dg,Bw.flush,R,(oq,op,oe,os),768//F); Rd.vout=vout
    work={1:Bw.steps(1),0:Bw.steps(0)}
    stages=[Rd.s0,Rd.s1,Rd.s2,Rd.s3,Rd.s4,Rd.s5,Rd.s6,Rd.s7,Rd.s8]
    pl.semaphore_wait(bar,len(peers))
    for kind,i,k in order:
        if kind==0: work[i][k]()
        elif kind==1: stages[k](i)
        else: Rd.vstage(k)
    Rd.finish()

def backward(D,F,lens,gp,vecs,g,x0,y0,saved0,saved1,cid,order=None):
    sd=jax.ShapeDtypeStruct; S=pltpu.SemaphoreType.DMA; VM=pltpu.VMEM
    V=pl.BlockSpec(memory_space=pltpu.VMEM); ANY=pl.BlockSpec(memory_space=pl.ANY); SM=pl.BlockSpec(memory_space=pltpu.SMEM)
    A=4;B=F//4;O=D//4; r=768//F; rs=3072//F; n=4*r; pcs,o=pieces(F); NP=len(pcs); hmax=max(p.h for p in pcs); K=8+2*B+A+O
    shp=dict(zip(SAVED,saved_shapes()))
    buf={k:VM(shp[k].shape,shp[k].dtype) for k in ("qkv","pb","ctx","h1")}
    buf.update(xh=VM((512,768),f32),rsd=VM((512,128),f32))
    buf.update(x=VM((512,768),bf16),act=VM((2,512,768),bf16),der=VM((2,512,768),bf16),wa=VM((4,F,r,768),bf16),we=VM((2,F,r,768),bf16),wsx=VM((2,F//4,rs,768),bf16),
        acc=VM((512,768),f32),dr=VM((512,768),bf16),st=VM((3,768,768),bf16),
        T=VM((3,F,n,384),bf16),RCV=VM((F,n,384),bf16),RPX=VM((F,o["hp"],384),bf16),RPY=VM((B-1,A,o["hp"],384),bf16),RQY=VM((B-1,A,o["q"],384),bf16),
        RQX=VM((A,o["hq"],384),bf16),T3=VM((3,A,hmax,384),bf16),RZ=VM((A-1,o["h"],384),bf16),FIN=VM((o["n"],768),bf16),
        VS=VM((5,24,768),f32),VRC=VM((1,24,768),f32),VRX=VM((1,24,768),f32),VRY=VM((B-1,24,768),f32),VRZ=VM((A-1,24,768),f32),
        isem=S((9,)),wsem=S((4,)),csem=S((2,4)),ssem=S((3,)),LS=S((NP,2)),OS=S((NP,4)),SS=S((NP,K)),RS=S((NP,K)),VSS=S((K,)),VRS=S((K,)))
    if O>1: buf.update(RO=VM((O-1,o["h"],384),bf16),TO=VM((o["h"],384),bf16),VRO=VM((O-1,24,768),f32))
    outs=[sd((2,F,12*r,768),bf16),sd((512,768),bf16),sd((2,r,2304),bf16),sd((2,r,768),bf16),sd((2,r,3072),bf16),sd((2,rs,768),bf16),sd((24,768),f32),sd((F,o["n"],384),bf16)]
    res=pl.pallas_call(functools.partial(backward_kernel,D,F,(BORDER if r%32==0 else BORDER_COARSE) if order is None else order,list(buf)),out_shape=outs,
        in_specs=[SM,V,V]+[ANY]*23,out_specs=[ANY,V,ANY,ANY,ANY,ANY,V,ANY],scratch_shapes=list(buf.values()),
        compiler_params=pltpu.CompilerParams(collective_id=cid,has_side_effects=True,vmem_limit_bytes=62<<20),name="backward")(lens,gp,vecs,g,x0,y0,*saved0,*saved1)
    return res[1:7]
BORDER = (
    (0, 1, 0), (0, 1, 1), (0, 1, 2), (1, 0, 0), (0, 1, 3), (1, 0, 1), (0, 1, 4), (1, 0, 2), (1, 1, 0), (1, 2, 0),
    (0, 1, 5), (1, 0, 3), (1, 1, 1), (0, 1, 6), (1, 1, 2), (1, 2, 1), (0, 1, 7), (1, 0, 4), (1, 2, 2), (1, 1, 3),
    (0, 1, 8), (0, 1, 9), (1, 0, 5), (1, 1, 4), (0, 1, 10), (0, 1, 11), (1, 3, 0), (0, 0, 0), (1, 0, 6), (0, 0, 1),
    (1, 2, 3), (1, 2, 4), (1, 1, 5), (1, 3, 1), (0, 0, 2), (1, 0, 7), (1, 3, 2), (1, 4, 0), (0, 0, 3), (1, 0, 8),
    (1, 1, 6), (1, 2, 5), (1, 4, 1), (0, 0, 4), (1, 4, 2), (1, 5, 0), (1, 6, 0), (0, 0, 5), (1, 1, 7), (1, 3, 3),
    (1, 3, 4), (1, 5, 1), (1, 7, 0), (1, 4, 3), (0, 0, 6), (1, 1, 8), (1, 2, 6), (1, 4, 4), (1, 5, 2), (0, 0, 7),
    (1, 2, 7), (1, 3, 5), (1, 6, 1), (0, 0, 8), (1, 2, 8), (1, 4, 5), (1, 6, 2), (1, 7, 1), (0, 0, 9), (1, 5, 3),
    (1, 5, 4), (1, 7, 2), (0, 0, 10), (0, 0, 11), (1, 3, 6), (1, 8, 0), (2, 0, 0), (1, 6, 3), (2, 0, 1), (1, 4, 6),
    (1, 6, 4), (2, 0, 2), (1, 5, 5), (1, 7, 3), (1, 8, 1), (2, 0, 3), (1, 8, 2), (1, 3, 7), (1, 7, 4), (1, 4, 7),
    (2, 0, 4), (1, 3, 8), (1, 4, 8), (1, 5, 6), (2, 0, 5), (1, 6, 5), (1, 8, 3), (1, 8, 4), (1, 7, 5), (1, 5, 7),
    (1, 5, 8), (1, 6, 6), (1, 8, 5), (1, 7, 6), (1, 6, 7), (1, 7, 7), (1, 6, 8), (1, 7, 8), (1, 8, 6), (1, 8, 7),
    (1, 8, 8),
)
BORDER_COARSE = (
    (0, 1, 0), (0, 1, 1), (0, 1, 2), (1, 0, 0), (0, 1, 3), (1, 0, 1), (0, 1, 4), (1, 0, 2), (1, 1, 0), (1, 2, 0),
    (0, 1, 5), (1, 1, 1), (0, 1, 6), (1, 0, 3), (1, 1, 2), (1, 0, 4), (1, 2, 1), (0, 1, 7), (1, 2, 2), (1, 1, 3),
    (0, 1, 8), (1, 0, 5), (0, 1, 9), (1, 1, 4), (0, 1, 10), (0, 1, 11), (1, 3, 0), (1, 2, 3), (1, 0, 6), (0, 0, 0),
    (0, 0, 1), (1, 0, 7), (1, 2, 4), (1, 3, 1), (0, 0, 2), (1, 0, 8), (1, 1, 5), (1, 3, 2), (1, 4, 0), (0, 0, 3),
    (1, 2, 5), (1, 4, 1), (0, 0, 4), (1, 1, 6), (1, 3, 3), (1, 4, 2), (1, 5, 0), (1, 6, 0), (0, 0, 5), (1, 1, 7),
    (1, 5, 1), (1, 3, 4), (1, 4, 3), (0, 0, 6), (1, 1, 8), (1, 2, 6), (1, 5, 2), (0, 0, 7), (1, 3, 5), (1, 6, 1),
    (0, 0, 8), (1, 2, 7), (1, 4, 4), (1, 6, 2), (1, 2, 8), (1, 5, 3), (0, 0, 9), (0, 0, 10), (1, 4, 5), (1, 5, 4),
    (0, 0, 11), (1, 3, 6), (1, 7, 0), (2, 0, 0), (1, 6, 3), (2, 0, 1), (1, 4, 6), (1, 7, 1), (2, 0, 2), (1, 7, 2),
    (1, 3, 7), (2, 0, 3), (1, 6, 4), (1, 3, 8), (1, 4, 7), (1, 5, 5), (2, 0, 4), (1, 4, 8), (2, 0, 5), (1, 7, 3),
    (1, 5, 6), (1, 6, 5), (1, 5, 7), (1, 5, 8), (1, 7, 4), (1, 6, 6), (1, 7, 5), (1, 6, 7), (1, 6, 8), (1, 7, 6),
    (1, 7, 7), (1, 7, 8),
)


def on_device(dp, fsdp, x_query, x_key, len_query, len_key, queue, *params):
    query_params, key_params = params[:13], params[13:]
    num_crops, seq_len, width = x_query.shape
    r = width // fsdp
    order = (1, 2, 4, 5, 6, 10, 11, 12)
    row = lax.broadcasted_iota(jnp.int32, (2, 8, r), 1)

    def stacked(params):
        out = params[order[0]][:, None, :]
        for k in range(1, 8):
            out = jnp.where(row == k, params[order[k]][:, None, :], out)
        return out

    small_q, small_k = stacked(query_params), stacked(key_params)
    bias_q, bias_k = query_params[8], key_params[8]
    mix = lambda k, q: (MOM * k + (1.0 - MOM) * q.astype(f32)).astype(bf16)
    small = jnp.concatenate([small_q, mix(small_k, small_q)], 0).reshape(32, r)
    wide = jnp.concatenate([bias_q, mix(bias_k, bias_q)], 0)
    wide = jnp.pad(wide[:, None, :], ((0, 0), (0, 7), (0, 384 - wide.shape[1]))).reshape(32, 384)
    msg = jnp.concatenate([jnp.pad(small, ((0, 0), (0, 128 - r))), wide], 1)
    big = (0, 3, 7, 9)
    x0 = x_query.reshape(num_crops * seq_len, width)
    xk = x_key.reshape(num_crops * seq_len, width)
    (gathered, vecs, y0, y1, loss, grad_pooled), saved0, saved1 = forward(
        dp, fsdp, len_query, len_key, x0, xk, queue, msg,
        [query_params[i] for i in big], [key_params[i] for i in big], 1)
    dx0, *grads, vsum = backward(dp, fsdp, len_query, grad_pooled, vecs, gathered, x0, y0, saved0, saved1, 2)
    grad_qkv, grad_proj, grad_expand, sh_g = [v.astype(f32) for v in grads]
    me = lax.axis_index("fsdp")
    vsum = vsum.reshape(2, 12, width)
    mine = lax.dynamic_slice_in_dim(vsum[:, :8], me * r, r, 2)
    ebg = lax.dynamic_slice_in_dim(vsum[:, 8:12].reshape(2, 4 * width), me * 4 * r, 4 * r, 1)
    qb, vb, pb, g1, b1, sb, g2, b2 = [mine[:, i] for i in range(8)]
    hidden = y1.reshape(num_crops, seq_len, width)
    grad_input = dx0.reshape(num_crops, seq_len, width)
    return (hidden, grad_input, grad_qkv, qb, vb, grad_proj, pb, g1, b1, grad_expand, ebg, sh_g, sb, g2, b2, loss[:, 0])


def solution(mesh):
    in_specs = (
        P(("dp", "fsdp"), None, None),
        P(("dp", "fsdp"), None, None),
        P(("dp", "fsdp")),
        P(("dp", "fsdp")),
        P(("dp", "fsdp"), None),
        P(None, "fsdp", None),
        P(None, "fsdp"),
        P(None, "fsdp"),
        P(None, "fsdp", None),
        P(None, "fsdp"),
        P(None, "fsdp"),
        P(None, "fsdp"),
        P(None, "fsdp", None),
        P(None, "fsdp"),
        P(None, "fsdp", None),
        P(None, "fsdp"),
        P(None, "fsdp"),
        P(None, "fsdp"),
        P(None, "fsdp", None),
        P(None, "fsdp"),
        P(None, "fsdp"),
        P(None, "fsdp", None),
        P(None, "fsdp"),
        P(None, "fsdp"),
        P(None, "fsdp"),
        P(None, "fsdp", None),
        P(None, "fsdp"),
        P(None, "fsdp", None),
        P(None, "fsdp"),
        P(None, "fsdp"),
        P(None, "fsdp"),
    )
    out_specs = (
        P(("dp", "fsdp"), None, None),
        P(("dp", "fsdp"), None, None),
        P(None, "fsdp", None),
        P(None, "fsdp"),
        P(None, "fsdp"),
        P(None, "fsdp", None),
        P(None, "fsdp"),
        P(None, "fsdp"),
        P(None, "fsdp"),
        P(None, "fsdp", None),
        P(None, "fsdp"),
        P(None, "fsdp", None),
        P(None, "fsdp"),
        P(None, "fsdp"),
        P(None, "fsdp"),
        P(("dp", "fsdp")),
    )
    return jax.shard_map(
        functools.partial(on_device, mesh.shape["dp"], mesh.shape["fsdp"]), mesh=mesh, in_specs=in_specs, out_specs=out_specs, check_vma=False
    )
```
